32 devices in a mesh: dp: 2 (over core), fsdp: 16 (over z, y, x).
Axes of the slice: x: 2, y: 2, z: 4, core: 2. Of those that a mesh axis runs over, the one named last changes fastest.
Arguments:
- tokens: bfloat16 [32, 1024, 512], P(('dp', 'fsdp'))
- lengths: int32 [32, 256], P(('dp', 'fsdp')), may hold values from 0 to 250, as said below
- attend_weight: float32 [512, 1536], P('fsdp'), may hold values from -0.1875 to 0.1875
- merger_weight: float32 [512, 512], P('fsdp'), may hold values from -1 to 1
- expand_weight: float32 [512, 2048], P('fsdp'), may hold values from -0.25 to 0.25
- shrink_weight: float32 [2048, 512], P('fsdp'), may hold values from -0.125 to 0.125
- vectors: float32 [6, 512], P(None, 'fsdp')
- attend_rows: float32 [512], P('fsdp'), may hold values from 2.2230691e-07 to 8.8922764e-07
- attend_columns: float32 [1536], P('fsdp'), may hold values from 2.2230691e-07 to 8.8922764e-07
- merger_rows: float32 [512], P('fsdp'), may hold values from 1.1115345e-08 to 4.446138e-08
- merger_columns: float32 [512], P('fsdp'), may hold values from 1.1115345e-08 to 4.446138e-08
- expand_rows: float32 [512], P('fsdp'), may hold values from 1.2703252e-08 to 5.0813007e-08
- expand_columns: float32 [2048], P('fsdp'), may hold values from 1.2703252e-08 to 5.0813007e-08
- shrink_rows: float32 [2048], P('fsdp'), may hold values from 3.175813e-08 to 1.2703252e-07
- shrink_columns: float32 [512], P('fsdp'), may hold values from 3.175813e-08 to 1.2703252e-07
- vector_moments: float32 [6, 512], P(None, 'fsdp'), may hold values from 8.8922764e-07 to 3.4933944e-06
- cotangent: bfloat16 [32, 1024, 512], P(('dp', 'fsdp')), may hold values from -6 to 6
Outputs:
- block_output: bfloat16 [32, 1024, 512], P(('dp', 'fsdp'))
- input_gradient: float32 [32, 1024, 512], P(('dp', 'fsdp'))
- global_norm: float32 [], replicated
- attend_gradient: float32 [512, 1536], P('fsdp')
- attend_newrows: float32 [512], P('fsdp')
- attend_newcols: float32 [1536], P('fsdp')
- attend_updated: float32 [512, 1536], P('fsdp')
- attend_bfloat: bfloat16 [512, 1536], P('fsdp')
- merger_gradient: float32 [512, 512], P('fsdp')
- merger_newrows: float32 [512], P('fsdp')
- merger_newcols: float32 [512], P('fsdp')
- merger_updated: float32 [512, 512], P('fsdp')
- merger_bfloat: bfloat16 [512, 512], P('fsdp')
- expand_gradient: float32 [512, 2048], P('fsdp')
- expand_newrows: float32 [512], P('fsdp')
- expand_newcols: float32 [2048], P('fsdp')
- expand_updated: float32 [512, 2048], P('fsdp')
- expand_bfloat: bfloat16 [512, 2048], P('fsdp')
- shrink_gradient: float32 [2048, 512], P('fsdp')
- shrink_newrows: float32 [2048], P('fsdp')
- shrink_newcols: float32 [512], P('fsdp')
- shrink_updated: float32 [2048, 512], P('fsdp')
- shrink_bfloat: bfloat16 [2048, 512], P('fsdp')
- vector_gradient: float32 [6, 512], P(None, 'fsdp')
- vector_variance: float32 [6, 512], P(None, 'fsdp')
- vector_updated: float32 [6, 512], P(None, 'fsdp')
The draws below stay inside these ranges and needn't reach their ends.
Inputs may be any that keep to these rules, and one draw needn't show every extreme that they name: Each row of 1024 slots holds documents of these lengths in order, then padding; a row's lengths sum to at most 1024; exactly one entry of each row equals 250, the others are shorter; zeros come only after the last document.
All inputs are finite; a program needn't handle non-finite values.
Results may differ from the reference program's by a relative error of at most 0.012.
The reference program's roundings to bfloat16 on the way count: a program that leaves them out, or rounds other values in their place, can miss the bound.
Values may be sent and summed in bfloat16 or wider, within the bound.
A program may use at most 192 MiB of HBM per device.

```python
import math
import jax
import jax.numpy as jnp
from jax import lax

D = 512
HEAD_DIM = 64
FF = 2048
SLOTS = 1024
OUTLIER = 250
STEP = 3
ROWS = 32
MAXDOCS = 256


def draw_tokens(key, part):
    key = jax.random.fold_in(key, 11)
    first_key, second_key = jax.random.split(key)
    position = jnp.arange(D, dtype=jnp.float32) / (D - 1)
    rising = 1.0 + 2.0 * position
    base = jax.random.normal(first_key, (ROWS, SLOTS, D), jnp.float32)
    jitter = jax.random.uniform(second_key, (D,), jnp.float32, 0.7, 1.3)
    return (base * rising * jitter).astype(jnp.bfloat16)


def draw_vectors(key, part):
    key = jax.random.fold_in(key, 29)
    first_key, second_key = jax.random.split(key)
    position = jnp.arange(D, dtype=jnp.float32) / (D - 1)
    rising = 1.0 + 2.0 * position
    spread = jax.random.uniform(first_key, (6, D), jnp.float32, 0.5, 0.9)
    noise = 0.5 * jax.random.normal(second_key, (6, D), jnp.float32)
    kinds = (jnp.arange(6, dtype=jnp.int32) % 3)[:, None]
    return jnp.where(kinds == 2, noise, rising[None, :] * spread)


def draw_lengths(key, part):
    key = jax.random.fold_in(key, 23)
    first_key, second_key, third_key = jax.random.split(key, 3)
    shorts = jax.random.randint(first_key, (ROWS, MAXDOCS), 4, max(6, SLOTS // 24), dtype=jnp.int32)
    outlier_place = jax.random.randint(second_key, (ROWS, 1), 0, 4, dtype=jnp.int32)
    columns = jnp.arange(MAXDOCS, dtype=jnp.int32)[None, :]
    wanted = jnp.where(columns == outlier_place, OUTLIER, shorts).astype(jnp.int32)
    row_total = jax.random.randint(third_key, (ROWS, 1), SLOTS * 5 // 8, SLOTS + 1, dtype=jnp.int32)
    before = jnp.cumsum(wanted, axis=1, dtype=jnp.int32) - wanted
    return jnp.clip(row_total - before, 0, wanted).astype(jnp.int32)


def block_levels(key, extent, shards, smallest, largest):
    loudness = 1.0
    for dim, parts in shards:
        draws = jax.random.uniform(jax.random.fold_in(jax.random.fold_in(key, 6), dim), (parts,), jnp.float32, smallest / len(shards), largest / len(shards))
        loudness = loudness * jnp.repeat(jnp.exp(draws), extent[dim] // parts).reshape((-1,) + (1,) * (len(extent) - 1 - dim))
    return loudness


def centred(stream_key, extent, scale, reach, cuts=(), kind=jnp.bfloat16):
    entries = scale * jax.random.normal(stream_key, extent, jnp.float32)
    if cuts:
        entries = entries * block_levels(stream_key, extent, cuts, -0.22, 0.18)
    return jnp.clip(entries, -reach, reach).astype(kind)


def setup_inputs(seed: int = 0) -> dict:
    key_of = jax.random.split(jax.random.key(seed), 18)
    return {
        "tokens": draw_tokens(jax.random.fold_in(key_of[17], 71), 0),
        "lengths": draw_lengths(jax.random.fold_in(key_of[17], 71), 0),
        "attend_weight": centred(key_of[2], (D, 3 * D), (2 * D) ** -0.5, 0.1875, ((0, 16),), jnp.float32),
        "merger_weight": centred(key_of[3], (D, D), (D // 16) ** -0.5, 1.0, ((0, 16),), jnp.float32),
        "expand_weight": centred(key_of[4], (D, FF), D ** -0.5, 0.25, ((0, 16),), jnp.float32),
        "shrink_weight": centred(key_of[5], (FF, D), FF ** -0.5, 0.125, ((0, 16),), jnp.float32),
        "vectors": draw_vectors(jax.random.fold_in(key_of[17], 71), 0),
        "attend_rows": jnp.clip(jnp.exp(math.log(8.89227635525458e-07) - 1.3862944 * jax.random.uniform(key_of[7], (D,), jnp.float32) ** block_levels(key_of[7], (D,), ((0, 16),), -0.2, 0.2)), 2.223069088813645e-07, 8.89227635525458e-07),
        "attend_columns": jnp.clip(jnp.exp(math.log(8.89227635525458e-07) - 1.3862944 * jax.random.uniform(key_of[8], (3 * D,), jnp.float32) ** block_levels(key_of[8], (3 * D,), ((0, 16),), -0.2, 0.2)), 2.223069088813645e-07, 8.89227635525458e-07),
        "merger_rows": jnp.clip(jnp.exp(math.log(4.446138035518743e-08) - 1.3862944 * jax.random.uniform(key_of[9], (D,), jnp.float32) ** block_levels(key_of[9], (D,), ((0, 16),), -0.2, 0.2)), 1.1115345088796857e-08, 4.446138035518743e-08),
        "merger_columns": jnp.clip(jnp.exp(math.log(4.446138035518743e-08) - 1.3862944 * jax.random.uniform(key_of[10], (D,), jnp.float32) ** block_levels(key_of[10], (D,), ((0, 16),), -0.2, 0.2)), 1.1115345088796857e-08, 4.446138035518743e-08),
        "expand_rows": jnp.clip(jnp.exp(math.log(5.0813007135275257e-08) - 1.3862944 * jax.random.uniform(key_of[11], (D,), jnp.float32) ** block_levels(key_of[11], (D,), ((0, 16),), -0.2, 0.2)), 1.2703251783818814e-08, 5.0813007135275257e-08),
        "expand_columns": jnp.clip(jnp.exp(math.log(5.0813007135275257e-08) - 1.3862944 * jax.random.uniform(key_of[12], (FF,), jnp.float32) ** block_levels(key_of[12], (FF,), ((0, 16),), -0.2, 0.2)), 1.2703251783818814e-08, 5.0813007135275257e-08),
        "shrink_rows": jnp.clip(jnp.exp(math.log(1.2703252139090182e-07) - 1.3862944 * jax.random.uniform(key_of[13], (FF,), jnp.float32) ** block_levels(key_of[13], (FF,), ((0, 16),), -0.2, 0.2)), 3.1758130347725455e-08, 1.2703252139090182e-07),
        "shrink_columns": jnp.clip(jnp.exp(math.log(1.2703252139090182e-07) - 1.3862944 * jax.random.uniform(key_of[14], (D,), jnp.float32) ** block_levels(key_of[14], (D,), ((0, 16),), -0.2, 0.2)), 3.1758130347725455e-08, 1.2703252139090182e-07),
        "vector_moments": jnp.clip(jnp.exp(math.log(3.4933943879877916e-06) - 1.3682759 * jax.random.uniform(key_of[15], (6, D), jnp.float32) ** block_levels(key_of[15], (6, D), ((1, 16),), -0.2, 0.2)), 8.89227635525458e-07, 3.4933943879877916e-06),
        "cotangent": centred(key_of[16], (ROWS, SLOTS, D), 1.0, 6.0, ((0, 32),)),
    }


EPSILON = 1e-05
TINY_VALUE = 1e-30
NEGATIVE = -1e+30
THRESHOLD = 1.0
UPDATE_LIMIT = 1.0
LEARN_RATE = 0.5

@jax.custom_vjp
def low(v):
    return lax.optimization_barrier(v.astype(jnp.bfloat16)).astype(jnp.float32)

@jax.custom_vjp
def low_back(v):
    return v

def low_keep(v):
    return (low(v), None)

def low_pass(kept, grad):
    return (grad,)

def back_keep(v):
    return (v, None)

def back_low(kept, grad):
    return (low(grad),)
low.defvjp(low_keep, low_pass)
low_back.defvjp(back_keep, back_low)

def both_round(values):
    return low(low_back(values))

def layout(lengths_row, slot_count):
    doc_ends = jnp.cumsum(lengths_row, dtype=jnp.int32)
    places = jnp.arange(slot_count, dtype=jnp.int32)
    segment = lax.optimization_barrier(jnp.sum((doc_ends[None, :] <= places[:, None]).astype(jnp.int32), axis=1, dtype=jnp.int32))
    valid_slot = places < doc_ends[-1]
    allowed = (segment[:, None] == segment[None, :]) & (places[None, :] <= places[:, None]) & valid_slot[None, :]
    allowed = allowed | (places[:, None] == places[None, :])
    return (allowed, valid_slot)

def norm_apply(values, gain_row, shift_row):
    centered = values - lax.optimization_barrier(jnp.mean(values, axis=-1, keepdims=True))
    scale_inv = lax.rsqrt(lax.optimization_barrier(jnp.mean(centered * centered, axis=-1, keepdims=True)) + EPSILON)
    return centered * scale_inv * gain_row + shift_row

def attend_row(pieces):
    queries, keys_all, values_all, allowed = pieces
    raw_scores = low_back(jnp.einsum('qhd,khd->hqk', queries, keys_all, precision=lax.Precision.HIGHEST))
    scores = jnp.where(allowed[None], raw_scores * 0.125, NEGATIVE)
    highest = lax.optimization_barrier(jnp.max(scores, axis=-1, keepdims=True))
    expone = jnp.exp(scores - highest)
    probs = low(expone / lax.optimization_barrier(jnp.sum(expone, axis=-1, keepdims=True)))
    return jnp.einsum('hqk,khd->qhd', probs, values_all, precision=lax.Precision.HIGHEST)

def block_forward(params, inputs, allowed):
    attend_matrix = low(params[0])
    merger_matrix = low(params[1])
    expand_matrix = low(params[2])
    shrink_matrix = low(params[3])
    vector_rows = low(params[4])
    groups, length, width = inputs.shape
    heads = width // HEAD_DIM
    projected = both_round(jnp.einsum('gsd,de->gse', inputs, attend_matrix, precision=lax.Precision.HIGHEST))
    queries = projected[..., :width].reshape(groups, length, heads, HEAD_DIM)
    keys_all = projected[..., width:2 * width].reshape(groups, length, heads, HEAD_DIM)
    values_all = projected[..., 2 * width:].reshape(groups, length, heads, HEAD_DIM)
    context = lax.map(jax.checkpoint(attend_row), (queries, keys_all, values_all, allowed))
    context = both_round(context.reshape(groups, length, width))
    branch = low_back(jnp.einsum('gse,ed->gsd', context, merger_matrix, precision=lax.Precision.HIGHEST))
    first_out = norm_apply(vector_rows[0] * inputs + branch, vector_rows[1], vector_rows[2])
    hidden = low_back(jnp.einsum('gsd,df->gsf', low(first_out), expand_matrix, precision=lax.Precision.HIGHEST))
    active = low(jax.nn.gelu(hidden))
    second_sum = vector_rows[3] * first_out + low_back(jnp.einsum('gsf,fd->gsd', active, shrink_matrix, precision=lax.Precision.HIGHEST))
    return norm_apply(second_sum, vector_rows[4], vector_rows[5])

def factored(gradient, weight, rows_old, cols_old, clip, forget):
    clipped = clip * gradient
    square = clipped * clipped + TINY_VALUE
    new_rows = forget * rows_old + (1.0 - forget) * lax.optimization_barrier(jnp.mean(square, axis=1))
    new_cols = forget * cols_old + (1.0 - forget) * lax.optimization_barrier(jnp.mean(square, axis=0))
    estimate = new_rows[:, None] * new_cols[None, :] / jnp.mean(new_rows)
    update = clipped * lax.rsqrt(estimate)
    update = update / jnp.maximum(1.0, jnp.sqrt(jnp.mean(update * update)) / UPDATE_LIMIT)
    stride = LEARN_RATE * jnp.maximum(0.001, jnp.sqrt(jnp.mean(weight * weight)))
    updated = weight - stride * update
    return (clipped, new_rows, new_cols, updated, updated.astype(jnp.bfloat16))

def reference(tokens, lengths, attend_weight, merger_weight, expand_weight, shrink_weight, vectors, attend_rows, attend_columns, merger_rows, merger_columns, expand_rows, expand_columns, shrink_rows, shrink_columns, vector_moments, cotangent):
    params = (attend_weight, merger_weight, expand_weight, shrink_weight, vectors)
    group_rows = 4
    group_count = ROWS // group_rows
    token_groups = tokens.reshape(group_count, group_rows, SLOTS, D)
    length_groups = lengths.reshape(group_count, group_rows, MAXDOCS)
    cotangent_groups = cotangent.reshape(group_count, group_rows, SLOTS, D)

    def one_group(running, pieces):
        token_block, length_block, cotangent_block = pieces
        allowed, valid_slot = jax.vmap(lambda row_lengths: layout(row_lengths, SLOTS))(length_block)
        inputs = token_block.astype(jnp.float32)
        result, pull = jax.vjp(lambda weights_now, inputs_now: block_forward(weights_now, inputs_now, allowed), params, inputs)
        arriving = cotangent_block.astype(jnp.float32) * valid_slot[..., None].astype(jnp.float32)
        weight_grads, input_grad = pull(arriving)
        running = jax.tree.map(jnp.add, running, weight_grads)
        return (running, (result.astype(jnp.bfloat16), input_grad))
    zeros = jax.tree.map(jnp.zeros_like, params)
    summed, (outputs, input_grads) = lax.scan(one_group, zeros, (token_groups, length_groups, cotangent_groups))
    block_output = outputs.reshape(ROWS, SLOTS, D)
    input_gradient = input_grads.reshape(ROWS, SLOTS, D)
    total_square = jnp.sum(summed[0] * summed[0]) + jnp.sum(summed[1] * summed[1]) + jnp.sum(summed[2] * summed[2]) + jnp.sum(summed[3] * summed[3]) + jnp.sum(summed[4] * summed[4])
    global_norm = jnp.sqrt(total_square)
    clip = jnp.minimum(1.0, THRESHOLD / global_norm)
    forget = 1.0 - float(STEP) ** (-0.8)
    attend_out = factored(summed[0], attend_weight, attend_rows, attend_columns, clip, forget)
    merger_out = factored(summed[1], merger_weight, merger_rows, merger_columns, clip, forget)
    expand_out = factored(summed[2], expand_weight, expand_rows, expand_columns, clip, forget)
    shrink_out = factored(summed[3], shrink_weight, shrink_rows, shrink_columns, clip, forget)
    vector_gradient = clip * summed[4]
    vector_variance = forget * vector_moments + (1.0 - forget) * (vector_gradient * vector_gradient + TINY_VALUE)
    update = vector_gradient * lax.rsqrt(vector_variance)
    update = update / jnp.maximum(1.0, jnp.sqrt(lax.optimization_barrier(jnp.mean(update * update, axis=1, keepdims=True))) / UPDATE_LIMIT)
    stride = LEARN_RATE * jnp.maximum(0.001, jnp.sqrt(lax.optimization_barrier(jnp.mean(vectors * vectors, axis=1, keepdims=True))))
    vector_updated = vectors - stride * update
    return (block_output, input_gradient, global_norm, attend_out[0], attend_out[1], attend_out[2], attend_out[3], attend_out[4], merger_out[0], merger_out[1], merger_out[2], merger_out[3], merger_out[4], expand_out[0], expand_out[1], expand_out[2], expand_out[3], expand_out[4], shrink_out[0], shrink_out[1], shrink_out[2], shrink_out[3], shrink_out[4], vector_gradient, vector_variance, vector_updated)
```

```python
import functools

import jax
import jax.numpy as jnp
from jax import lax
from jax.experimental import pallas as pl
from jax.experimental.pallas import tpu as pltpu
from jax.sharding import PartitionSpec as P

F32 = jnp.float32
BF16 = jnp.bfloat16
HEAD_DIM = 64
STEP = 3
EPSILON = 1e-05
TINY_VALUE = 1e-30
NEGATIVE = -1e30
THRESHOLD = 1.0
UPDATE_LIMIT = 1.0
LEARN_RATE = 0.5
FORGET = 1.0 - float(STEP) ** (-0.8)
LOG2_E = 1.4426950408889634
GELU_A = 0.7978845608028654
GELU_B = 0.044715 * GELU_A

REACH = 256
QUERY_BLOCK = 256
TILE = 256
GROUP = 4
DP, FSDP = "dp", "fsdp"
ATTEND, MERGER, EXPAND, SHRINK = "attend", "merger", "expand", "shrink"
MATRICES = (ATTEND, MERGER, EXPAND, SHRINK)
MESH = pl.DeviceIdType.MESH
VMEM_LIMIT = 63 << 20


def dot_general(left, right, left_dim, right_dim):
    return lax.dot_general(
        left, right, (((left_dim,), (right_dim,)), ((), ())), preferred_element_type=F32
    )


def dot_nn(left, right):
    return dot_general(left, right, 1, 0)


def dot_nt(left, right):
    return dot_general(left, right, 1, 1)


def dot_tn(left, right):
    return dot_general(left, right, 0, 0)


def flat(value):
    return value.reshape(-1, value.shape[-1])


def fold_rows(value):
    return jnp.sum(value.reshape(value.shape[0] // 8, 8, value.shape[1]), axis=0)


def fold_lanes(row):
    total = row[:, :128]
    for start in range(128, row.shape[1], 128):
        total = total + row[:, start : start + 128]
    return total


def diagonal(size):
    return lax.broadcasted_iota(jnp.int32, (size, size), 0) == lax.broadcasted_iota(
        jnp.int32, (size, size), 1
    )


def column_of(row):
    size = row.shape[1]
    return jnp.sum(jnp.where(diagonal(size), row, 0.0), axis=1, keepdims=True)


def row_of(column):
    size = column.shape[0]
    return jnp.sum(jnp.where(diagonal(size), column, 0.0), axis=0, keepdims=True)


def lane_mean(value):
    return jnp.mean(value, axis=-1, keepdims=True)


def aligned(start, size):
    return pl.ds(pl.multiple_of(start, size), size)


def band(slots):
    pieces = []
    place = 0
    for first in range(0, slots, QUERY_BLOCK):
        low = max(0, first - REACH)
        high = first + QUERY_BLOCK
        pieces.append((first, low, high, place))
        place += high - low
    return pieces, place


def prepare(r):
    slots = r.tokens.shape[0]
    count = r.lengths.shape[1]
    for start in range(0, slots, TILE):
        r.tokens_t[:, start : start + TILE] = r.tokens[start : start + TILE, :].T
    lengths = r.lengths[...].astype(F32)
    rows = jnp.broadcast_to(lengths, (8, count)).astype(BF16)
    upto = lax.broadcasted_iota(jnp.int32, (count, count), 1) <= lax.broadcasted_iota(
        jnp.int32, (count, count), 0
    )
    ends = dot_nt(jnp.where(upto, 1.0, 0.0).astype(BF16), rows)[:, 0:1]
    places = lax.broadcasted_iota(jnp.int32, (count, slots), 1).astype(F32)
    ended = jnp.where(ends <= places, 1.0, 0.0).astype(BF16)
    begin = dot_nn(rows, ended)[0:1, :]
    total = jnp.sum(lengths, axis=1, keepdims=True)
    r.total[...] = jnp.broadcast_to(total, r.total.shape)
    slot = lax.broadcasted_iota(jnp.int32, (1, slots), 1).astype(F32)
    begin = jnp.where(slot < total, begin, slot)
    for first, low, high, place in band(slots)[0]:
        key = (lax.broadcasted_iota(jnp.int32, (high - low, QUERY_BLOCK), 0) + low).astype(F32)
        query = slot[:, first : first + QUERY_BLOCK]
        fits = (key >= begin[:, first : first + QUERY_BLOCK]) & (key <= query)
        r.mask[place : place + high - low, :] = jnp.where(fits, 1.0, 0.0).astype(BF16)


def project(r):
    width = r.tokens.shape[1]

    def tile(step, carry):
        columns = aligned(step * TILE, TILE)
        r.projected_t[columns, :] = dot_tn(flat(r.attend[..., columns]), r.tokens_t[...]).astype(
            BF16
        )
        return carry

    lax.fori_loop(0, 3 * width // TILE, tile, 0)

    def turn(step, carry):
        columns = aligned(step * TILE, TILE)
        r.key_value[:, columns] = r.projected_t[aligned(width + step * TILE, TILE), :].T
        return carry

    lax.fori_loop(0, 2 * width // TILE, turn, 0)


def beside_zeros(value, head):
    zeros = jnp.zeros_like(value)
    return jnp.concatenate([value, zeros] if head == 0 else [zeros, value], axis=0)


def attend_forward(r, hooks):
    slots, width = r.tokens.shape
    factor = HEAD_DIM ** -0.5 * LOG2_E

    def pair(step, carry):
        for at, hook in hooks:
            pl.when(step == at)(hook)
        start = pl.multiple_of(step * 128, 128)
        for first, low, high, place in band(slots)[0]:
            keys = r.key_value[low:high, pl.ds(start, 128)]
            fits = r.mask[place : place + high - low, :].astype(F32) > 0.5
            for head in (0, 1):
                mine = pl.ds(start + 64 * head, 64)
                queries = r.projected_t[mine, first : first + QUERY_BLOCK]
                scores = dot_nn(keys, beside_zeros(queries, head))
                scores = jnp.where(fits, scores * factor, NEGATIVE)
                highest = jnp.max(scores, axis=0, keepdims=True)
                weights = jnp.exp2(scores - highest)
                inverse = 1.0 / jnp.sum(weights, axis=0, keepdims=True)
                probs = (weights * inverse).astype(BF16)
                r.probs[2 * step + head, place : place + high - low, :] = probs
                values = r.projected_t[pl.ds(2 * width + start + 64 * head, 64), low:high]
                r.context_t[mine, first : first + QUERY_BLOCK] = dot_nn(values, probs).astype(BF16)
        return carry

    lax.fori_loop(0, width // 128, pair, 0)


def attend_backward(r, hooks):
    slots, width = r.tokens.shape
    scale = HEAD_DIM ** -0.5

    def pair(step, carry):
        for at, hook in hooks:
            pl.when(step == at)(hook)
        start = pl.multiple_of(step * 128, 128)
        for head in (0, 1):
            mine = pl.ds(start + 64 * head, 64)
            mine_keys = pl.ds(width + start + 64 * head, 64)
            mine_values = pl.ds(2 * width + start + 64 * head, 64)
            queries = r.projected_t[mine, :]
            keys_t = r.projected_t[mine_keys, :]
            upstream = r.d_context_t[mine, :]
            open_keys = None
            open_values = None
            for first, low, high, place in band(slots)[0]:
                values = r.key_value[low:high, pl.ds(width + start, 128)]
                arriving = upstream[:, first : first + QUERY_BLOCK]
                d_probs = dot_nn(values, beside_zeros(arriving, head))
                probs = r.probs[2 * step + head, place : place + high - low, :]
                wide = probs.astype(F32)
                inner = jnp.sum(wide * d_probs, axis=0, keepdims=True)
                d_scores = (wide * (d_probs - inner)).astype(BF16)
                r.projected_t[mine, first : first + QUERY_BLOCK] = (
                    dot_nn(keys_t[:, low:high], d_scores) * scale
                ).astype(BF16)
                d_keys = dot_nt(queries[:, first : first + QUERY_BLOCK], d_scores)
                d_values = dot_nt(arriving, probs)
                done = first - low
                if done:
                    r.projected_t[mine_keys, low:first] = (
                        (open_keys + d_keys[:, :done]) * scale
                    ).astype(BF16)
                    r.projected_t[mine_values, low:first] = (
                        open_values + d_values[:, :done]
                    ).astype(BF16)
                open_keys = d_keys[:, done:]
                open_values = d_values[:, done:]
            r.projected_t[mine_keys, slots - QUERY_BLOCK :] = (open_keys * scale).astype(BF16)
            r.projected_t[mine_values, slots - QUERY_BLOCK :] = open_values.astype(BF16)
        return carry

    lax.fori_loop(0, width // 128, pair, 0)


def feed_forward(r):
    slots, width = r.tokens.shape
    r.vector_sums[...] = jnp.zeros_like(r.vector_sums)

    def block(step, carry):
        rows = aligned(step * TILE, TILE)
        omega_one, gain_one, shift_one, omega_two, gain_two, shift_two = [
            r.vectors[place : place + 1, :] for place in range(6)
        ]
        inputs = r.tokens[rows, :].astype(F32)
        first_sum = omega_one * inputs + dot_tn(r.context_t[:, rows], flat(r.merger[...]))
        centered = first_sum - lane_mean(first_sum)
        first_inv = lax.rsqrt(lane_mean(centered * centered) + EPSILON)
        first_normed = centered * first_inv
        first_out = first_normed * gain_one + shift_one
        first_low = first_out.astype(BF16)
        r.first_t[:, rows] = first_low.T
        hidden = dot_nn(first_low, flat(r.expand[...]))
        square = hidden * hidden
        bend = jnp.tanh(hidden * (GELU_A + GELU_B * square))
        half = 0.5 * hidden
        lifted = 1.0 + bend
        active = (half * lifted).astype(BF16)
        r.slope[...] = 0.5 * lifted + half * (1.0 - bend * bend) * (GELU_A + 3 * GELU_B * square)
        r.active[rows, :] = active
        second_sum = omega_two * first_out + dot_nn(active, flat(r.shrink[...]))
        centered = second_sum - lane_mean(second_sum)
        second_inv = lax.rsqrt(lane_mean(centered * centered) + EPSILON)
        second_normed = centered * second_inv
        arriving = r.cotangent[rows, :].astype(F32)
        r.result[rows, :] = (second_normed * gain_two + shift_two).astype(BF16)
        place = (lax.broadcasted_iota(jnp.int32, (TILE, 1), 0) + step * TILE).astype(F32)
        upstream = arriving * jnp.where(place < r.total[0:1, 0:1], 1.0, 0.0)
        scaled = upstream * gain_two
        d_second = second_inv * (
            scaled - lane_mean(scaled) - second_normed * lane_mean(scaled * second_normed)
        )
        r.vector_sums[4] += fold_rows(upstream * second_normed)
        r.vector_sums[5] += fold_rows(upstream)
        r.vector_sums[3] += fold_rows(first_out * d_second)
        second_low = d_second.astype(BF16)
        r.d_second_t[:, rows] = second_low.T
        d_hidden = (dot_nt(second_low, flat(r.shrink[...])) * r.slope[...]).astype(BF16)
        r.d_hidden[rows, :] = d_hidden
        d_first = dot_nt(d_hidden, flat(r.expand[...])) + omega_two * d_second
        r.vector_sums[1] += fold_rows(d_first * first_normed)
        r.vector_sums[2] += fold_rows(d_first)
        scaled = d_first * gain_one
        d_first_sum = first_inv * (
            scaled - lane_mean(scaled) - first_normed * lane_mean(scaled * first_normed)
        )
        r.vector_sums[0] += fold_rows(inputs * d_first_sum)
        r.straight[rows, :] = omega_one * d_first_sum
        branch_low = d_first_sum.astype(BF16)
        r.d_branch[rows, :] = branch_low
        r.d_context_t[:, rows] = dot_nt(flat(r.merger[...]), branch_low).astype(BF16)
        return carry

    lax.fori_loop(0, slots // TILE, block, 0)


def vector_total(r):
    rows = [jnp.sum(r.vector_sums[place], axis=0, keepdims=True) for place in range(6)]
    return jnp.concatenate(rows + [jnp.zeros((2, rows[0].shape[1]), F32)], axis=0)


def by_columns(columns, store):
    def tile(step, carry):
        store(step)
        return carry

    lax.fori_loop(0, columns // TILE, tile, 0)


def put_tile(ref, columns, value):
    ref[..., columns] = value.astype(ref.dtype).reshape(ref.shape[:-1] + (value.shape[1],))


def shrink_gradient(r):
    width, wide = r.tokens.shape[1], r.active.shape[1]
    if len(r.g_shrink.shape) == 2:

        def store(step):
            columns = aligned(step * TILE, TILE)
            r.g_shrink[:, columns] = dot_nn(r.d_second_t[...], r.active[:, columns]).astype(
                r.g_shrink.dtype
            )

        by_columns(wide, store)
        return
    owned = r.g_shrink.shape[-1]
    per_tile = max(1, TILE // owned)
    span = owned * per_tile

    def tile(step, carry):
        value = dot_nn(r.d_second_t[...], r.active[:, aligned(step * span, span)]).astype(BF16)
        for piece in range(per_tile):
            owner = step * per_tile + piece
            r.g_shrink[owner // GROUP, lax.rem(owner, GROUP)] = value[
                :, piece * owned : (piece + 1) * owned
            ].reshape(2, width // 2, owned)
        return carry

    lax.fori_loop(0, wide // span, tile, 0)


def expand_gradient(r):
    def store(step):
        columns = aligned(step * TILE, TILE)
        put_tile(r.g_expand, columns, dot_nn(r.first_t[...], r.d_hidden[:, columns]))

    by_columns(r.active.shape[1], store)


def merger_gradient(r):
    def store(step):
        columns = aligned(step * TILE, TILE)
        put_tile(r.g_merger, columns, dot_nn(r.context_t[...], r.d_branch[:, columns]))

    by_columns(r.tokens.shape[1], store)


def attend_gradient(r):
    def store(step):
        columns = aligned(step * TILE, TILE)
        put_tile(r.g_attend, columns, dot_nt(r.tokens_t[...], r.projected_t[columns, :]))

    by_columns(3 * r.tokens.shape[1], store)


def input_gradient(r):
    def tile(step, carry):
        rows = aligned(step * TILE, TILE)
        r.straight[rows, :] += dot_nn(flat(r.attend[...]), r.projected_t[:, rows]).T
        return carry

    lax.fori_loop(0, r.tokens.shape[0] // TILE, tile, 0)


def row_scratch(slots, width, wide):
    packed = band(slots)[1]
    heads = width // HEAD_DIM
    return dict(
        tokens_t=pltpu.VMEM((width, slots), BF16),
        mask=pltpu.VMEM((packed, QUERY_BLOCK), BF16),
        total=pltpu.VMEM((8, 128), F32),
        projected_t=pltpu.VMEM((3 * width, slots), BF16),
        key_value=pltpu.VMEM((slots, 2 * width), BF16),
        probs=pltpu.VMEM((heads, packed, QUERY_BLOCK), BF16),
        context_t=pltpu.VMEM((width, slots), BF16),
        d_context_t=pltpu.VMEM((width, slots), BF16),
        active=pltpu.VMEM((slots, wide), BF16),
        d_hidden=pltpu.VMEM((slots, wide), BF16),
        first_t=pltpu.VMEM((width, slots), BF16),
        d_second_t=pltpu.VMEM((width, slots), BF16),
        vector_sums=pltpu.VMEM((6, 8, width), F32),
        slope=pltpu.VMEM((TILE, wide), F32),
    )


class Refs:
    def __init__(self, names, refs):
        for name, ref in zip(names, refs, strict=True):
            setattr(self, name, ref)


def spread_rows(width, columns_of):
    places = {}
    start = 0
    for name in MATRICES:
        places[name] = (start, columns_of[name] // width)
        start += columns_of[name] // width
    return places, start


def joined(ref, start, count):
    return jnp.concatenate([ref[place : place + 1, :] for place in range(start, start + count)], 1)


def split_into(ref, start, row, width):
    for piece in range(row.shape[1] // width):
        ref[start + piece : start + piece + 1, :] = row[:, piece * width : (piece + 1) * width]


def scalar_sum(value):
    return jnp.sum(jnp.sum(value, axis=1, keepdims=True), axis=0, keepdims=True)


def clip_of(columns_ref, places, vector_gradient):
    squares = {
        name: scalar_sum(joined(columns_ref, *places[name])) for name in MATRICES
    }
    total = scalar_sum(vector_gradient * vector_gradient)
    for name in MATRICES:
        total = total + squares[name]
    norm = jnp.sqrt(total)
    return norm, jnp.minimum(1.0, THRESHOLD / norm), squares


def factored_step(name, gradient, rows_old, columns_ref, early_ref, places, clip, squares, rows_all):
    start, count = places[name]
    wide = gradient.shape[1]
    power = clip * clip
    row_mean = jnp.sum(gradient * gradient, axis=1, keepdims=True) * (1.0 / wide)
    new_rows = FORGET * column_of(rows_old) + (1.0 - FORGET) * (power * row_mean + TINY_VALUE)
    new_columns = FORGET * joined(early_ref, start, count) + (1.0 - FORGET) * (
        power * (joined(columns_ref, start, count) * (1.0 / rows_all)) + TINY_VALUE
    )
    old = early_ref[ROW_SUMS : ROW_SUMS + 1, :]
    at = MATRICES.index(name) * 128
    old_mean = jnp.sum(old[:, at : at + 128], axis=1, keepdims=True) * (1.0 / rows_all)
    mean = FORGET * old_mean + (1.0 - FORGET) * (
        power * (squares[name] * (1.0 / (rows_all * wide))) + TINY_VALUE
    )
    clipped = clip * gradient
    step = clipped * lax.rsqrt(new_rows * new_columns * (1.0 / mean))
    return clipped, new_rows, new_columns, step


def vector_steps(gradient, moments, clip):
    clipped = clip * gradient
    variance = FORGET * moments + (1.0 - FORGET) * (clipped * clipped + TINY_VALUE)
    return clipped, variance, clipped * lax.rsqrt(variance)


SQUARES = 9
ROW_SUMS = 10
VECTORS = 16
MOMENTS = 24
EARLY_ROWS = 32
COLUMN_ROWS = 16


def shard_kernel(layout_sizes, names, *refs):
    outer, width, wide = layout_sizes
    r = Refs(names, refs)
    r.result = r.cotangent
    r.d_branch = r.tokens
    core = lax.axis_index(DP)
    chip = lax.axis_index(FSDP)
    far = chip // GROUP
    near = lax.rem(chip, GROUP)
    sibling = (1 - core, chip)
    near_steps = range(1, GROUP)
    far_steps = range(1, outer)

    def at_near(step):
        return jnp.bitwise_xor(near, step)

    def at_far(step):
        return lax.rem(far + step, outer)

    def from_far(step):
        return lax.rem(far + outer - step, outer)

    def near_device(step):
        return (core, far * GROUP + at_near(step))

    def far_device(step):
        return (core, at_far(step) * GROUP + near)

    def remote(source, target, device, sends, receives, index):
        return pltpu.make_async_remote_copy(
            src_ref=source,
            dst_ref=target,
            send_sem=sends.at[index],
            recv_sem=receives.at[index],
            device_id=device,
            device_id_type=MESH,
        )

    def start(copy):
        copy.start()

    def local(source, target, index):
        return pltpu.make_async_copy(source, target, r.local_sems.at[index])

    load_tokens = local(r.tokens_in, r.tokens, 0)
    load_cotangent = local(r.cotangent_in, r.cotangent, 1)
    load_tokens.start()
    load_cotangent.start()

    barrier = pltpu.get_barrier_semaphore()
    for step in near_steps:
        pl.semaphore_signal(barrier, inc=1, device_id=near_device(step), device_id_type=MESH)
    for step in far_steps:
        pl.semaphore_signal(barrier, inc=1, device_id=far_device(step), device_id_type=MESH)
    pl.semaphore_signal(barrier, inc=1, device_id=sibling, device_id_type=MESH)
    pl.semaphore_wait(barrier, len(near_steps) + len(far_steps) + 1)


    class Sum:
        def __init__(self, name):
            self.near = getattr(r, name + "_near")
            self.far = getattr(r, name + "_far")
            self.sends = getattr(r, name + "_sends")
            self.receives = getattr(r, name + "_receives")

        def begin(self, value=None):
            if value is not None:
                self.near[near] = value
            for step in near_steps:
                start(
                    remote(
                        self.near.at[near], self.near.at[near], near_device(step),
                        self.sends, self.receives, step - 1,
                    )
                )

        def turn(self):
            for step in near_steps:
                slot = self.near.at[at_near(step)]
                remote(
                    slot, slot, near_device(step), self.sends, self.receives, step - 1
                ).wait_recv()
            self.far[far] = jnp.sum(self.near[...], axis=0)
            for step in far_steps:
                start(
                    remote(
                        self.far.at[far], self.far.at[far], far_device(step),
                        self.sends, self.receives, GROUP + step - 1,
                    )
                )

        def end(self):
            for step in far_steps:
                slot = self.far.at[from_far(step)]
                remote(
                    slot, slot, far_device(step), self.sends, self.receives, GROUP + step - 1
                ).wait_recv()
            return jnp.sum(self.far[...], axis=0)


    class Gather:
        def __init__(self, name):
            self.held = getattr(r, name)
            self.sends = getattr(r, name + "_sends")
            self.receives = getattr(r, name + "_receives")

        def far_copy(self, step, slot):
            ref = self.held.at[slot, near, core]
            return remote(ref, ref, far_device(step), self.sends, self.receives, step - 1)

        def near_copy(self, step, back, slot):
            ref = self.held.at[slot, near if back is None else back, core]
            index = outer + (step - 1) * outer
            return remote(ref, ref, near_device(step), self.sends, self.receives, index)

        def cross(self, step, half, whose):
            ref = self.held.at[:, whose, half]
            index = outer * GROUP + step
            return remote(ref, ref, sibling, self.sends, self.receives, index)

        def near_piece(self, step, hop, whose, half):
            ref = self.held.at[from_far(hop) if hop else far, whose, half]
            index = outer + (step - 1) * outer + hop
            return remote(ref, ref, near_device(step), self.sends, self.receives, index)

        def place(self, shard):
            rows = shard.shape[0] // 2
            mine = shard[pl.ds(pl.multiple_of(core * rows, rows), rows), :]
            self.held[far, near, core] = mine.astype(BF16)

        def begin(self):
            for step in far_steps:
                start(self.far_copy(step, far))
            for step in near_steps:
                start(self.near_piece(step, 0, near, core))

        def turn(self):
            for hop in far_steps:
                self.far_copy(hop, from_far(hop)).wait_recv()
                for step in near_steps:
                    start(self.near_piece(step, hop, near, core))
            start(self.cross(0, core, near))

        def pass_on(self):
            for step in near_steps:
                for hop in range(outer):
                    self.near_piece(step, hop, at_near(step), core).wait_recv()
                start(self.cross(step, core, at_near(step)))

        def end(self):
            for step in range(GROUP):
                self.cross(step, 1 - core, at_near(step) if step else near).wait_recv()


    class Reduce:
        def __init__(self, name):
            for part in ("g", "pair", "near", "far", "done"):
                setattr(self, part, getattr(r, part + "_" + name))
            self.sends = getattr(r, "sum_" + name + "_sends")
            self.receives = getattr(r, "sum_" + name + "_receives")

        def pair_copy(self):
            return remote(
                self.g.at[:, :, 1 - core], self.pair, sibling, self.sends, self.receives, 0
            )

        def near_copy(self, step):
            return remote(
                self.pair.at[:, at_near(step)], self.near.at[step - 1], near_device(step),
                self.sends, self.receives, step,
            )

        def far_copy(self, step):
            return remote(
                self.pair.at[at_far(step), near], self.far.at[step - 1], far_device(step),
                self.sends, self.receives, GROUP + step - 1,
            )

        def done_copy(self, half):
            ref = self.done.at[half]
            return remote(ref, ref, sibling, self.sends, self.receives, GROUP + outer)

        def begin(self):
            start(self.pair_copy())

        def turn(self):
            self.pair_copy().wait_recv()

            def block(step, carry):
                both = self.g[step, :, core].astype(F32) + self.pair[step].astype(F32)
                self.pair[step] = both.astype(BF16)
                return carry

            lax.fori_loop(0, outer, block, 0)
            for step in near_steps:
                start(self.near_copy(step))

        def pass_on(self):
            for step in near_steps:
                self.near_copy(step).wait_recv()

            def block(step, carry):
                total = self.pair[step, near].astype(F32)
                for other in near_steps:
                    total = total + self.near[other - 1, step].astype(F32)
                self.pair[step, near] = total.astype(BF16)
                return carry

            lax.fori_loop(0, outer, block, 0)
            for step in far_steps:
                start(self.far_copy(step))

        def collect(self):
            for step in far_steps:
                self.far_copy(step).wait_recv()
            total = self.pair[far, near].astype(F32)
            for step in far_steps:
                total = total + self.far[step - 1].astype(F32)
            self.done[core] = total
            start(self.done_copy(core))

        def end(self):
            self.done_copy(1 - core).wait_recv()

    early = Sum("early")
    vector_sum = Sum("vector")
    column_sum = Sum("column")
    step_sum = Sum("step")
    gathers = {name: Gather(name) for name in MATRICES}
    sums = {name: Reduce(name) for name in MATRICES}
    shards = {name: getattr(r, name + "_weight") for name in MATRICES}

    gathers[ATTEND].place(shards[ATTEND])
    gathers[ATTEND].begin()


    columns_of = {name: getattr(r, name + "_columns").shape[1] * outer * GROUP for name in MATRICES}
    places, _ = spread_rows(width, columns_of)
    r.early_own[...] = jnp.zeros_like(r.early_own)
    r.spread[...] = jnp.zeros_like(r.spread)
    for name in MATRICES:
        row, count = places[name]
        own = getattr(r, name + "_columns")
        size = own.shape[1]
        if count == 1:
            r.early_own[row : row + 1, 0:size] = own[...]
        else:
            r.spread[0:1, 0:size] = own[...]
            whole = pltpu.roll(r.spread[:, : columns_of[name]], chip * size, 1)[0:1, :]
            split_into(r.early_wide, row, whole, width)
            r.spread[0:1, 0:size] = jnp.zeros_like(own)
        at = MATRICES.index(name) * 128
        shard = shards[name][...]
        r.early_wide[SQUARES : SQUARES + 1, at : at + 128] = fold_lanes(
            jnp.sum(fold_rows(shard * shard), axis=0, keepdims=True)
        )
        rows_old = getattr(r, name + "_rows")
        sums_row = jnp.broadcast_to(jnp.sum(rows_old[...], axis=1, keepdims=True), (1, 128))
        first_lane = lax.broadcasted_iota(jnp.int32, (1, 128), 1) == 0
        r.early_wide[ROW_SUMS : ROW_SUMS + 1, at : at + 128] = jnp.where(first_lane, sums_row, 0.0)
    thin = r.vectors_own.shape[1]
    r.early_own[VECTORS : VECTORS + 6, 0:thin] = r.vectors_own[...]
    r.early_own[MOMENTS : MOMENTS + 6, 0:thin] = r.moments_own[...]
    narrow = pltpu.roll(r.early_own[...], chip * thin, 1)
    kind = lax.broadcasted_iota(jnp.int32, narrow.shape, 0)
    taken = kind >= VECTORS
    for name in MATRICES:
        row, count = places[name]
        if count == 1:
            taken = taken | (kind == row)
    filled = kind <= ROW_SUMS
    early.begin(
        jnp.where(taken, narrow, jnp.where(filled, r.early_wide[...], 0.0))
    )


    for name in (MERGER, EXPAND, SHRINK):
        gathers[name].place(shards[name])
    load_tokens.wait()
    prepare(r)
    gathers[ATTEND].turn()
    gathers[MERGER].begin()
    gathers[EXPAND].begin()
    early.turn()
    gathers[ATTEND].pass_on()
    gathers[SHRINK].begin()
    gathers[ATTEND].end()
    project(r)
    gathers[MERGER].turn()
    gathers[EXPAND].turn()

    def second_hook():
        gathers[SHRINK].turn()

    def third_hook():
        gathers[MERGER].pass_on()

    attend_forward(r, ((1, second_hook), (2, third_hook)))
    gathers[EXPAND].pass_on()
    gathers[SHRINK].pass_on()
    r.early[...] = early.end()
    r.vectors[...] = r.early[VECTORS : VECTORS + 8, :].astype(BF16).astype(F32)
    for name in (MERGER, EXPAND, SHRINK):
        gathers[name].end()
    load_cotangent.wait()
    feed_forward(r)
    store_result = local(r.result, r.result_out, 0)
    store_result.start()


    r.vector_pair[core] = vector_total(r)
    vector_copy = remote(
        r.vector_pair.at[core], r.vector_pair.at[core], sibling,
        r.vector_sends, r.vector_receives, GROUP + outer,
    )
    vector_copy.start()
    shrink_gradient(r)
    sums[SHRINK].begin()
    expand_gradient(r)
    sums[EXPAND].begin()
    sums[SHRINK].turn()
    merger_gradient(r)
    sums[MERGER].begin()
    sums[EXPAND].turn()
    remote(
        r.vector_pair.at[1 - core], r.vector_pair.at[1 - core], sibling,
        r.vector_sends, r.vector_receives, GROUP + outer,
    ).wait_recv()
    vector_sum.begin(r.vector_pair[0] + r.vector_pair[1])

    def merger_hook():
        sums[MERGER].turn()
        vector_sum.turn()

    def shrink_hook():
        sums[SHRINK].pass_on()

    attend_backward(r, ((1, merger_hook), (3, shrink_hook)))
    attend_gradient(r)
    sums[ATTEND].begin()
    sums[EXPAND].pass_on()
    sums[ATTEND].turn()
    sums[MERGER].pass_on()
    input_gradient(r)
    store_input = local(r.straight, r.input_out, 1)
    store_input.start()
    r.vector_out[...] = vector_sum.end()
    sums[SHRINK].collect()
    sums[EXPAND].collect()
    sums[ATTEND].pass_on()
    sums[MERGER].collect()
    sums[ATTEND].collect()


    r.column_near[near] = jnp.zeros(r.column_near.shape[1:], F32)
    grads = {}
    for name in (SHRINK, EXPAND, MERGER, ATTEND):
        sums[name].end()
        if name == SHRINK:
            whole = flat(r.done_shrink[...]).T
        else:
            whole = flat(getattr(r, "done_" + name)[...])
        grads[name] = whole
        getattr(r, "out_" + name)[...] = whole
        row, _ = places[name]
        squares = jnp.sum(whole * whole, axis=0, keepdims=True)
        split_into(r.column_near.at[near], row, squares, width)
    column_sum.begin()
    column_sum.turn()
    r.column_out[...] = column_sum.end()
    r.early_out[...] = r.early[...]
    norm, clip, squares = clip_of(r.column_out, places, r.vector_out[...])
    for name in MATRICES:
        rows_all = float(getattr(r, name + "_rows").shape[1] * outer * GROUP)
        _, _, _, step = factored_step(
            name, grads[name], getattr(r, name + "_rows")[...], r.column_out, r.early, places,
            clip, squares, rows_all,
        )
        at = MATRICES.index(name)
        r.step_near[near, at : at + 1, :] = fold_lanes(
            jnp.sum(step * step, axis=0, keepdims=True)
        )
    r.step_near[near, 4:8, :] = jnp.zeros((4, 128), F32)
    step_sum.begin()
    step_sum.turn()
    r.step_out[...] = step_sum.end()


    for name in MATRICES:
        gather, total = gathers[name], sums[name]
        for step in far_steps:
            gather.far_copy(step, far).wait_send()
            total.far_copy(step).wait_send()
        for step in near_steps:
            for hop in range(outer):
                gather.near_piece(step, hop, near, core).wait_send()
            total.near_copy(step).wait_send()
        for step in range(GROUP):
            gather.cross(step, core, at_near(step) if step else near).wait_send()
        total.pair_copy().wait_send()
        total.done_copy(core).wait_send()
    for small in (early, vector_sum, column_sum, step_sum):
        for step in near_steps:
            slot = small.near.at[near]
            remote(
                slot, slot, near_device(step), small.sends, small.receives, step - 1
            ).wait_send()
        for step in far_steps:
            slot = small.far.at[far]
            remote(
                slot, slot, far_device(step), small.sends, small.receives, GROUP + step - 1
            ).wait_send()
    vector_copy.wait_send()
    store_result.wait()
    store_input.wait()


def update_kernel(layout_sizes, names, *refs):
    outer, width, wide = layout_sizes
    r = Refs(names, refs)
    chip = lax.axis_index(FSDP)
    columns_of = {name: getattr(r, name + "_columns").shape[1] * outer * GROUP for name in MATRICES}
    places, _ = spread_rows(width, columns_of)
    copies = [
        pltpu.make_async_copy(r.result_in, r.block_output, r.sems.at[0]),
        pltpu.make_async_copy(r.input_in, r.input_gradient, r.sems.at[1]),
    ]
    for copy in copies:
        copy.start()
    vector_gradient = r.vector_sum[...]
    norm, clip, squares = clip_of(r.column_sum, places, vector_gradient)
    r.global_norm[...] = norm
    for name in MATRICES:
        weight = getattr(r, name + "_weight")[...]
        rows_all = float(weight.shape[0] * outer * GROUP)
        count = rows_all * weight.shape[1]
        clipped, new_rows, new_columns, step = factored_step(
            name, getattr(r, name + "_sum")[...], getattr(r, name + "_rows")[...], r.column_sum,
            r.early, places, clip, squares, rows_all,
        )
        at = MATRICES.index(name)
        step_square = jnp.sum(r.step_sum[at : at + 1, :], axis=1, keepdims=True)
        weight_square = jnp.sum(
            r.early[SQUARES : SQUARES + 1, at * 128 : at * 128 + 128], axis=1, keepdims=True
        )
        shrunk = jnp.maximum(1.0, jnp.sqrt(step_square * (1.0 / count)) * (1.0 / UPDATE_LIMIT))
        stride = LEARN_RATE * jnp.maximum(0.001, jnp.sqrt(weight_square * (1.0 / count)))
        updated = weight - (stride / shrunk) * step
        getattr(r, name + "_gradient")[...] = clipped
        getattr(r, name + "_updated")[...] = updated
        getattr(r, name + "_bfloat")[...] = updated.astype(BF16)
        getattr(r, name + "_newrows")[...] = row_of(new_rows)
        size = getattr(r, name + "_newcols").shape[1]
        wide_row = jnp.broadcast_to(new_columns, (8, new_columns.shape[1]))
        own = pltpu.roll(wide_row, lax.rem(new_columns.shape[1] - chip * size, columns_of[name]), 1)
        getattr(r, name + "_newcols")[...] = own[0:1, 0:size]
    vectors = r.early[VECTORS : VECTORS + 8, :]
    clipped, variance, step = vector_steps(
        vector_gradient, r.early[MOMENTS : MOMENTS + 8, :], clip
    )
    shrunk = jnp.maximum(1.0, jnp.sqrt(lane_mean(step * step)) * (1.0 / UPDATE_LIMIT))
    stride = LEARN_RATE * jnp.maximum(0.001, jnp.sqrt(lane_mean(vectors * vectors)))
    updated = vectors - stride * (step / shrunk)
    thin = r.vector_updated.shape[1]
    turn = lax.rem(width - chip * thin, width)
    for ref, value in (
        (r.vector_gradient, clipped),
        (r.vector_variance, variance),
        (r.vector_updated, updated),
    ):
        ref[...] = pltpu.roll(value, turn, 1)[0:6, 0:thin]
    for copy in copies:
        copy.wait()


def in_vmem():
    return pl.BlockSpec(memory_space=pltpu.VMEM)


def anywhere():
    return pl.BlockSpec(memory_space=pl.ANY)


def call(kernel, sizes, inputs, outputs, scratch, held, params, name):
    names = list(inputs) + list(outputs) + list(scratch)
    results = pl.pallas_call(
        functools.partial(kernel, sizes, names),
        in_specs=[anywhere() if key in held else in_vmem() for key in inputs],
        out_specs=[anywhere() if key in held else in_vmem() for key in outputs],
        out_shape=list(outputs.values()),
        scratch_shapes=list(scratch.values()),
        compiler_params=params,
        name=name,
    )(*inputs.values())
    return dict(zip(outputs, results, strict=True))


def staged_shards(devices, tokens, lengths, weights, vectors, rows, columns, moments, cotangent):
    outer = devices // GROUP
    slots, width = tokens.shape[1:]
    wide = weights[EXPAND].shape[1]
    sizes = (outer, width, wide)
    shape = jax.ShapeDtypeStruct
    row_in = {name + "_rows": rows[name].reshape(1, -1) for name in MATRICES}
    column_in = {name + "_columns": columns[name].reshape(1, -1) for name in MATRICES}
    weight_in = {name + "_weight": weights[name] for name in MATRICES}
    inputs = dict(
        tokens_in=tokens[0], lengths=lengths, cotangent_in=cotangent[0],
        vectors_own=vectors, moments_own=moments, **weight_in, **row_in, **column_in,
    )
    outputs = dict(
        result_out=shape((slots, width), BF16),
        input_out=shape((slots, width), F32),
        vector_out=shape((8, width), F32),
        early_out=shape((EARLY_ROWS, width), F32),
        column_out=shape((COLUMN_ROWS, width), F32),
        step_out=shape((8, 128), F32),
        **{"out_" + name: shape(weights[name].shape, F32) for name in MATRICES},
    )
    scratch = row_scratch(slots, width, wide)
    scratch.update(
        tokens=pltpu.VMEM((slots, width), BF16),
        cotangent=pltpu.VMEM((slots, width), BF16),
        straight=pltpu.VMEM((slots, width), F32),
        vectors=pltpu.VMEM((8, width), F32),
        early=pltpu.VMEM((EARLY_ROWS, width), F32),
        early_own=pltpu.VMEM((EARLY_ROWS, width), F32),
        early_wide=pltpu.VMEM((EARLY_ROWS, width), F32),
        spread=pltpu.VMEM((8, wide), F32),
        vector_pair=pltpu.VMEM((2, 8, width), F32),
        local_sems=pltpu.SemaphoreType.DMA((2,)),
    )
    for name, size in (
        ("early", (EARLY_ROWS, width)),
        ("vector", (8, width)),
        ("column", (COLUMN_ROWS, width)),
        ("step", (8, 128)),
    ):
        scratch[name + "_near"] = pltpu.VMEM((GROUP,) + size, F32)
        scratch[name + "_far"] = pltpu.VMEM((outer,) + size, F32)
        scratch[name + "_sends"] = pltpu.SemaphoreType.DMA((GROUP + outer + 1,))
        scratch[name + "_receives"] = pltpu.SemaphoreType.DMA((GROUP + outer + 1,))
    for name in MATRICES:
        held, wide_now = weights[name].shape
        scratch[name] = pltpu.VMEM((outer, GROUP, 2, held // 2, wide_now), BF16)
        half = (held // 2, wide_now)
        if name == SHRINK:
            half = (wide_now // 2, held)
        scratch["g_" + name] = pltpu.VMEM((outer, GROUP, 2) + half, BF16)
        scratch["pair_" + name] = pltpu.VMEM((outer, GROUP) + half, BF16)
        scratch["near_" + name] = pltpu.VMEM((GROUP - 1, outer) + half, BF16)
        scratch["far_" + name] = pltpu.VMEM((max(1, outer - 1),) + half, BF16)
        scratch["done_" + name] = pltpu.VMEM((2,) + half, F32)
        for kind, count in (("", GROUP * outer + GROUP), ("sum_", GROUP + outer + 1)):
            for way in ("_sends", "_receives"):
                scratch[kind + name + way] = pltpu.SemaphoreType.DMA((count,))
    got = call(
        shard_kernel, sizes, inputs, outputs, scratch,
        ("tokens_in", "cotangent_in", "result_out", "input_out"),
        pltpu.CompilerParams(
            collective_id=1, has_side_effects=True, vmem_limit_bytes=VMEM_LIMIT
        ),
        "row_and_sums",
    )
    inputs = dict(
        result_in=got["result_out"], input_in=got["input_out"], vector_sum=got["vector_out"],
        early=got["early_out"], column_sum=got["column_out"], step_sum=got["step_out"],
        **{name + "_sum": got["out_" + name] for name in MATRICES},
        **weight_in, **row_in, **column_in,
    )
    outputs = dict(
        block_output=shape((slots, width), BF16),
        input_gradient=shape((slots, width), F32),
        global_norm=shape((1, 1), F32),
    )
    for name in MATRICES:
        outputs[name + "_gradient"] = shape(weights[name].shape, F32)
        outputs[name + "_newrows"] = shape(row_in[name + "_rows"].shape, F32)
        outputs[name + "_newcols"] = shape(column_in[name + "_columns"].shape, F32)
        outputs[name + "_updated"] = shape(weights[name].shape, F32)
        outputs[name + "_bfloat"] = shape(weights[name].shape, BF16)
    for name in ("vector_gradient", "vector_variance", "vector_updated"):
        outputs[name] = shape(vectors.shape, F32)
    out = call(
        update_kernel, sizes, inputs, outputs, dict(sems=pltpu.SemaphoreType.DMA((2,))),
        ("result_in", "input_in", "block_output", "input_gradient"),
        pltpu.CompilerParams(vmem_limit_bytes=VMEM_LIMIT // 2),
        "update",
    )
    out["block_output"] = out["block_output"][None]
    out["input_gradient"] = out["input_gradient"][None]
    out["global_norm"] = out["global_norm"].reshape(())
    for name in MATRICES:
        for kind in ("_newrows", "_newcols"):
            out[name + kind] = out[name + kind].reshape(-1)
    return tuple(out.values())


def row_kernel(names, *refs):
    r = Refs(names, refs)
    prepare(r)
    project(r)
    attend_forward(r, ())
    feed_forward(r)
    r.g_vectors[...] = vector_total(r)
    shrink_gradient(r)
    expand_gradient(r)
    merger_gradient(r)
    attend_backward(r, ())
    attend_gradient(r)
    input_gradient(r)


def plain_shards(devices, tokens, lengths, weights, vectors, rows, columns, moments, cotangent):
    slots, width = tokens.shape[1:]
    wide = weights[EXPAND].shape[1]
    shape = jax.ShapeDtypeStruct
    whole = {
        name: lax.all_gather(weights[name].astype(BF16), FSDP, axis=0, tiled=True)
        for name in MATRICES
    }
    vector_rows = lax.all_gather(vectors.astype(BF16), FSDP, axis=1, tiled=True).astype(F32)
    vector_rows = jnp.concatenate([vector_rows, jnp.zeros((2, width), F32)], axis=0)
    inputs = dict(
        tokens=tokens[0], lengths=lengths, cotangent=cotangent[0], vectors=vector_rows, **whole
    )
    outputs = dict(
        result=shape((slots, width), BF16),
        straight=shape((slots, width), F32),
        g_vectors=shape((8, width), F32),
        g_attend=shape((width, 3 * width), BF16),
        g_merger=shape((width, width), BF16),
        g_expand=shape((width, wide), BF16),
        g_shrink=shape((width, wide), BF16),
    )
    scratch = row_scratch(slots, width, wide)
    scratch["d_branch"] = pltpu.VMEM((slots, width), BF16)
    names = list(inputs) + list(outputs) + list(scratch)
    got = pl.pallas_call(
        functools.partial(row_kernel, names),
        in_specs=[in_vmem()] * len(inputs),
        out_specs=[in_vmem()] * len(outputs),
        out_shape=list(outputs.values()),
        scratch_shapes=list(scratch.values()),
        compiler_params=pltpu.CompilerParams(vmem_limit_bytes=VMEM_LIMIT),
        name="row",
    )(*inputs.values())
    got = dict(zip(outputs, got, strict=True))
    grads = []
    for name in MATRICES:
        value = lax.psum(got["g_" + name], DP).astype(F32)
        if name == SHRINK:
            grads.append(lax.psum_scatter(value.T, FSDP, scatter_dimension=0, tiled=True))
        else:
            grads.append(lax.psum_scatter(value, FSDP, scatter_dimension=0, tiled=True))
    vector_all = lax.psum(got["g_vectors"][:6], (DP, FSDP))
    index = lax.axis_index(FSDP)

    def spread(own, dim):
        size = own.shape[dim]
        extent = own.shape[:dim] + (size * devices,) + own.shape[dim + 1 :]
        return lax.dynamic_update_slice_in_dim(
            jnp.zeros(extent, F32), own, index * size, dim
        )

    early = (
        [spread(columns[name], 0) for name in MATRICES],
        [jnp.sum(weights[name] * weights[name]) for name in MATRICES],
        [jnp.sum(rows[name]) for name in MATRICES],
        [jnp.sum(grad * grad, axis=0) for grad in grads],
        jnp.sum(vectors * vectors, axis=1),
    )
    old_columns, weight_squares, row_sums, columns_now, vector_squares = lax.psum(early, FSDP)
    squares = [jnp.sum(value) for value in columns_now]
    total = jnp.sum(vector_all * vector_all)
    for value in squares:
        total = total + value
    norm = jnp.sqrt(total)
    clip = jnp.minimum(1.0, THRESHOLD / norm)
    power = clip * clip
    pieces = []
    for at, name in enumerate(MATRICES):
        grad = grads[at]
        rows_all = float(grad.shape[0] * devices)
        count = rows_all * grad.shape[1]
        new_rows = FORGET * rows[name] + (1.0 - FORGET) * (
            power * jnp.mean(grad * grad, axis=1) + TINY_VALUE
        )
        new_columns = FORGET * old_columns[at] + (1.0 - FORGET) * (
            power * columns_now[at] / rows_all + TINY_VALUE
        )
        mean = FORGET * row_sums[at] / rows_all + (1.0 - FORGET) * (
            power * squares[at] / count + TINY_VALUE
        )
        clipped = clip * grad
        step = clipped * lax.rsqrt(new_rows[:, None] * new_columns[None, :] / mean)
        pieces.append((clipped, new_rows, new_columns, step, count))
    thin = vectors.shape[1]
    vector_clipped = clip * lax.dynamic_slice_in_dim(vector_all, index * thin, thin, 1)
    variance = FORGET * moments + (1.0 - FORGET) * (vector_clipped * vector_clipped + TINY_VALUE)
    vector_step = vector_clipped * lax.rsqrt(variance)
    step_squares, vector_step_squares = lax.psum(
        (
            [jnp.sum(piece[3] * piece[3]) for piece in pieces],
            jnp.sum(vector_step * vector_step, axis=1),
        ),
        FSDP,
    )
    results = [got["result"][None], got["straight"][None], norm]
    for at, name in enumerate(MATRICES):
        clipped, new_rows, new_columns, step, count = pieces[at]
        shrunk = jnp.maximum(1.0, jnp.sqrt(step_squares[at] / count) / UPDATE_LIMIT)
        stride = LEARN_RATE * jnp.maximum(0.001, jnp.sqrt(weight_squares[at] / count))
        updated = weights[name] - stride * (step / shrunk)
        size = columns[name].shape[0]
        own = lax.dynamic_slice_in_dim(new_columns, index * size, size, 0)
        results.extend([clipped, new_rows, own, updated, updated.astype(BF16)])
    extent = float(width)
    shrunk = jnp.maximum(1.0, jnp.sqrt(vector_step_squares / extent) / UPDATE_LIMIT)[:, None]
    stride = LEARN_RATE * jnp.maximum(0.001, jnp.sqrt(vector_squares / extent))[:, None]
    results.extend([vector_clipped, variance, vectors - stride * (vector_step / shrunk)])
    return tuple(results)


def shards(
    devices,
    tokens,
    lengths,
    attend_weight,
    merger_weight,
    expand_weight,
    shrink_weight,
    vectors,
    attend_rows,
    attend_columns,
    merger_rows,
    merger_columns,
    expand_rows,
    expand_columns,
    shrink_rows,
    shrink_columns,
    vector_moments,
    cotangent,
):
    weights = dict(
        attend=attend_weight, merger=merger_weight, expand=expand_weight, shrink=shrink_weight
    )
    rows = dict(attend=attend_rows, merger=merger_rows, expand=expand_rows, shrink=shrink_rows)
    columns = dict(
        attend=attend_columns, merger=merger_columns, expand=expand_columns, shrink=shrink_columns
    )
    assert tokens.shape[0] == 1
    fits = devices % GROUP == 0 and all(
        weight.shape[0] % 32 == 0 for weight in weights.values()
    ) and shrink_weight.shape[0] % 128 == 0
    body = staged_shards if fits else plain_shards
    return body(
        devices, tokens, lengths, weights, vectors, rows, columns, vector_moments, cotangent
    )


def solution(mesh):
    split = P(FSDP, None)
    row = P((DP, FSDP), None, None)
    one = P(FSDP)
    thin = P(None, FSDP)
    in_specs = (
        (row, P((DP, FSDP), None)) + (split,) * 4 + (thin,) + (one,) * 8 + (thin, row)
    )
    out_specs = (row, row, P()) + (split, one, one, split, split) * 4 + (thin,) * 3
    return jax.shard_map(
        functools.partial(shards, mesh.shape[FSDP]),
        mesh=mesh, in_specs=in_specs, out_specs=out_specs, check_vma=False,
    )
```

```python
import functools

import jax
import jax.numpy as jnp
from jax import lax
from jax.experimental import pallas as pl
from jax.experimental.pallas import tpu as pltpu
from jax.sharding import PartitionSpec as P

F32 = jnp.float32
BF16 = jnp.bfloat16
HEAD_DIM = 64
STEP = 3
EPSILON = 1e-05
TINY_VALUE = 1e-30
NEGATIVE = -1e30
THRESHOLD = 1.0
UPDATE_LIMIT = 1.0
LEARN_RATE = 0.5
FORGET = 1.0 - float(STEP) ** (-0.8)
LOG2_E = 1.4426950408889634
GELU_A = 0.7978845608028654
GELU_B = 0.044715 * GELU_A

REACH = 256
QUERY_BLOCK = 256
TILE = 256
GROUP = 4
DP, FSDP = "dp", "fsdp"
ATTEND, MERGER, EXPAND, SHRINK = "attend", "merger", "expand", "shrink"
MATRICES = (ATTEND, MERGER, EXPAND, SHRINK)
MESH = pl.DeviceIdType.MESH
VMEM_LIMIT = 63 << 20


def dot_general(left, right, left_dim, right_dim):
    return lax.dot_general(
        left, right, (((left_dim,), (right_dim,)), ((), ())), preferred_element_type=F32
    )


def dot_nn(left, right):
    return dot_general(left, right, 1, 0)


def dot_nt(left, right):
    return dot_general(left, right, 1, 1)


def dot_tn(left, right):
    return dot_general(left, right, 0, 0)


def flat(value):
    return value.reshape(-1, value.shape[-1])


def fold_rows(value):
    return jnp.sum(value.reshape(value.shape[0] // 8, 8, value.shape[1]), axis=0)


def fold_lanes(row):
    total = row[:, :128]
    for start in range(128, row.shape[1], 128):
        total = total + row[:, start : start + 128]
    return total


def diagonal(size):
    return lax.broadcasted_iota(jnp.int32, (size, size), 0) == lax.broadcasted_iota(
        jnp.int32, (size, size), 1
    )


def column_of(row):
    size = row.shape[1]
    return jnp.sum(jnp.where(diagonal(size), row, 0.0), axis=1, keepdims=True)


def row_of(column):
    size = column.shape[0]
    return jnp.sum(jnp.where(diagonal(size), column, 0.0), axis=0, keepdims=True)


def lane_mean(value):
    return jnp.mean(value, axis=-1, keepdims=True)


def aligned(start, size):
    return pl.ds(pl.multiple_of(start, size), size)


def band(slots):
    pieces = []
    place = 0
    for first in range(0, slots, QUERY_BLOCK):
        low = max(0, first - REACH)
        high = first + QUERY_BLOCK
        pieces.append((first, low, high, place))
        place += high - low
    return pieces, place


def prepare(r):
    slots = r.tokens.shape[0]
    count = r.lengths.shape[1]
    for start in range(0, slots, TILE):
        r.tokens_t[:, start : start + TILE] = r.tokens[start : start + TILE, :].T
    lengths = r.lengths[...].astype(F32)
    rows = jnp.broadcast_to(lengths, (8, count)).astype(BF16)
    upto = lax.broadcasted_iota(jnp.int32, (count, count), 1) <= lax.broadcasted_iota(
        jnp.int32, (count, count), 0
    )
    ends = dot_nt(jnp.where(upto, 1.0, 0.0).astype(BF16), rows)[:, 0:1]
    places = lax.broadcasted_iota(jnp.int32, (count, slots), 1).astype(F32)
    ended = jnp.where(ends <= places, 1.0, 0.0).astype(BF16)
    begin = dot_nn(rows, ended)[0:1, :]
    total = jnp.sum(lengths, axis=1, keepdims=True)
    r.total[...] = jnp.broadcast_to(total, r.total.shape)
    slot = lax.broadcasted_iota(jnp.int32, (1, slots), 1).astype(F32)
    begin = jnp.where(slot < total, begin, slot)
    for first, low, high, place in band(slots)[0]:
        key = (lax.broadcasted_iota(jnp.int32, (high - low, QUERY_BLOCK), 0) + low).astype(F32)
        query = slot[:, first : first + QUERY_BLOCK]
        fits = (key >= begin[:, first : first + QUERY_BLOCK]) & (key <= query)
        r.mask[place : place + high - low, :] = jnp.where(fits, 1.0, 0.0).astype(BF16)


def project(r):
    width = r.tokens.shape[1]

    def tile(step, carry):
        columns = aligned(step * TILE, TILE)
        r.projected_t[columns, :] = dot_tn(flat(r.attend[..., columns]), r.tokens_t[...]).astype(
            BF16
        )
        return carry

    lax.fori_loop(0, 3 * width // TILE, tile, 0)

    def turn(step, carry):
        columns = aligned(step * TILE, TILE)
        r.key_value[:, columns] = r.projected_t[aligned(width + step * TILE, TILE), :].T
        return carry

    lax.fori_loop(0, 2 * width // TILE, turn, 0)


def beside_zeros(value, head):
    zeros = jnp.zeros_like(value)
    return jnp.concatenate([value, zeros] if head == 0 else [zeros, value], axis=0)


def attend_forward(r, hooks):
    slots, width = r.tokens.shape
    factor = HEAD_DIM ** -0.5 * LOG2_E

    def pair(step, carry):
        start = pl.multiple_of(step * 128, 128)
        for head in (0, 1):
            for at, hook in hooks:
                if at % 2 == head:
                    pl.when(step == at // 2)(hook)
            for first, low, high, place in band(slots)[0]:
                keys = r.key_value[low:high, pl.ds(start, 128)]
                fits = r.mask[place : place + high - low, :].astype(F32) > 0.5
                mine = pl.ds(start + 64 * head, 64)
                queries = r.projected_t[mine, first : first + QUERY_BLOCK]
                scores = dot_nn(keys, beside_zeros(queries, head))
                scores = jnp.where(fits, scores * factor, NEGATIVE)
                highest = jnp.max(scores, axis=0, keepdims=True)
                weights = jnp.exp2(scores - highest)
                inverse = 1.0 / jnp.sum(weights, axis=0, keepdims=True)
                probs = (weights * inverse).astype(BF16)
                r.probs[2 * step + head, place : place + high - low, :] = probs
                values = r.projected_t[pl.ds(2 * width + start + 64 * head, 64), low:high]
                r.context_t[mine, first : first + QUERY_BLOCK] = dot_nn(values, probs).astype(BF16)
        return carry

    lax.fori_loop(0, width // 128, pair, 0)


def attend_backward(r, hooks):
    slots, width = r.tokens.shape
    scale = HEAD_DIM ** -0.5

    def pair(step, carry):
        start = pl.multiple_of(step * 128, 128)
        for head in (0, 1):
            for at, hook in hooks:
                if at % 2 == head:
                    pl.when(step == at // 2)(hook)
            mine = pl.ds(start + 64 * head, 64)
            mine_keys = pl.ds(width + start + 64 * head, 64)
            mine_values = pl.ds(2 * width + start + 64 * head, 64)
            queries = r.projected_t[mine, :]
            keys_t = r.projected_t[mine_keys, :]
            upstream = r.d_context_t[mine, :]
            open_keys = None
            open_values = None
            for first, low, high, place in band(slots)[0]:
                values = r.key_value[low:high, pl.ds(width + start, 128)]
                arriving = upstream[:, first : first + QUERY_BLOCK]
                d_probs = dot_nn(values, beside_zeros(arriving, head))
                probs = r.probs[2 * step + head, place : place + high - low, :]
                wide = probs.astype(F32)
                inner = jnp.sum(wide * d_probs, axis=0, keepdims=True)
                d_scores = (wide * (d_probs - inner)).astype(BF16)
                r.projected_t[mine, first : first + QUERY_BLOCK] = (
                    dot_nn(keys_t[:, low:high], d_scores) * scale
                ).astype(BF16)
                d_keys = dot_nt(queries[:, first : first + QUERY_BLOCK], d_scores)
                d_values = dot_nt(arriving, probs)
                done = first - low
                if done:
                    r.projected_t[mine_keys, low:first] = (
                        (open_keys + d_keys[:, :done]) * scale
                    ).astype(BF16)
                    r.projected_t[mine_values, low:first] = (
                        open_values + d_values[:, :done]
                    ).astype(BF16)
                open_keys = d_keys[:, done:]
                open_values = d_values[:, done:]
            r.projected_t[mine_keys, slots - QUERY_BLOCK :] = (open_keys * scale).astype(BF16)
            r.projected_t[mine_values, slots - QUERY_BLOCK :] = open_values.astype(BF16)
        return carry

    lax.fori_loop(0, width // 128, pair, 0)


def vector_rows(r):
    return [r.vectors[place : place + 1, :] for place in range(6)]


def by_tokens(r, body):
    def block(step, carry):
        body(step, aligned(step * TILE, TILE))
        return carry

    lax.fori_loop(0, r.tokens.shape[0] // TILE, block, 0)


def first_half(r):
    omega_one, gain_one, shift_one = vector_rows(r)[:3]

    def body(step, rows):
        inputs = r.tokens[rows, :].astype(F32)
        first_sum = omega_one * inputs + dot_tn(r.context_t[:, rows], flat(r.merger[...]))
        centered = first_sum - lane_mean(first_sum)
        first_inv = lax.rsqrt(lane_mean(centered * centered) + EPSILON)
        first_normed = centered * first_inv
        r.first_inv[rows, :] = jnp.broadcast_to(first_inv, (TILE, 128))
        r.straight[rows, :] = first_normed
        first_low = (first_normed * gain_one + shift_one).astype(BF16)
        r.first_t[:, rows] = first_low.T
        hidden = dot_nn(first_low, flat(r.expand[...]))
        square = hidden * hidden
        bend = jnp.tanh(hidden * (GELU_A + GELU_B * square))
        half = 0.5 * hidden
        lifted = 1.0 + bend
        r.active[rows, :] = (half * lifted).astype(BF16)
        slope = 0.5 * lifted + half * (1.0 - bend * bend) * (GELU_A + 3 * GELU_B * square)
        r.d_hidden[rows, :] = slope.astype(BF16)

    by_tokens(r, body)


def second_half(r):
    _, gain_one, shift_one, omega_two, gain_two, shift_two = vector_rows(r)
    r.vector_sums[...] = jnp.zeros_like(r.vector_sums)

    def body(step, rows):
        first_out = r.straight[rows, :] * gain_one + shift_one
        second_sum = omega_two * first_out + dot_nn(r.active[rows, :], flat(r.shrink[...]))
        centered = second_sum - lane_mean(second_sum)
        second_inv = lax.rsqrt(lane_mean(centered * centered) + EPSILON)
        second_normed = centered * second_inv
        arriving = r.cotangent[rows, :].astype(F32)
        r.result[rows, :] = (second_normed * gain_two + shift_two).astype(BF16)
        place = (lax.broadcasted_iota(jnp.int32, (TILE, 1), 0) + step * TILE).astype(F32)
        upstream = arriving * jnp.where(place < r.total[0:1, 0:1], 1.0, 0.0)
        scaled = upstream * gain_two
        d_second = second_inv * (
            scaled - lane_mean(scaled) - second_normed * lane_mean(scaled * second_normed)
        )
        r.vector_sums[4] += fold_rows(upstream * second_normed)
        r.vector_sums[5] += fold_rows(upstream)
        r.vector_sums[3] += fold_rows(first_out * d_second)
        r.d_second[rows, :] = d_second
        r.d_second_t[:, rows] = d_second.astype(BF16).T

    by_tokens(r, body)


def way_back(r):
    omega_one, gain_one, _, omega_two = vector_rows(r)[:4]

    def body(step, rows):
        d_second = r.d_second[rows, :]
        d_active = dot_nt(d_second.astype(BF16), flat(r.shrink[...]))
        d_hidden = (d_active * r.d_hidden[rows, :].astype(F32)).astype(BF16)
        r.d_hidden[rows, :] = d_hidden
        d_first = dot_nt(d_hidden, flat(r.expand[...])) + omega_two * d_second
        first_normed = r.straight[rows, :]
        r.vector_sums[1] += fold_rows(d_first * first_normed)
        r.vector_sums[2] += fold_rows(d_first)
        scaled = d_first * gain_one
        d_first_sum = r.first_inv[rows, 0:1] * (
            scaled - lane_mean(scaled) - first_normed * lane_mean(scaled * first_normed)
        )
        r.vector_sums[0] += fold_rows(r.tokens[rows, :].astype(F32) * d_first_sum)
        r.straight[rows, :] = omega_one * d_first_sum
        branch_low = d_first_sum.astype(BF16)
        r.d_branch[rows, :] = branch_low
        r.d_context_t[:, rows] = dot_nt(flat(r.merger[...]), branch_low).astype(BF16)

    by_tokens(r, body)


def vector_total(r):
    rows = [jnp.sum(r.vector_sums[place], axis=0, keepdims=True) for place in range(6)]
    return jnp.concatenate(rows + [jnp.zeros((2, rows[0].shape[1]), F32)], axis=0)


def by_columns(columns, store):
    def tile(step, carry):
        store(step)
        return carry

    lax.fori_loop(0, columns // TILE, tile, 0)


def put_tile(ref, columns, value):
    ref[..., columns] = value.astype(ref.dtype).reshape(ref.shape[:-1] + (value.shape[1],))


def shrink_gradient(r):
    width, wide = r.tokens.shape[1], r.active.shape[1]
    if len(r.g_shrink.shape) == 2:

        def store(step):
            columns = aligned(step * TILE, TILE)
            r.g_shrink[:, columns] = dot_nn(r.d_second_t[...], r.active[:, columns]).astype(
                r.g_shrink.dtype
            )

        by_columns(wide, store)
        return
    owned = r.g_shrink.shape[-1]
    per_tile = max(1, TILE // owned)
    span = owned * per_tile

    def tile(step, carry):
        value = dot_nn(r.d_second_t[...], r.active[:, aligned(step * span, span)]).astype(BF16)
        for piece in range(per_tile):
            owner = step * per_tile + piece
            r.g_shrink[owner // GROUP, lax.rem(owner, GROUP)] = value[
                :, piece * owned : (piece + 1) * owned
            ].reshape(2, width // 2, owned)
        return carry

    lax.fori_loop(0, wide // span, tile, 0)


def expand_gradient(r):
    def store(step):
        columns = aligned(step * TILE, TILE)
        put_tile(r.g_expand, columns, dot_nn(r.first_t[...], r.d_hidden[:, columns]))

    by_columns(r.active.shape[1], store)


def merger_gradient(r):
    def store(step):
        columns = aligned(step * TILE, TILE)
        put_tile(r.g_merger, columns, dot_nn(r.context_t[...], r.d_branch[:, columns]))

    by_columns(r.tokens.shape[1], store)


def attend_gradient(r, part):
    width = r.tokens.shape[1]
    half = width // 2
    into = r.g_attend[part]

    def store(step):
        columns = aligned(step * half, half)
        heads = r.projected_t[aligned(step * width + part * half, half), :]
        put_tile(into, columns, dot_nt(r.tokens_t[...], heads))

    def tile(step, carry):
        store(step)
        return carry

    lax.fori_loop(0, 3, tile, 0)


def heads_together(parts):
    half = parts[0].shape[1] // 3
    return jnp.concatenate(
        [part[:, at * half : (at + 1) * half] for at in range(3) for part in parts], axis=1
    )


def input_gradient(r):
    def tile(step, carry):
        rows = aligned(step * TILE, TILE)
        r.straight[rows, :] += dot_nn(flat(r.attend[...]), r.projected_t[:, rows]).T
        return carry

    lax.fori_loop(0, r.tokens.shape[0] // TILE, tile, 0)


def row_scratch(slots, width, wide):
    packed = band(slots)[1]
    heads = width // HEAD_DIM
    return dict(
        tokens_t=pltpu.VMEM((width, slots), BF16),
        mask=pltpu.VMEM((packed, QUERY_BLOCK), BF16),
        total=pltpu.VMEM((8, 128), F32),
        projected_t=pltpu.VMEM((3 * width, slots), BF16),
        key_value=pltpu.VMEM((slots, 2 * width), BF16),
        probs=pltpu.VMEM((heads, packed, QUERY_BLOCK), BF16),
        context_t=pltpu.VMEM((width, slots), BF16),
        d_context_t=pltpu.VMEM((width, slots), BF16),
        active=pltpu.VMEM((slots, wide), BF16),
        d_hidden=pltpu.VMEM((slots, wide), BF16),
        first_t=pltpu.VMEM((width, slots), BF16),
        d_second_t=pltpu.VMEM((width, slots), BF16),
        vector_sums=pltpu.VMEM((6, 8, width), F32),
        first_inv=pltpu.VMEM((slots, 128), F32),
        d_second=pltpu.VMEM((slots, width), F32),
    )


class Refs:
    def __init__(self, names, refs):
        for name, ref in zip(names, refs, strict=True):
            setattr(self, name, ref)


LOW, HIGH = "low", "high"
REDUCED = (SHRINK, EXPAND, MERGER, LOW, HIGH)
FOLDED = (SHRINK, EXPAND)


def packed_rows(first, order, columns_of, width):
    places = {}
    for name in order:
        places[name] = (first, columns_of[name] // width)
        first += columns_of[name] // width
    return places


SQUARES, ROW_SUMS, EARLY_ROWS = 6, 7, 8
LATE_COLUMNS, LATE_ROWS = 6, 16
COLUMN_ROWS = 8
ALL = slice(None)


def late_places(columns_of, width):
    return packed_rows(LATE_COLUMNS, (MERGER, SHRINK, ATTEND, EXPAND), columns_of, width)


def column_places(columns_of, width):
    places = packed_rows(0, (MERGER, EXPAND, SHRINK), columns_of, width)
    places.update(packed_rows(COLUMN_ROWS, (ATTEND,), columns_of, width))
    return places


def joined(ref, start, count):
    return jnp.concatenate([ref[place : place + 1, :] for place in range(start, start + count)], 1)


def split_into(ref, start, row, width):
    for piece in range(row.shape[1] // width):
        ref[start + piece : start + piece + 1, :] = row[:, piece * width : (piece + 1) * width]


def scalar_sum(value):
    return jnp.sum(jnp.sum(value, axis=1, keepdims=True), axis=0, keepdims=True)


def flat_slots(value):
    return value.reshape((-1,) + value.shape[2:])


class Statistics:
    def __init__(self, r, sizes, columns, vector_gradient):
        outer, self.width, _ = sizes
        self.devices = outer * GROUP
        columns_of = {
            name: getattr(r, name + "_columns").shape[1] * self.devices for name in MATRICES
        }
        self.early, self.late, self.columns = r.early, r.late, columns
        self.late_at = late_places(columns_of, self.width)
        self.column_at = column_places(columns_of, self.width)
        self.squares = {
            name: scalar_sum(joined(columns, *self.column_at[name])) for name in MATRICES
        }
        total = scalar_sum(vector_gradient * vector_gradient)
        for name in MATRICES:
            total = total + self.squares[name]
        self.norm = jnp.sqrt(total)
        self.clip = jnp.minimum(1.0, THRESHOLD / self.norm)

    def lanes(self, row, name):
        at = MATRICES.index(name) * 128
        return jnp.sum(self.early[row : row + 1, at : at + 128], axis=1, keepdims=True)

    def factored(self, name, gradient, rows_old, rows_all):
        wide = gradient.shape[1]
        power = self.clip * self.clip
        row_mean = jnp.sum(gradient * gradient, axis=1, keepdims=True) * (1.0 / wide)
        new_rows = FORGET * rows_old + (1.0 - FORGET) * (power * row_mean + TINY_VALUE)
        now = joined(self.columns, *self.column_at[name]) * (1.0 / rows_all)
        new_columns = FORGET * joined(self.late, *self.late_at[name]) + (1.0 - FORGET) * (
            power * now + TINY_VALUE
        )
        mean = FORGET * (self.lanes(ROW_SUMS, name) * (1.0 / rows_all)) + (1.0 - FORGET) * (
            power * (self.squares[name] * (1.0 / (rows_all * wide))) + TINY_VALUE
        )
        clipped = self.clip * gradient
        step = clipped * lax.rsqrt(new_rows * new_columns * (1.0 / mean))
        return clipped, new_rows, new_columns, step


def vector_steps(gradient, moments, clip):
    clipped = clip * gradient
    variance = FORGET * moments + (1.0 - FORGET) * (clipped * clipped + TINY_VALUE)
    return clipped, variance, clipped * lax.rsqrt(variance)


def shard_kernel(layout_sizes, names, *refs):
    outer, width, wide = layout_sizes
    r = Refs(names, refs)
    r.result = r.cotangent
    r.d_branch = r.tokens
    r.g_attend = (r.g_low, r.g_high)
    core = lax.axis_index(DP)
    chip = lax.axis_index(FSDP)
    far = chip // GROUP
    near = lax.rem(chip, GROUP)
    sibling = (1 - core, chip)
    near_steps = range(1, GROUP)
    far_steps = range(1, outer)

    near_places = [near] + [jnp.bitwise_xor(near, step) for step in near_steps]
    far_places = [lax.rem(far + step, outer) for step in range(outer)]
    far_origins = [lax.rem(far + outer - step, outer) for step in range(outer)]
    near_devices = [(core, far * GROUP + place) for place in near_places]
    far_devices = [(core, place * GROUP + near) for place in far_places]
    other = 1 - core
    fold_first = jnp.bitwise_xor(near, 1 + core)
    fold_second = jnp.bitwise_xor(near, 2 - core)
    diagonal_place = near_places[3]
    fold_devices = [
        (core, far * GROUP + place) for place in (fold_first, fold_first, fold_second)
    ]

    started = {}
    arrived = set()

    class Copy:
        def __init__(self, key, sems, index, device, source, target, landing=None):
            self.key = key + (index,)
            self.device = device
            self.sems = sems
            self.index = index
            self.source = source
            self.target = target
            self.landing = target if landing is None else landing

        def describe(self, source, target):
            return pltpu.make_async_remote_copy(
                src_ref=source[0].at[source[1]],
                dst_ref=target[0].at[target[1]],
                send_sem=self.sems[0].at[self.index],
                recv_sem=self.sems[1].at[self.index],
                device_id=self.device,
                device_id_type=MESH,
            )

        def start(self):
            self.describe(self.source, self.target).start()
            started[self.key] = self

        def arrive(self):
            self.describe(self.landing, self.landing).wait_recv()
            arrived.add(self.key)

        def leave(self):
            self.describe(self.source, self.target).wait_send()

    def local(source, target, index):
        return pltpu.make_async_copy(source, target, r.local_sems.at[index])

    load_tokens = local(r.tokens_in, r.tokens, 0)
    load_cotangent = local(r.cotangent_in, r.cotangent, 1)
    load_tokens.start()
    load_cotangent.start()

    barrier = pltpu.get_barrier_semaphore()
    for step in near_steps:
        pl.semaphore_signal(barrier, inc=1, device_id=near_devices[step], device_id_type=MESH)
    for step in far_steps:
        pl.semaphore_signal(barrier, inc=1, device_id=far_devices[step], device_id_type=MESH)
    pl.semaphore_signal(barrier, inc=1, device_id=sibling, device_id_type=MESH)
    pl.semaphore_wait(barrier, len(near_steps) + len(far_steps) + 1)


    class Sum:
        def __init__(self, name, cores):
            self.key = (name,)
            self.near = getattr(r, name + "_near")
            self.far = getattr(r, name + "_far")
            self.sems = (getattr(r, name + "_sends"), getattr(r, name + "_receives"))
            self.steps = [(0, step) for step in near_steps]
            if cores == 2:
                self.steps += [(1, step) for step in range(GROUP)]
            self.mine = core if cores == 2 else 0
            self.other = other if cores == 2 else 0

        def near_copy(self, cross, step):
            mine = (self.near, (self.mine, near))
            whose = self.other if cross else self.mine
            device = (other if cross else core, near_devices[step][1])
            return Copy(
                self.key, self.sems, cross * GROUP + step, device, mine, mine,
                (self.near, (whose, near_places[step])),
            )

        def far_copy(self, step):
            mine = (self.far, far)
            return Copy(
                self.key, self.sems, 2 * GROUP + step, far_devices[step], mine, mine,
                (self.far, far_origins[step]),
            )

        def begin(self, value):
            self.near[self.mine, near] = value
            for cross, step in self.steps:
                self.near_copy(cross, step).start()

        def turn(self):
            for cross, step in self.steps:
                self.near_copy(cross, step).arrive()
            self.far[far] = jnp.sum(flat_slots(self.near[...]), axis=0)
            for step in far_steps:
                self.far_copy(step).start()

        def end(self):
            for step in far_steps:
                self.far_copy(step).arrive()
            return jnp.sum(self.far[...], axis=0)


    class Gather:
        def __init__(self, name, fine):
            self.key = (name,)
            self.fine = fine
            self.hops = range(outer if fine else 1)
            self.held = getattr(r, name)
            self.sems = (getattr(r, name + "_sends"), getattr(r, name + "_receives"))

        def far_copy(self, step):
            mine = (self.held, (far, near, core))
            return Copy(
                self.key, self.sems, step, far_devices[step], mine, mine,
                (self.held, (far_origins[step], near, core)),
            )

        def near_copy(self, step, hop):
            slot = far_origins[hop] if self.fine else ALL
            mine = (self.held, (slot, near, core))
            return Copy(
                self.key, self.sems, step * outer + hop, near_devices[step], mine, mine,
                (self.held, (slot, near_places[step], core)),
            )

        def cross(self, step):
            whose = near_places[step]
            mine = (self.held, (ALL, whose, core))
            return Copy(
                self.key, self.sems, GROUP * outer + step, sibling, mine, mine,
                (self.held, (ALL, whose, other)),
            )

        def place(self, shard):
            rows = shard.shape[0] // 2
            mine = shard[pl.ds(pl.multiple_of(core * rows, rows), rows), :]
            self.held[far, near, core] = mine.astype(BF16)

        def begin(self):
            for step in far_steps:
                self.far_copy(step).start()

        def near_start(self, hop):
            for step in near_steps:
                self.near_copy(step, hop).start()

        def turn(self):
            for hop in far_steps:
                self.far_copy(hop).arrive()
                if self.fine:
                    self.near_start(hop)
            if not self.fine:
                self.near_start(0)
            self.cross(0).start()

        def pass_on(self):
            for step in near_steps:
                for hop in self.hops:
                    self.near_copy(step, hop).arrive()
                self.cross(step).start()

        def end(self):
            for step in range(GROUP):
                self.cross(step).arrive()


    class Reduce:
        def __init__(self, name, folds):
            self.key = ("sum", name)
            self.folds = folds
            for part in ("g", "pair", "near", "far", "done"):
                setattr(self, part, getattr(r, part + "_" + name))
            self.sems = (
                getattr(r, "sum_" + name + "_sends"), getattr(r, "sum_" + name + "_receives")
            )

        def pair_copy(self):
            return Copy(
                self.key, self.sems, 0, sibling, (self.g, (ALL, ALL, other)),
                (self.pair, ALL),
            )

        def near_copy(self, step):
            return Copy(
                self.key, self.sems, step, near_devices[step],
                (self.pair, (ALL, near_places[step])), (self.near, step - 1),
            )

        def fold_copy(self, place):
            block = (fold_first, diagonal_place, fold_second)[place]
            return Copy(
                self.key, self.sems, place + 1, fold_devices[place],
                (self.pair, (ALL, block)), (self.near, place),
            )

        def far_copy(self, step):
            return Copy(
                self.key, self.sems, GROUP + step - 1, far_devices[step],
                (self.pair, (far_places[step], near)), (self.far, step - 1),
            )

        def done_copy(self):
            mine = (self.done, core)
            return Copy(
                self.key, self.sems, GROUP + outer, sibling, mine, mine,
                (self.done, other),
            )

        def begin(self):
            self.pair_copy().start()

        def turn(self):
            self.pair_copy().arrive()

            def block(step, carry):
                both = self.g[step, :, core].astype(F32) + self.pair[step].astype(F32)
                self.pair[step] = both.astype(BF16)
                return carry

            lax.fori_loop(0, outer, block, 0)
            if self.folds:
                self.fold_copy(0).start()
                self.fold_copy(1).start()
                return
            for step in near_steps:
                self.near_copy(step).start()

        def add(self, place, landed):
            def block(step, carry):
                total = self.pair[step, place].astype(F32)
                for at in landed:
                    total = total + self.near[at, step].astype(F32)
                self.pair[step, place] = total.astype(BF16)
                return carry

            lax.fori_loop(0, outer, block, 0)

        def fold(self):
            self.fold_copy(1).arrive()
            self.add(fold_second, (1,))
            self.fold_copy(2).start()

        def pass_on(self):
            if self.folds:
                self.fold_copy(0).arrive()
                self.fold_copy(2).arrive()
                self.add(near, (0, 2))
            else:
                for step in near_steps:
                    self.near_copy(step).arrive()
                self.add(near, [step - 1 for step in near_steps])
            for step in far_steps:
                self.far_copy(step).start()

        def collect(self):
            for step in far_steps:
                self.far_copy(step).arrive()
            total = self.pair[far, near].astype(F32)
            for step in far_steps:
                total = total + self.far[step - 1].astype(F32)
            self.done[core] = total
            self.done_copy().start()

        def end(self):
            self.done_copy().arrive()

    early = Sum("early", 1)
    late = Sum("late", 1)
    vector_sum = Sum("vector", 2)
    column_sum = Sum("column", 1)
    last_sum = Sum("last", 2)
    step_sum = Sum("step", 2)
    gathers = {name: Gather(name, name == ATTEND) for name in MATRICES}
    sums = {name: Reduce(name, name in FOLDED) for name in REDUCED}
    shards = {name: getattr(r, name + "_weight") for name in MATRICES}

    gathers[ATTEND].place(shards[ATTEND])
    gathers[ATTEND].begin()


    columns_of = {name: getattr(r, name + "_columns").shape[1] * outer * GROUP for name in MATRICES}
    late_at = late_places(columns_of, width)
    column_at = column_places(columns_of, width)

    def early_value():
        thin = r.vectors_own.shape[1]
        r.packed[...] = jnp.zeros_like(r.packed)
        r.packed[0:6, 0:thin] = r.vectors_own[...]
        vectors = pltpu.roll(r.packed[0:8, :], chip * thin, 1)
        r.packed[0:8, :] = vectors
        for at, name in enumerate(MATRICES):
            lanes = slice(at * 128, at * 128 + 128)
            shard = shards[name][...]
            r.packed[SQUARES : SQUARES + 1, lanes] = fold_lanes(
                jnp.sum(fold_rows(shard * shard), axis=0, keepdims=True)
            )
            total = jnp.sum(getattr(r, name + "_rows")[...], axis=1, keepdims=True)
            first_lane = lax.broadcasted_iota(jnp.int32, (1, 128), 1) == 0
            r.packed[ROW_SUMS : ROW_SUMS + 1, lanes] = jnp.where(first_lane, total, 0.0)
        return r.packed[0:EARLY_ROWS, :]

    def late_value():
        thin = r.vectors_own.shape[1]
        r.packed[...] = jnp.zeros_like(r.packed)
        r.packed[0:6, 0:thin] = r.moments_own[...]
        for name in (MERGER, SHRINK):
            row, _ = late_at[name]
            r.packed[row : row + 1, 0:thin] = getattr(r, name + "_columns")[...]
        r.packed[0:8, :] = pltpu.roll(r.packed[0:8, :], chip * thin, 1)
        for name in (ATTEND, EXPAND):
            own = getattr(r, name + "_columns")
            size = own.shape[1]
            r.spread[...] = jnp.zeros_like(r.spread)
            r.spread[0:1, 0:size] = own[...]
            whole = pltpu.roll(r.spread[:, : columns_of[name]], chip * size, 1)[0:1, :]
            split_into(r.packed, late_at[name][0], whole, width)
        return r.packed[...]


    for name in (MERGER, EXPAND, SHRINK):
        gathers[name].place(shards[name])
    gathers[ATTEND].near_start(0)
    load_tokens.wait()
    prepare(r)
    gathers[ATTEND].turn()
    for name in (MERGER, EXPAND, SHRINK):
        gathers[name].begin()
    gathers[ATTEND].pass_on()
    early.begin(early_value())
    gathers[MERGER].turn()
    gathers[ATTEND].end()
    project(r)
    gathers[EXPAND].turn()

    def early_hook():
        early.turn()

    def shrink_gather_hook():
        gathers[SHRINK].turn()

    def merger_gather_hook():
        gathers[MERGER].pass_on()

    attend_forward(r, ((1, early_hook), (2, shrink_gather_hook), (3, merger_gather_hook)))
    gathers[EXPAND].pass_on()
    early_all = early.end()
    r.early[...] = early_all
    r.vectors[...] = early_all.astype(BF16).astype(F32)
    late.begin(late_value())
    gathers[MERGER].end()
    gathers[EXPAND].end()
    first_half(r)
    late.turn()
    gathers[SHRINK].pass_on()
    load_cotangent.wait()
    gathers[SHRINK].end()
    second_half(r)
    store_result = local(r.result, r.result_out, 0)
    store_result.start()
    r.late[...] = late.end()


    shrink_gradient(r)
    sums[SHRINK].begin()
    way_back(r)
    sums[SHRINK].turn()
    vector_sum.begin(vector_total(r))
    expand_gradient(r)
    sums[EXPAND].begin()
    merger_gradient(r)
    sums[MERGER].begin()
    sums[EXPAND].turn()

    def hook_one():
        sums[SHRINK].fold()
        vector_sum.turn()

    def hook_two():
        sums[MERGER].turn()

    def hook_three():
        attend_gradient(r, 0)
        sums[LOW].begin()

    def hook_four():
        sums[SHRINK].pass_on()
        sums[LOW].turn()

    def hook_five():
        sums[EXPAND].fold()

    attend_backward(
        r, ((1, hook_one), (2, hook_two), (4, hook_three), (5, hook_four), (6, hook_five))
    )
    attend_gradient(r, 1)
    sums[HIGH].begin()
    sums[EXPAND].pass_on()
    sums[MERGER].pass_on()
    sums[HIGH].turn()
    input_gradient(r)
    store_input = local(r.straight, r.input_out, 1)
    store_input.start()
    r.vector_out[...] = vector_sum.end()


    def keep(name, whole):
        getattr(r, "out_" + name)[...] = whole
        squares = jnp.sum(whole * whole, axis=0, keepdims=True)
        split_into(r.packed, column_at[name][0], squares, width)

    sums[SHRINK].collect()
    sums[LOW].pass_on()
    sums[EXPAND].collect()
    sums[MERGER].collect()
    r.packed[...] = jnp.zeros_like(r.packed)
    for name in (SHRINK, EXPAND, MERGER):
        sums[name].end()
        whole = flat(getattr(r, "done_" + name)[...])
        keep(name, whole.T if name == SHRINK else whole)
    column_sum.begin(r.packed[0:COLUMN_ROWS, :])
    sums[HIGH].pass_on()
    sums[LOW].collect()
    column_sum.turn()
    sums[HIGH].collect()
    attend_half = heads_together([getattr(r, "done_" + name)[core] for name in (LOW, HIGH)])
    squares = jnp.sum(attend_half * attend_half, axis=0, keepdims=True)
    split_into(r.packed, 0, squares, width)
    last_sum.begin(r.packed[0:COLUMN_ROWS, :])
    sums[LOW].end()
    sums[HIGH].end()
    r.out_attend[...] = heads_together([flat(getattr(r, "done_" + name)[...]) for name in (LOW, HIGH)])
    r.column_out[0:COLUMN_ROWS, :] = column_sum.end()
    last_sum.turn()
    r.early_out[...] = r.early[...]
    r.late_out[...] = r.late[...]
    r.column_out[COLUMN_ROWS : 2 * COLUMN_ROWS, :] = last_sum.end()
    facts = Statistics(r, layout_sizes, r.column_out, r.vector_out[...])

    def my_half(value):
        half = value.shape[0] // 2
        return jnp.where(core == 0, value[:half], value[half:])

    rows = []
    for name in MATRICES:
        rows_old = getattr(r, name + "_rows")[...]
        whole = getattr(r, "out_" + name)
        half = whole.shape[0] // 2
        mine = whole[pl.ds(pl.multiple_of(core * half, half), half), :]
        step = facts.factored(
            name, mine, my_half(column_of(rows_old)), float(rows_old.shape[1] * outer * GROUP)
        )[3]
        rows.append(fold_lanes(jnp.sum(step * step, axis=0, keepdims=True)))
    step_sum.begin(jnp.concatenate(rows + [jnp.zeros((4, 128), F32)], axis=0))
    step_sum.turn()
    r.step_out[...] = step_sum.end()


    for copy in started.values():
        copy.leave()
    store_result.wait()
    store_input.wait()


def update_kernel(layout_sizes, names, *refs):
    outer, width, wide = layout_sizes
    r = Refs(names, refs)
    chip = lax.axis_index(FSDP)
    copies = [
        pltpu.make_async_copy(r.result_in, r.block_output, r.sems.at[0]),
        pltpu.make_async_copy(r.input_in, r.input_gradient, r.sems.at[1]),
    ]
    for copy in copies:
        copy.start()
    vector_gradient = r.vector_sum[...]
    facts = Statistics(r, layout_sizes, r.column_sum, vector_gradient)
    r.global_norm[...] = facts.norm
    for name in MATRICES:
        weight = getattr(r, name + "_weight")[...]
        rows_all = float(weight.shape[0] * outer * GROUP)
        count = rows_all * weight.shape[1]
        clipped, new_rows, new_columns, step = facts.factored(
            name, getattr(r, name + "_sum")[...], column_of(getattr(r, name + "_rows")[...]), rows_all
        )
        at = MATRICES.index(name)
        step_square = jnp.sum(r.step_sum[at : at + 1, :], axis=1, keepdims=True)
        weight_square = facts.lanes(SQUARES, name)
        shrunk = jnp.maximum(1.0, jnp.sqrt(step_square * (1.0 / count)) * (1.0 / UPDATE_LIMIT))
        stride = LEARN_RATE * jnp.maximum(0.001, jnp.sqrt(weight_square * (1.0 / count)))
        updated = weight - (stride / shrunk) * step
        getattr(r, name + "_gradient")[...] = clipped
        getattr(r, name + "_updated")[...] = updated
        getattr(r, name + "_bfloat")[...] = updated.astype(BF16)
        getattr(r, name + "_newrows")[...] = row_of(new_rows)
        size = getattr(r, name + "_newcols").shape[1]
        wide_row = jnp.broadcast_to(new_columns, (8, new_columns.shape[1]))
        whole = new_columns.shape[1]
        own = pltpu.roll(wide_row, lax.rem(whole - chip * size, whole), 1)
        getattr(r, name + "_newcols")[...] = own[0:1, 0:size]
    vectors = r.early[...]
    clipped, variance, step = vector_steps(
        vector_gradient, r.late[0:8, :], facts.clip
    )
    shrunk = jnp.maximum(1.0, jnp.sqrt(lane_mean(step * step)) * (1.0 / UPDATE_LIMIT))
    stride = LEARN_RATE * jnp.maximum(0.001, jnp.sqrt(lane_mean(vectors * vectors)))
    updated = vectors - stride * (step / shrunk)
    thin = r.vector_updated.shape[1]
    turn = lax.rem(width - chip * thin, width)
    for ref, value in (
        (r.vector_gradient, clipped),
        (r.vector_variance, variance),
        (r.vector_updated, updated),
    ):
        ref[...] = pltpu.roll(value, turn, 1)[0:6, 0:thin]
    for copy in copies:
        copy.wait()


def in_vmem():
    return pl.BlockSpec(memory_space=pltpu.VMEM)


def anywhere():
    return pl.BlockSpec(memory_space=pl.ANY)


def call(kernel, sizes, inputs, outputs, scratch, held, params, name):
    names = list(inputs) + list(outputs) + list(scratch)
    results = pl.pallas_call(
        functools.partial(kernel, sizes, names),
        in_specs=[anywhere() if key in held else in_vmem() for key in inputs],
        out_specs=[anywhere() if key in held else in_vmem() for key in outputs],
        out_shape=list(outputs.values()),
        scratch_shapes=list(scratch.values()),
        compiler_params=params,
        name=name,
    )(*inputs.values())
    return dict(zip(outputs, results, strict=True))


def staged_shards(devices, tokens, lengths, weights, vectors, rows, columns, moments, cotangent):
    outer = devices // GROUP
    slots, width = tokens.shape[1:]
    wide = weights[EXPAND].shape[1]
    sizes = (outer, width, wide)
    shape = jax.ShapeDtypeStruct
    row_in = {name + "_rows": rows[name].reshape(1, -1) for name in MATRICES}
    column_in = {name + "_columns": columns[name].reshape(1, -1) for name in MATRICES}
    weight_in = {name + "_weight": weights[name] for name in MATRICES}
    inputs = dict(
        tokens_in=tokens[0], lengths=lengths, cotangent_in=cotangent[0],
        vectors_own=vectors, moments_own=moments, **weight_in, **row_in, **column_in,
    )
    outputs = dict(
        result_out=shape((slots, width), BF16),
        input_out=shape((slots, width), F32),
        vector_out=shape((8, width), F32),
        early_out=shape((EARLY_ROWS, width), F32),
        late_out=shape((LATE_ROWS, width), F32),
        column_out=shape((2 * COLUMN_ROWS, width), F32),
        step_out=shape((8, 128), F32),
        **{"out_" + name: shape(weights[name].shape, F32) for name in MATRICES},
    )
    scratch = row_scratch(slots, width, wide)
    scratch.update(
        tokens=pltpu.VMEM((slots, width), BF16),
        cotangent=pltpu.VMEM((slots, width), BF16),
        straight=pltpu.VMEM((slots, width), F32),
        vectors=pltpu.VMEM((8, width), F32),
        early=pltpu.VMEM((EARLY_ROWS, width), F32),
        late=pltpu.VMEM((LATE_ROWS, width), F32),
        packed=pltpu.VMEM((LATE_ROWS, width), F32),
        spread=pltpu.VMEM((8, wide), F32),
        local_sems=pltpu.SemaphoreType.DMA((2,)),
    )
    for name, cores, size in (
        ("early", 1, (EARLY_ROWS, width)),
        ("late", 1, (LATE_ROWS, width)),
        ("vector", 2, (8, width)),
        ("column", 1, (COLUMN_ROWS, width)),
        ("last", 2, (COLUMN_ROWS, width)),
        ("step", 2, (8, 128)),
    ):
        scratch[name + "_near"] = pltpu.VMEM((cores, GROUP) + size, F32)
        scratch[name + "_far"] = pltpu.VMEM((outer,) + size, F32)
        for way in ("_sends", "_receives"):
            scratch[name + way] = pltpu.SemaphoreType.DMA((2 * GROUP + outer,))
    for name in MATRICES:
        held, wide_now = weights[name].shape
        scratch[name] = pltpu.VMEM((outer, GROUP, 2, held // 2, wide_now), BF16)
        for way in ("_sends", "_receives"):
            scratch[name + way] = pltpu.SemaphoreType.DMA((GROUP * outer + GROUP,))
    for name in REDUCED:
        held, wide_now = weights[ATTEND if name in (LOW, HIGH) else name].shape
        half = (held // 2, wide_now)
        if name == SHRINK:
            half = (wide_now // 2, held)
        elif name in (LOW, HIGH):
            half = (held // 2, wide_now // 2)
        scratch["g_" + name] = pltpu.VMEM((outer, GROUP, 2) + half, BF16)
        scratch["pair_" + name] = pltpu.VMEM((outer, GROUP) + half, BF16)
        scratch["near_" + name] = pltpu.VMEM((GROUP - 1, outer) + half, BF16)
        scratch["far_" + name] = pltpu.VMEM((max(1, outer - 1),) + half, BF16)
        scratch["done_" + name] = pltpu.VMEM((2,) + half, F32)
        for way in ("_sends", "_receives"):
            scratch["sum_" + name + way] = pltpu.SemaphoreType.DMA((GROUP + outer + 1,))
    got = call(
        shard_kernel, sizes, inputs, outputs, scratch,
        ("tokens_in", "cotangent_in", "result_out", "input_out"),
        pltpu.CompilerParams(
            collective_id=1, has_side_effects=True, vmem_limit_bytes=VMEM_LIMIT
        ),
        "row_and_sums",
    )
    inputs = dict(
        result_in=got["result_out"], input_in=got["input_out"], vector_sum=got["vector_out"],
        early=got["early_out"], late=got["late_out"], column_sum=got["column_out"], step_sum=got["step_out"],
        **{name + "_sum": got["out_" + name] for name in MATRICES},
        **weight_in, **row_in, **column_in,
    )
    outputs = dict(
        block_output=shape((slots, width), BF16),
        input_gradient=shape((slots, width), F32),
        global_norm=shape((1, 1), F32),
    )
    for name in MATRICES:
        outputs[name + "_gradient"] = shape(weights[name].shape, F32)
        outputs[name + "_newrows"] = shape(row_in[name + "_rows"].shape, F32)
        outputs[name + "_newcols"] = shape(column_in[name + "_columns"].shape, F32)
        outputs[name + "_updated"] = shape(weights[name].shape, F32)
        outputs[name + "_bfloat"] = shape(weights[name].shape, BF16)
    for name in ("vector_gradient", "vector_variance", "vector_updated"):
        outputs[name] = shape(vectors.shape, F32)
    out = call(
        update_kernel, sizes, inputs, outputs, dict(sems=pltpu.SemaphoreType.DMA((2,))),
        ("block_output", "input_gradient"),
        pltpu.CompilerParams(vmem_limit_bytes=VMEM_LIMIT),
        "update",
    )
    out["block_output"] = out["block_output"][None]
    out["input_gradient"] = out["input_gradient"][None]
    out["global_norm"] = out["global_norm"].reshape(())
    for name in MATRICES:
        for kind in ("_newrows", "_newcols"):
            out[name + kind] = out[name + kind].reshape(-1)
    return tuple(out.values())


def row_kernel(names, *refs):
    r = Refs(names, refs)
    prepare(r)
    project(r)
    attend_forward(r, ())
    first_half(r)
    second_half(r)
    shrink_gradient(r)
    way_back(r)
    r.g_vectors[...] = vector_total(r)
    expand_gradient(r)
    merger_gradient(r)
    attend_backward(r, ())
    r.g_attend = (r.g_attend_low, r.g_attend_high)
    attend_gradient(r, 0)
    attend_gradient(r, 1)
    input_gradient(r)


def plain_shards(devices, tokens, lengths, weights, vectors, rows, columns, moments, cotangent):
    slots, width = tokens.shape[1:]
    wide = weights[EXPAND].shape[1]
    shape = jax.ShapeDtypeStruct
    whole = {
        name: lax.all_gather(weights[name].astype(BF16), FSDP, axis=0, tiled=True)
        for name in MATRICES
    }
    vector_rows = lax.all_gather(vectors.astype(BF16), FSDP, axis=1, tiled=True).astype(F32)
    vector_rows = jnp.concatenate([vector_rows, jnp.zeros((2, width), F32)], axis=0)
    inputs = dict(
        tokens=tokens[0], lengths=lengths, cotangent=cotangent[0], vectors=vector_rows, **whole
    )
    outputs = dict(
        result=shape((slots, width), BF16),
        straight=shape((slots, width), F32),
        g_vectors=shape((8, width), F32),
        g_attend_low=shape((width, 3 * width // 2), BF16),
        g_attend_high=shape((width, 3 * width // 2), BF16),
        g_merger=shape((width, width), BF16),
        g_expand=shape((width, wide), BF16),
        g_shrink=shape((width, wide), BF16),
    )
    scratch = row_scratch(slots, width, wide)
    scratch["d_branch"] = pltpu.VMEM((slots, width), BF16)
    names = list(inputs) + list(outputs) + list(scratch)
    got = pl.pallas_call(
        functools.partial(row_kernel, names),
        in_specs=[in_vmem()] * len(inputs),
        out_specs=[in_vmem()] * len(outputs),
        out_shape=list(outputs.values()),
        scratch_shapes=list(scratch.values()),
        compiler_params=pltpu.CompilerParams(vmem_limit_bytes=VMEM_LIMIT),
        name="row",
    )(*inputs.values())
    got = dict(zip(outputs, got, strict=True))
    got["g_" + ATTEND] = heads_together((got["g_attend_low"], got["g_attend_high"]))
    grads = []
    for name in MATRICES:
        value = lax.psum(got["g_" + name], DP).astype(F32)
        if name == SHRINK:
            grads.append(lax.psum_scatter(value.T, FSDP, scatter_dimension=0, tiled=True))
        else:
            grads.append(lax.psum_scatter(value, FSDP, scatter_dimension=0, tiled=True))
    vector_all = lax.psum(got["g_vectors"][:6], (DP, FSDP))
    index = lax.axis_index(FSDP)

    def spread(own, dim):
        size = own.shape[dim]
        extent = own.shape[:dim] + (size * devices,) + own.shape[dim + 1 :]
        return lax.dynamic_update_slice_in_dim(
            jnp.zeros(extent, F32), own, index * size, dim
        )

    early = (
        [spread(columns[name], 0) for name in MATRICES],
        [jnp.sum(weights[name] * weights[name]) for name in MATRICES],
        [jnp.sum(rows[name]) for name in MATRICES],
        [jnp.sum(grad * grad, axis=0) for grad in grads],
        jnp.sum(vectors * vectors, axis=1),
    )
    old_columns, weight_squares, row_sums, columns_now, vector_squares = lax.psum(early, FSDP)
    squares = [jnp.sum(value) for value in columns_now]
    total = jnp.sum(vector_all * vector_all)
    for value in squares:
        total = total + value
    norm = jnp.sqrt(total)
    clip = jnp.minimum(1.0, THRESHOLD / norm)
    power = clip * clip
    pieces = []
    for at, name in enumerate(MATRICES):
        grad = grads[at]
        rows_all = float(grad.shape[0] * devices)
        count = rows_all * grad.shape[1]
        new_rows = FORGET * rows[name] + (1.0 - FORGET) * (
            power * jnp.mean(grad * grad, axis=1) + TINY_VALUE
        )
        new_columns = FORGET * old_columns[at] + (1.0 - FORGET) * (
            power * columns_now[at] / rows_all + TINY_VALUE
        )
        mean = FORGET * row_sums[at] / rows_all + (1.0 - FORGET) * (
            power * squares[at] / count + TINY_VALUE
        )
        clipped = clip * grad
        step = clipped * lax.rsqrt(new_rows[:, None] * new_columns[None, :] / mean)
        pieces.append((clipped, new_rows, new_columns, step, count))
    thin = vectors.shape[1]
    vector_clipped = clip * lax.dynamic_slice_in_dim(vector_all, index * thin, thin, 1)
    variance = FORGET * moments + (1.0 - FORGET) * (vector_clipped * vector_clipped + TINY_VALUE)
    vector_step = vector_clipped * lax.rsqrt(variance)
    step_squares, vector_step_squares = lax.psum(
        (
            [jnp.sum(piece[3] * piece[3]) for piece in pieces],
            jnp.sum(vector_step * vector_step, axis=1),
        ),
        FSDP,
    )
    results = [got["result"][None], got["straight"][None], norm]
    for at, name in enumerate(MATRICES):
        clipped, new_rows, new_columns, step, count = pieces[at]
        shrunk = jnp.maximum(1.0, jnp.sqrt(step_squares[at] / count) / UPDATE_LIMIT)
        stride = LEARN_RATE * jnp.maximum(0.001, jnp.sqrt(weight_squares[at] / count))
        updated = weights[name] - stride * (step / shrunk)
        size = columns[name].shape[0]
        own = lax.dynamic_slice_in_dim(new_columns, index * size, size, 0)
        results.extend([clipped, new_rows, own, updated, updated.astype(BF16)])
    extent = float(width)
    shrunk = jnp.maximum(1.0, jnp.sqrt(vector_step_squares / extent) / UPDATE_LIMIT)[:, None]
    stride = LEARN_RATE * jnp.maximum(0.001, jnp.sqrt(vector_squares / extent))[:, None]
    results.extend([vector_clipped, variance, vectors - stride * (vector_step / shrunk)])
    return tuple(results)


def shards(
    devices,
    tokens,
    lengths,
    attend_weight,
    merger_weight,
    expand_weight,
    shrink_weight,
    vectors,
    attend_rows,
    attend_columns,
    merger_rows,
    merger_columns,
    expand_rows,
    expand_columns,
    shrink_rows,
    shrink_columns,
    vector_moments,
    cotangent,
):
    weights = dict(
        attend=attend_weight, merger=merger_weight, expand=expand_weight, shrink=shrink_weight
    )
    rows = dict(attend=attend_rows, merger=merger_rows, expand=expand_rows, shrink=shrink_rows)
    columns = dict(
        attend=attend_columns, merger=merger_columns, expand=expand_columns, shrink=shrink_columns
    )
    assert tokens.shape[0] == 1
    fits = devices % GROUP == 0 and all(
        weight.shape[0] % 32 == 0 for weight in weights.values()
    ) and shrink_weight.shape[0] % 128 == 0
    body = staged_shards if fits else plain_shards
    return body(
        devices, tokens, lengths, weights, vectors, rows, columns, vector_moments, cotangent
    )


def solution(mesh):
    split = P(FSDP, None)
    row = P((DP, FSDP), None, None)
    one = P(FSDP)
    thin = P(None, FSDP)
    in_specs = (
        (row, P((DP, FSDP), None)) + (split,) * 4 + (thin,) + (one,) * 8 + (thin, row)
    )
    out_specs = (row, row, P()) + (split, one, one, split, split) * 4 + (thin,) * 3
    return jax.shard_map(
        functools.partial(shards, mesh.shape[FSDP]),
        mesh=mesh, in_specs=in_specs, out_specs=out_specs, check_vma=False,
    )
```

```python
import functools

import jax
import jax.numpy as jnp
from jax import lax
from jax.experimental import pallas as pl
from jax.experimental.pallas import tpu as pltpu
from jax.sharding import PartitionSpec as P

F32 = jnp.float32
BF16 = jnp.bfloat16
HEAD_DIM = 64
STEP = 3
EPSILON = 1e-05
TINY_VALUE = 1e-30
NEGATIVE = -1e30
THRESHOLD = 1.0
UPDATE_LIMIT = 1.0
LEARN_RATE = 0.5
FORGET = 1.0 - float(STEP) ** (-0.8)
LOG2_E = 1.4426950408889634
GELU_A = 0.7978845608028654
GELU_B = 0.044715 * GELU_A

REACH = 256
QUERY_BLOCK = 128
TILE = 256
GROUP = 4
DP, FSDP = "dp", "fsdp"
ATTEND, MERGER, EXPAND, SHRINK = "attend", "merger", "expand", "shrink"
MATRICES = (ATTEND, MERGER, EXPAND, SHRINK)
MESH = pl.DeviceIdType.MESH
VMEM_LIMIT = 63 << 20


def dot_general(left, right, left_dim, right_dim):
    return lax.dot_general(
        left, right, (((left_dim,), (right_dim,)), ((), ())), preferred_element_type=F32
    )


def dot_nn(left, right):
    return dot_general(left, right, 1, 0)


def dot_nt(left, right):
    return dot_general(left, right, 1, 1)


def dot_tn(left, right):
    return dot_general(left, right, 0, 0)


def flat(value):
    return value.reshape(-1, value.shape[-1])


def whole(parts):
    return jnp.concatenate([flat(part[...]) for part in parts], axis=1)


def fold_rows(value):
    return jnp.sum(value.reshape(value.shape[0] // 8, 8, value.shape[1]), axis=0)


def fold_lanes(row):
    total = row[:, :128]
    for start in range(128, row.shape[1], 128):
        total = total + row[:, start : start + 128]
    return total


def diagonal(size):
    return lax.broadcasted_iota(jnp.int32, (size, size), 0) == lax.broadcasted_iota(
        jnp.int32, (size, size), 1
    )


def column_of(row):
    size = row.shape[1]
    return jnp.sum(jnp.where(diagonal(size), row, 0.0), axis=1, keepdims=True)


def row_of(column):
    size = column.shape[0]
    return jnp.sum(jnp.where(diagonal(size), column, 0.0), axis=0, keepdims=True)


def lane_mean(value):
    return jnp.mean(value, axis=-1, keepdims=True)


def aligned(start, size):
    return pl.ds(pl.multiple_of(start, size), size)


def band(slots):
    pieces = []
    place = 0
    for first in range(0, slots, QUERY_BLOCK):
        low = max(0, first - REACH)
        high = first + QUERY_BLOCK
        pieces.append((first, low, high, place))
        place += high - low
    return pieces, place


def prepare(r):
    slots = r.tokens.shape[0]
    count = r.lengths.shape[1]
    for start in range(0, slots, TILE):
        r.tokens_t[:, start : start + TILE] = r.tokens[start : start + TILE, :].T
    lengths = r.lengths[...].astype(F32)
    rows = jnp.broadcast_to(lengths, (8, count)).astype(BF16)
    upto = lax.broadcasted_iota(jnp.int32, (count, count), 1) <= lax.broadcasted_iota(
        jnp.int32, (count, count), 0
    )
    ends = dot_nt(jnp.where(upto, 1.0, 0.0).astype(BF16), rows)[:, 0:1]
    places = lax.broadcasted_iota(jnp.int32, (count, slots), 1).astype(F32)
    ended = jnp.where(ends <= places, 1.0, 0.0).astype(BF16)
    begin = dot_nn(rows, ended)[0:1, :]
    total = jnp.sum(lengths, axis=1, keepdims=True)
    r.total[...] = jnp.broadcast_to(total, r.total.shape)
    slot = lax.broadcasted_iota(jnp.int32, (1, slots), 1).astype(F32)
    begin = jnp.where(slot < total, begin, slot)
    for first, low, high, place in band(slots)[0]:
        key = (lax.broadcasted_iota(jnp.int32, (high - low, QUERY_BLOCK), 0) + low).astype(F32)
        query = slot[:, first : first + QUERY_BLOCK]
        fits = (key >= begin[:, first : first + QUERY_BLOCK]) & (key <= query)
        r.mask[place : place + high - low, :] = jnp.where(fits, 1.0, 0.0).astype(BF16)


def project(r, part):
    width = r.tokens.shape[1]
    half = width // 2
    columns = flat(r.attend[part][...])
    for at in range(3):
        rows = slice(at * width + part * half, at * width + (part + 1) * half)
        value = dot_tn(columns[:, at * half : (at + 1) * half], r.tokens_t[...]).astype(BF16)
        r.projected_t[rows, :] = value
    for at in range(2):
        start = at * width + part * half
        r.key_value[:, start : start + half] = r.projected_t[
            width + start : width + start + half, :
        ].T


def beside_zeros(value, head):
    zeros = jnp.zeros_like(value)
    return jnp.concatenate([value, zeros] if head == 0 else [zeros, value], axis=0)


def head_rows(part, width, pair, head):
    return pl.ds(pl.multiple_of(part * width + pair * 128 + HEAD_DIM * head, HEAD_DIM), HEAD_DIM)


def by_pairs(first, last, hooks, body):
    def pair(step, carry):
        for at, hook in hooks:
            pl.when(step == at)(hook)
        body(step)
        return carry

    lax.fori_loop(first, last, pair, 0)


def attend_forward(r, first_pair, last_pair, hooks):
    slots, width = r.tokens.shape
    factor = HEAD_DIM ** -0.5 * LOG2_E
    items = [(head,) + piece for head in (0, 1) for piece in band(slots)[0]]

    def body(pair):
        lanes = pl.ds(pl.multiple_of(pair * 128, 128), 128)

        def scores_of(item):
            head, first, low, high, _ = item
            queries = r.projected_t[head_rows(0, width, pair, head), first : first + QUERY_BLOCK]
            return dot_nn(r.key_value[low:high, lanes], beside_zeros(queries, head))

        def probs_of(item, scores):
            head, _, low, high, place = item
            fits = r.mask[place : place + high - low, :].astype(F32) > 0.5
            scores = jnp.where(fits, scores * factor, NEGATIVE)
            weights = jnp.exp2(scores - jnp.max(scores, axis=0, keepdims=True))
            inverse = 1.0 / jnp.sum(weights, axis=0, keepdims=True)
            probs = (weights * inverse).astype(BF16)
            r.probs[2 * pair + head, place : place + high - low, :] = probs
            return probs

        def put_context(item, probs):
            head, first, low, high, _ = item
            values = r.projected_t[head_rows(2, width, pair, head), low:high]
            r.context_t[head_rows(0, width, pair, head), first : first + QUERY_BLOCK] = dot_nn(
                values, probs
            ).astype(BF16)

        scores = [scores_of(item) for item in items]
        probs = [probs_of(item, value) for item, value in zip(items, scores)]
        for item, value in zip(items, probs):
            put_context(item, value)

    by_pairs(first_pair, last_pair, hooks, body)


def attend_backward(r, first_pair, last_pair, hooks):
    slots, width = r.tokens.shape
    scale = HEAD_DIM ** -0.5
    pieces = band(slots)[0]
    count = len(pieces)
    items = [(head, at) for head in (0, 1) for at in range(count)]

    def body(pair):
        lanes = pl.ds(pl.multiple_of(width + pair * 128, 128), 128)
        queries = [r.projected_t[head_rows(0, width, pair, head), :] for head in (0, 1)]
        keys_t = [r.projected_t[head_rows(1, width, pair, head), :] for head in (0, 1)]
        upstream = [r.d_context_t[head_rows(0, width, pair, head), :] for head in (0, 1)]

        def probs_of(item):
            _, low, high, place = pieces[item[1]]
            return r.probs[2 * pair + item[0], place : place + high - low, :]

        def d_probs_of(item):
            first, low, high, _ = pieces[item[1]]
            arriving = upstream[item[0]][:, first : first + QUERY_BLOCK]
            return dot_nn(r.key_value[low:high, lanes], beside_zeros(arriving, item[0]))

        def d_scores_of(item, d_probs):
            wide = probs_of(item).astype(F32)
            inner = jnp.sum(wide * d_probs, axis=0, keepdims=True)
            return (wide * (d_probs - inner)).astype(BF16)

        def put_queries(item, d_scores):
            first, low, high, _ = pieces[item[1]]
            value = dot_nn(keys_t[item[0]][:, low:high], d_scores) * scale
            r.projected_t[
                head_rows(0, width, pair, item[0]), first : first + QUERY_BLOCK
            ] = value.astype(BF16)

        def put_keys_and_values(item, known):
            head, at = item
            begin = pieces[at][0]
            seen = [i for i in range(count) if pieces[i][1] <= begin <= pieces[i][0]]
            span = slice(pieces[seen[0]][0], pieces[seen[-1]][0] + QUERY_BLOCK)
            here = slice(begin, begin + QUERY_BLOCK)

            def together(values):
                parts = []
                for i, value in zip(seen, values):
                    start = begin - pieces[i][1]
                    parts.append(value[start : start + QUERY_BLOCK, :])
                return jnp.concatenate(parts, axis=1)

            d_scores = together([known[(head, i)] for i in seen])
            probs = together([probs_of((head, i)) for i in seen])
            r.projected_t[head_rows(1, width, pair, head), here] = (
                dot_nt(queries[head][:, span], d_scores) * scale
            ).astype(BF16)
            r.projected_t[head_rows(2, width, pair, head), here] = dot_nt(
                upstream[head][:, span], probs
            ).astype(BF16)

        d_probs = [d_probs_of(item) for item in items]
        known = {item: d_scores_of(item, value) for item, value in zip(items, d_probs)}
        for item in items:
            put_queries(item, known[item])
        for item in items:
            put_keys_and_values(item, known)

    by_pairs(first_pair, last_pair, hooks, body)


def vector_rows(r):
    return [r.vectors[place : place + 1, :] for place in range(6)]


def token_blocks(r):
    return [slice(start, start + TILE) for start in range(0, r.tokens.shape[0], TILE)]


def keep_sums(r, places, folded):
    for place, parts in zip(places, zip(*folded)):
        r.vector_sums[place] = sum(parts[1:], parts[0])


def first_half(r):
    omega_one, gain_one, shift_one = vector_rows(r)[:3]

    def front(rows):
        inputs = r.tokens[rows, :].astype(F32)
        first_sum = omega_one * inputs + dot_tn(r.context_t[:, rows], flat(r.merger[...]))
        centered = first_sum - lane_mean(first_sum)
        first_inv = lax.rsqrt(lane_mean(centered * centered) + EPSILON)
        first_normed = centered * first_inv
        r.first_inv[rows, :] = jnp.broadcast_to(first_inv, (TILE, 128))
        r.straight[rows, :] = first_normed
        first_low = (first_normed * gain_one + shift_one).astype(BF16)
        r.first_t[:, rows] = first_low.T
        return first_low

    def gelu(rows, hidden):
        square = hidden * hidden
        part = 0.5 + 0.5 * jnp.tanh(hidden * (GELU_A + GELU_B * square))
        active = hidden * part
        r.active[rows, :] = active.astype(BF16)
        slope = part + active * (1.0 - part) * (2 * GELU_A + 6 * GELU_B * square)
        r.d_hidden[rows, :] = slope.astype(BF16)

    blocks = token_blocks(r)
    lows = [front(rows) for rows in blocks]
    for rows, low in zip(blocks, lows):
        gelu(rows, dot_nn(low, whole(r.expand)))


def second_half(r):
    _, gain_one, shift_one, omega_two, gain_two, shift_two = vector_rows(r)

    def rest(rows, product):
        first_out = r.straight[rows, :] * gain_one + shift_one
        second_sum = omega_two * first_out + product
        centered = second_sum - lane_mean(second_sum)
        second_inv = lax.rsqrt(lane_mean(centered * centered) + EPSILON)
        second_normed = centered * second_inv
        arriving = r.cotangent[rows, :].astype(F32)
        r.result[rows, :] = (second_normed * gain_two + shift_two).astype(BF16)
        place = (lax.broadcasted_iota(jnp.int32, (TILE, 1), 0) + rows.start).astype(F32)
        upstream = arriving * jnp.where(place < r.total[0:1, 0:1], 1.0, 0.0)
        scaled = upstream * gain_two
        d_second = second_inv * (
            scaled - lane_mean(scaled) - second_normed * lane_mean(scaled * second_normed)
        )
        r.d_second[rows, :] = d_second
        r.d_second_t[:, rows] = d_second.astype(BF16).T
        return (
            fold_rows(upstream * second_normed),
            fold_rows(upstream),
            fold_rows(first_out * d_second),
        )

    blocks = token_blocks(r)
    products = [dot_nn(r.active[rows, :], whole(r.shrink)) for rows in blocks]
    keep_sums(r, (4, 5, 3), [rest(rows, value) for rows, value in zip(blocks, products)])


def way_back(r, hook=None):
    omega_one, gain_one, _, omega_two = vector_rows(r)[:4]

    def to_hidden(rows):
        d_active = dot_nt(r.d_second[rows, :].astype(BF16), whole(r.shrink))
        d_hidden = (d_active * r.d_hidden[rows, :].astype(F32)).astype(BF16)
        r.d_hidden[rows, :] = d_hidden
        return d_hidden

    def to_branch(rows, product):
        d_first = product + omega_two * r.d_second[rows, :]
        first_normed = r.straight[rows, :]
        scaled = d_first * gain_one
        d_first_sum = r.first_inv[rows, 0:1] * (
            scaled - lane_mean(scaled) - first_normed * lane_mean(scaled * first_normed)
        )
        inputs = r.tokens[rows, :].astype(F32)
        r.straight[rows, :] = omega_one * d_first_sum
        branch_low = d_first_sum.astype(BF16)
        r.d_branch[rows, :] = branch_low
        folded = (
            fold_rows(inputs * d_first_sum),
            fold_rows(d_first * first_normed),
            fold_rows(d_first),
        )
        return branch_low, folded

    blocks = token_blocks(r)
    hidden = [to_hidden(rows) for rows in blocks]
    if hook is not None:
        hook()
    products = [dot_nt(value, whole(r.expand)) for value in hidden]
    got = [to_branch(rows, value) for rows, value in zip(blocks, products)]
    for rows, value in zip(blocks, got):
        r.d_context_t[:, rows] = dot_nt(flat(r.merger[...]), value[0]).astype(BF16)
    keep_sums(r, (0, 1, 2), [value[1] for value in got])


def vector_total(r):
    rows = [jnp.sum(r.vector_sums[place], axis=0, keepdims=True) for place in range(6)]
    return jnp.concatenate(rows + [jnp.zeros((2, rows[0].shape[1]), F32)], axis=0)


def put_tile(ref, columns, value):
    ref[..., columns] = value.astype(ref.dtype).reshape(ref.shape[:-1] + (value.shape[1],))


def shrink_gradient(r, part):
    into = r.g_shrink[part]
    half = r.tokens.shape[1] // 2
    owned = into.shape[-1]
    rows = r.d_second_t[part * half : (part + 1) * half, :]
    value = dot_nn(rows, r.active[...]).astype(BF16)
    for owner in range(value.shape[1] // owned):
        into[owner // GROUP, owner % GROUP] = value[
            :, owner * owned : (owner + 1) * owned
        ].reshape(2, half // 2, owned)


def expand_gradient(r, part):
    half = r.active.shape[1] // 2
    columns = slice(part * half, (part + 1) * half)
    put_tile(r.g_expand[part], slice(None), dot_nn(r.first_t[...], r.d_hidden[:, columns]))


def merger_gradient(r):
    put_tile(r.g_merger, slice(None), dot_nn(r.context_t[...], r.d_branch[...]))


def half_heads(r, part, slots):
    width = r.tokens.shape[1]
    half = width // 2
    starts = [at * width + part * half for at in range(3)]
    return jnp.concatenate([r.projected_t[start : start + half, slots] for start in starts], axis=0)


def attend_gradient(r, part):
    put_tile(r.g_attend[part], slice(None), dot_nt(r.tokens_t[...], half_heads(r, part, slice(None))))


def heads_together(parts):
    half = parts[0].shape[1] // 3
    return jnp.concatenate(
        [part[:, at * half : (at + 1) * half] for at in range(3) for part in parts], axis=1
    )


def heads_apart(whole):
    half = whole.shape[1] // 6
    return [
        jnp.concatenate(
            [whole[:, (2 * at + part) * half : (2 * at + part + 1) * half] for at in range(3)],
            axis=1,
        )
        for part in range(2)
    ]


def input_gradient(r):
    blocks = token_blocks(r)
    products = []
    for rows in blocks:
        halves = [
            dot_general(half_heads(r, part, rows), flat(r.attend[part][...]), 0, 1)
            for part in range(2)
        ]
        products.append(halves[0] + halves[1])
    for rows, value in zip(blocks, products):
        r.straight[rows, :] += value


def row_scratch(slots, width, wide):
    packed = band(slots)[1]
    heads = width // HEAD_DIM
    return dict(
        tokens_t=pltpu.VMEM((width, slots), BF16),
        mask=pltpu.VMEM((packed, QUERY_BLOCK), BF16),
        total=pltpu.VMEM((8, 128), F32),
        projected_t=pltpu.VMEM((3 * width, slots), BF16),
        key_value=pltpu.VMEM((slots, 2 * width), BF16),
        probs=pltpu.VMEM((heads, packed, QUERY_BLOCK), BF16),
        context_t=pltpu.VMEM((width, slots), BF16),
        d_context_t=pltpu.VMEM((width, slots), BF16),
        active=pltpu.VMEM((slots, wide), BF16),
        d_hidden=pltpu.VMEM((slots, wide), BF16),
        first_t=pltpu.VMEM((width, slots), BF16),
        d_second_t=pltpu.VMEM((width, slots), BF16),
        vector_sums=pltpu.VMEM((6, 8, width), F32),
        first_inv=pltpu.VMEM((slots, 128), F32),
        d_second=pltpu.VMEM((slots, width), F32),
    )


class Refs:
    def __init__(self, names, refs):
        for name, ref in zip(names, refs, strict=True):
            setattr(self, name, ref)


LOW, HIGH = "low", "high"
EXPAND_A, EXPAND_B, SHRINK_A, SHRINK_B = "ea", "eb", "sa", "sb"
PARTS_OF = {
    ATTEND: (LOW, HIGH),
    MERGER: (MERGER,),
    EXPAND: (EXPAND_A, EXPAND_B),
    SHRINK: (SHRINK_A, SHRINK_B),
}
PARTS = (LOW, HIGH, MERGER, EXPAND_A, EXPAND_B, SHRINK_A, SHRINK_B)
NEAR_FIRST = (EXPAND_B,)
FAR_FIRST = (SHRINK_A, MERGER)


def in_parts(name, value):
    if name == ATTEND:
        return heads_apart(value)
    count = len(PARTS_OF[name])
    size = value.shape[1] // count
    return [value[:, at * size : (at + 1) * size] for at in range(count)]


def packed_rows(first, order, columns_of, width):
    places = {}
    for name in order:
        places[name] = (first, columns_of[name] // width)
        first += columns_of[name] // width
    return places


SQUARES, ROW_SUMS, EARLY_ROWS = 6, 7, 8
LATE_COLUMNS, LATE_ROWS = 6, 16
COLUMN_ROWS = 8
ALL = slice(None)


def late_places(columns_of, width):
    return packed_rows(LATE_COLUMNS, (MERGER, SHRINK, ATTEND, EXPAND), columns_of, width)


def column_places(columns_of, width):
    places = packed_rows(0, (MERGER, EXPAND, SHRINK), columns_of, width)
    places.update(packed_rows(COLUMN_ROWS, (ATTEND,), columns_of, width))
    return places


def joined(ref, start, count):
    return jnp.concatenate([ref[place : place + 1, :] for place in range(start, start + count)], 1)


def split_into(ref, start, row, width):
    for piece in range(row.shape[1] // width):
        ref[start + piece : start + piece + 1, :] = row[:, piece * width : (piece + 1) * width]


def scalar_sum(value):
    return jnp.sum(jnp.sum(value, axis=1, keepdims=True), axis=0, keepdims=True)


def flat_slots(value):
    return value.reshape((-1,) + value.shape[2:])


class Statistics:
    def __init__(self, r, sizes, columns, vector_gradient):
        outer, self.width, _ = sizes
        self.devices = outer * GROUP
        columns_of = {
            name: getattr(r, name + "_columns").shape[1] * self.devices for name in MATRICES
        }
        self.early, self.late, self.columns = r.early, r.late, columns
        self.late_at = late_places(columns_of, self.width)
        self.column_at = column_places(columns_of, self.width)
        self.squares = {
            name: scalar_sum(joined(columns, *self.column_at[name])) for name in MATRICES
        }
        total = scalar_sum(vector_gradient * vector_gradient)
        for name in MATRICES:
            total = total + self.squares[name]
        self.norm = jnp.sqrt(total)
        self.clip = jnp.minimum(1.0, THRESHOLD / self.norm)

    def lanes(self, row, name):
        at = MATRICES.index(name) * 128
        return jnp.sum(self.early[row : row + 1, at : at + 128], axis=1, keepdims=True)

    def factored(self, name, gradient, rows_old, rows_all):
        wide = gradient.shape[1]
        power = self.clip * self.clip
        row_mean = jnp.sum(gradient * gradient, axis=1, keepdims=True) * (1.0 / wide)
        new_rows = FORGET * rows_old + (1.0 - FORGET) * (power * row_mean + TINY_VALUE)
        now = joined(self.columns, *self.column_at[name]) * (1.0 / rows_all)
        new_columns = FORGET * joined(self.late, *self.late_at[name]) + (1.0 - FORGET) * (
            power * now + TINY_VALUE
        )
        mean = FORGET * (self.lanes(ROW_SUMS, name) * (1.0 / rows_all)) + (1.0 - FORGET) * (
            power * (self.squares[name] * (1.0 / (rows_all * wide))) + TINY_VALUE
        )
        clipped = self.clip * gradient
        step = clipped * lax.rsqrt(new_rows * new_columns * (1.0 / mean))
        return clipped, new_rows, new_columns, step


def vector_steps(gradient, moments, clip):
    clipped = clip * gradient
    variance = FORGET * moments + (1.0 - FORGET) * (clipped * clipped + TINY_VALUE)
    return clipped, variance, clipped * lax.rsqrt(variance)


def shard_kernel(layout_sizes, names, *refs):
    outer, width, wide = layout_sizes
    r = Refs(names, refs)
    r.result = r.cotangent
    r.d_branch = r.tokens
    for name in (ATTEND, EXPAND, SHRINK):
        setattr(r, name, [getattr(r, part) for part in PARTS_OF[name]])
        setattr(r, "g_" + name, [getattr(r, "g_" + part) for part in PARTS_OF[name]])
    core = lax.axis_index(DP)
    chip = lax.axis_index(FSDP)
    far = chip // GROUP
    near = lax.rem(chip, GROUP)
    sibling = (1 - core, chip)
    near_steps = range(1, GROUP)
    far_steps = range(1, outer)

    near_places = [near] + [jnp.bitwise_xor(near, step) for step in near_steps]
    far_places = [lax.rem(far + step, outer) for step in range(outer)]
    far_origins = [lax.rem(far + outer - step, outer) for step in range(outer)]
    near_devices = [(core, far * GROUP + place) for place in near_places]
    far_devices = [(core, place * GROUP + near) for place in far_places]
    other = 1 - core
    started = {}
    arrived = set()

    class Copy:
        def __init__(self, key, sems, index, device, source, target, landing=None):
            self.key = key + (index,)
            self.device = device
            self.sems = sems
            self.index = index
            self.source = source
            self.target = target
            self.landing = target if landing is None else landing

        def describe(self, source, target):
            return pltpu.make_async_remote_copy(
                src_ref=source[0].at[source[1]],
                dst_ref=target[0].at[target[1]],
                send_sem=self.sems[0].at[self.index],
                recv_sem=self.sems[1].at[self.index],
                device_id=self.device,
                device_id_type=MESH,
            )

        def start(self):
            self.describe(self.source, self.target).start()
            started[self.key] = self

        def arrive(self):
            self.describe(self.landing, self.landing).wait_recv()
            arrived.add(self.key)

        def leave(self):
            self.describe(self.source, self.target).wait_send()

    def local(source, target, index):
        return pltpu.make_async_copy(source, target, r.local_sems.at[index])

    load_tokens = local(r.tokens_in, r.tokens, 0)
    load_cotangent = local(r.cotangent_in, r.cotangent, 1)
    load_tokens.start()
    load_cotangent.start()

    barrier = pltpu.get_barrier_semaphore()
    for step in near_steps:
        pl.semaphore_signal(barrier, inc=1, device_id=near_devices[step], device_id_type=MESH)
    for step in far_steps:
        pl.semaphore_signal(barrier, inc=1, device_id=far_devices[step], device_id_type=MESH)
    pl.semaphore_signal(barrier, inc=1, device_id=sibling, device_id_type=MESH)
    pl.semaphore_wait(barrier, len(near_steps) + len(far_steps) + 1)


    class Sum:
        def __init__(self, name, cores):
            self.key = (name,)
            self.near = getattr(r, name + "_near")
            self.far = getattr(r, name + "_far")
            self.sems = (getattr(r, name + "_sends"), getattr(r, name + "_receives"))
            self.steps = [(0, step) for step in near_steps]
            if cores == 2:
                self.steps += [(1, step) for step in range(GROUP)]
            self.mine = core if cores == 2 else 0
            self.other = other if cores == 2 else 0

        def near_copy(self, cross, step):
            mine = (self.near, (self.mine, near))
            whose = self.other if cross else self.mine
            device = (other if cross else core, near_devices[step][1])
            return Copy(
                self.key, self.sems, cross * GROUP + step, device, mine, mine,
                (self.near, (whose, near_places[step])),
            )

        def far_copy(self, step):
            mine = (self.far, far)
            return Copy(
                self.key, self.sems, 2 * GROUP + step, far_devices[step], mine, mine,
                (self.far, far_origins[step]),
            )

        def begin(self, value):
            self.near[self.mine, near] = value
            for cross, step in self.steps:
                self.near_copy(cross, step).start()

        def turn(self):
            for cross, step in self.steps:
                self.near_copy(cross, step).arrive()
            self.far[far] = jnp.sum(flat_slots(self.near[...]), axis=0)
            for step in far_steps:
                self.far_copy(step).start()

        def end(self):
            for step in far_steps:
                self.far_copy(step).arrive()
            return jnp.sum(self.far[...], axis=0)


    class Gather:
        def __init__(self, name):
            self.key = (name,)
            self.near_first = name in NEAR_FIRST
            self.held = getattr(r, name)
            self.sems = (getattr(r, name + "_sends"), getattr(r, name + "_receives"))

        def far_copy(self, step):
            block = ALL if self.near_first else near
            mine = (self.held, (far, block, core))
            return Copy(
                self.key, self.sems, step, far_devices[step], mine, mine,
                (self.held, (far_origins[step], block, core)),
            )

        def near_copy(self, step, hop):
            slot = far_origins[hop]
            mine = (self.held, (slot, near, core))
            return Copy(
                self.key, self.sems, step * outer + hop, near_devices[step], mine, mine,
                (self.held, (slot, near_places[step], core)),
            )

        def cross(self, step):
            if self.near_first:
                block = (far_origins[step], ALL)
            else:
                block = (ALL, near_places[step])
            mine = (self.held, block + (core,))
            return Copy(
                self.key, self.sems, GROUP * outer + step, sibling, mine, mine,
                (self.held, block + (other,)),
            )

        def place(self, mine):
            self.held[far, near, core] = mine.astype(BF16)

        def far_start(self):
            for step in far_steps:
                self.far_copy(step).start()

        def near_start(self, hop):
            for step in near_steps:
                self.near_copy(step, hop).start()

        def begin(self):
            if not self.near_first:
                self.far_start()

        def turn(self):
            if self.near_first:
                for step in near_steps:
                    self.near_copy(step, 0).arrive()
                self.far_start()
            else:
                for hop in far_steps:
                    self.far_copy(hop).arrive()
                    self.near_start(hop)
            self.cross(0).start()

        def pass_on(self):
            if self.near_first:
                for step in far_steps:
                    self.far_copy(step).arrive()
                    self.cross(step).start()
                return
            for step in near_steps:
                for hop in range(outer):
                    self.near_copy(step, hop).arrive()
                self.cross(step).start()

        def end(self):
            for step in range(outer if self.near_first else GROUP):
                self.cross(step).arrive()


    class Reduce:
        def __init__(self, name):
            self.key = ("sum", name)
            self.far_first = name in FAR_FIRST
            for part in ("g", "pair", "near", "far", "done"):
                setattr(self, part, getattr(r, part + "_" + name))
            self.sems = (
                getattr(r, "sum_" + name + "_sends"), getattr(r, "sum_" + name + "_receives")
            )

        def pair_copy(self):
            return Copy(
                self.key, self.sems, 0, sibling, (self.g, (ALL, ALL, other)),
                (self.pair, ALL),
            )

        def near_copy(self, step):
            block = far if self.far_first else ALL
            return Copy(
                self.key, self.sems, step, near_devices[step],
                (self.pair, (block, near_places[step])), (self.near, step - 1),
            )

        def far_copy(self, step):
            block = ALL if self.far_first else near
            return Copy(
                self.key, self.sems, GROUP + step - 1, far_devices[step],
                (self.pair, (far_places[step], block)), (self.far, step - 1),
            )

        def done_copy(self):
            mine = (self.done, core)
            return Copy(
                self.key, self.sems, GROUP + outer, sibling, mine, mine,
                (self.done, other),
            )

        def begin(self):
            self.pair_copy().start()

        def turn(self):
            self.pair_copy().arrive()

            def block(step, carry):
                both = self.g[step, :, core].astype(F32) + self.pair[step].astype(F32)
                self.pair[step] = both.astype(BF16)
                return carry

            lax.fori_loop(0, outer, block, 0)
            if self.far_first:
                for step in far_steps:
                    self.far_copy(step).start()
            else:
                for step in near_steps:
                    self.near_copy(step).start()

        def pass_on(self):
            if self.far_first:
                for step in far_steps:
                    self.far_copy(step).arrive()
                total = self.pair[far].astype(F32)
                for step in far_steps:
                    total = total + self.far[step - 1].astype(F32)
                self.pair[far] = total.astype(BF16)
                for step in near_steps:
                    self.near_copy(step).start()
                return
            for step in near_steps:
                self.near_copy(step).arrive()

            def block(step, carry):
                total = self.pair[step, near].astype(F32)
                for place in near_steps:
                    total = total + self.near[place - 1, step].astype(F32)
                self.pair[step, near] = total.astype(BF16)
                return carry

            lax.fori_loop(0, outer, block, 0)
            for step in far_steps:
                self.far_copy(step).start()

        def collect(self):
            total = self.pair[far, near].astype(F32)
            if self.far_first:
                for step in near_steps:
                    self.near_copy(step).arrive()
                    total = total + self.near[step - 1].astype(F32)
            else:
                for step in far_steps:
                    self.far_copy(step).arrive()
                    total = total + self.far[step - 1].astype(F32)
            self.done[core] = total
            self.done_copy().start()

        def end(self):
            self.done_copy().arrive()

    early = Sum("early", 1)
    late = Sum("late", 1)
    vector_sum = Sum("vector", 2)
    column_sum = Sum("column", 1)
    last_sum = Sum("last", 2)
    step_sum = Sum("step", 2)
    gathers = {name: Gather(name) for name in PARTS}
    sums = {name: Reduce(name) for name in PARTS}
    shards = {name: getattr(r, name + "_weight") for name in MATRICES}

    def my_rows(shard):
        half = shard.shape[0] // 2
        return shard[pl.ds(pl.multiple_of(core * half, half), half), :]

    def place(name):
        for part, mine in zip(PARTS_OF[name], in_parts(name, my_rows(shards[name]))):
            gathers[part].place(mine)

    place(ATTEND)
    gathers[LOW].begin()
    gathers[LOW].near_start(0)
    gathers[HIGH].begin()
    place(EXPAND)
    for part in NEAR_FIRST:
        gathers[part].near_start(0)
    gathers[HIGH].near_start(0)


    columns_of = {name: getattr(r, name + "_columns").shape[1] * outer * GROUP for name in MATRICES}
    late_at = late_places(columns_of, width)
    column_at = column_places(columns_of, width)

    def early_value():
        thin = r.vectors_own.shape[1]
        r.packed[...] = jnp.zeros_like(r.packed)
        r.packed[0:6, 0:thin] = r.vectors_own[...]
        vectors = pltpu.roll(r.packed[0:8, :], chip * thin, 1)
        r.packed[0:8, :] = vectors
        for at, name in enumerate(MATRICES):
            lanes = slice(at * 128, at * 128 + 128)
            shard = shards[name][...]
            r.packed[SQUARES : SQUARES + 1, lanes] = fold_lanes(
                jnp.sum(fold_rows(shard * shard), axis=0, keepdims=True)
            )
            total = jnp.sum(getattr(r, name + "_rows")[...], axis=1, keepdims=True)
            first_lane = lax.broadcasted_iota(jnp.int32, (1, 128), 1) == 0
            r.packed[ROW_SUMS : ROW_SUMS + 1, lanes] = jnp.where(first_lane, total, 0.0)
        return r.packed[0:EARLY_ROWS, :]

    def late_value():
        thin = r.vectors_own.shape[1]
        r.packed[...] = jnp.zeros_like(r.packed)
        r.packed[0:6, 0:thin] = r.moments_own[...]
        for name in (MERGER, SHRINK):
            row, _ = late_at[name]
            r.packed[row : row + 1, 0:thin] = getattr(r, name + "_columns")[...]
        r.packed[0:8, :] = pltpu.roll(r.packed[0:8, :], chip * thin, 1)
        for name in (ATTEND, EXPAND):
            own = getattr(r, name + "_columns")
            size = own.shape[1]
            r.spread[...] = jnp.zeros_like(r.spread)
            r.spread[0:1, 0:size] = own[...]
            whole = pltpu.roll(r.spread[:, : columns_of[name]], chip * size, 1)[0:1, :]
            split_into(r.packed, late_at[name][0], whole, width)
        return r.packed[...]


    place(MERGER)
    place(SHRINK)
    early.begin(early_value())
    load_tokens.wait()
    prepare(r)
    gathers[LOW].turn()
    later = [part for part in PARTS[2:] if part not in NEAR_FIRST]
    for part in later:
        gathers[part].begin()
    gathers[HIGH].turn()
    early.turn()
    for part in later:
        gathers[part].near_start(0)
    for part in NEAR_FIRST:
        gathers[part].turn()
    gathers[LOW].pass_on()
    gathers[LOW].end()
    project(r, 0)
    gathers[MERGER].turn()
    attend_forward(r, 0, 2, ())
    gathers[HIGH].pass_on()
    gathers[EXPAND_A].turn()
    gathers[HIGH].end()
    project(r, 1)
    gathers[SHRINK_A].turn()
    gathers[SHRINK_B].turn()
    attend_forward(r, 2, 4, ())
    gathers[MERGER].pass_on()
    early_all = early.end()
    r.early[...] = early_all
    r.vectors[...] = early_all.astype(BF16).astype(F32)
    gathers[EXPAND_A].pass_on()
    gathers[MERGER].end()
    gathers[EXPAND_B].pass_on()
    gathers[EXPAND_A].end()
    gathers[EXPAND_B].end()
    first_half(r)
    late.begin(late_value())
    load_cotangent.wait()
    gathers[SHRINK_A].pass_on()
    gathers[SHRINK_B].pass_on()
    gathers[SHRINK_A].end()
    gathers[SHRINK_B].end()
    second_half(r)
    store_result = local(r.result, r.result_out, 0)
    store_result.start()


    shrink_gradient(r, 0)
    sums[SHRINK_A].begin()
    shrink_gradient(r, 1)
    sums[SHRINK_B].begin()
    sums[SHRINK_A].turn()
    late.turn()
    way_back(r, sums[SHRINK_B].turn)
    expand_gradient(r, 0)
    sums[EXPAND_A].begin()
    expand_gradient(r, 1)
    sums[EXPAND_B].begin()
    vector_sum.begin(vector_total(r))
    merger_gradient(r)
    sums[MERGER].begin()
    sums[EXPAND_A].turn()

    def hook_one():
        sums[EXPAND_B].turn()
        sums[MERGER].turn()

    def hook_three():
        sums[LOW].turn()
        vector_sum.turn()
        sums[SHRINK_A].pass_on()

    pairs = width // 128
    attend_backward(r, 0, pairs // 2, ((1, hook_one),))
    attend_gradient(r, 0)
    sums[LOW].begin()
    attend_backward(r, pairs // 2, pairs, ((pairs // 2 + 1, hook_three),))
    attend_gradient(r, 1)
    sums[HIGH].begin()
    sums[SHRINK_B].pass_on()
    sums[HIGH].turn()
    sums[MERGER].pass_on()
    input_gradient(r)
    store_input = local(r.straight, r.input_out, 1)
    store_input.start()
    sums[EXPAND_A].pass_on()
    r.late[...] = late.end()
    r.vector_out[...] = vector_sum.end()
    sums[LOW].pass_on()


    def keep(name, whole):
        getattr(r, "out_" + name)[...] = whole
        squares = jnp.sum(whole * whole, axis=0, keepdims=True)
        split_into(r.packed, column_at[name][0], squares, width)

    sums[SHRINK_A].collect()
    sums[EXPAND_B].pass_on()
    sums[MERGER].collect()
    sums[SHRINK_B].collect()
    sums[LOW].collect()
    sums[HIGH].pass_on()
    sums[EXPAND_A].collect()
    sums[EXPAND_B].collect()
    r.packed[...] = jnp.zeros_like(r.packed)
    for name in (SHRINK, EXPAND, MERGER):
        for part in PARTS_OF[name]:
            sums[part].end()
        done = [flat(getattr(r, "done_" + part)[...]) for part in PARTS_OF[name]]
        if name == SHRINK:
            done = [value.T for value in done]
        keep(name, jnp.concatenate(done, axis=1))
    column_sum.begin(r.packed[0:COLUMN_ROWS, :])
    sums[HIGH].collect()
    attend_half = heads_together([getattr(r, "done_" + name)[core] for name in (LOW, HIGH)])
    squares = jnp.sum(attend_half * attend_half, axis=0, keepdims=True)
    split_into(r.packed, 0, squares, width)
    last_sum.begin(r.packed[0:COLUMN_ROWS, :])
    column_sum.turn()
    sums[LOW].end()
    sums[HIGH].end()
    r.out_attend[...] = heads_together([flat(getattr(r, "done_" + name)[...]) for name in (LOW, HIGH)])
    r.column_out[0:COLUMN_ROWS, :] = column_sum.end()
    last_sum.turn()
    r.early_out[...] = r.early[...]
    r.late_out[...] = r.late[...]
    r.column_out[COLUMN_ROWS : 2 * COLUMN_ROWS, :] = last_sum.end()
    facts = Statistics(r, layout_sizes, r.column_out, r.vector_out[...])

    def my_half(value):
        half = value.shape[0] // 2
        return jnp.where(core == 0, value[:half], value[half:])

    rows = []
    for name in MATRICES:
        rows_old = getattr(r, name + "_rows")[...]
        step = facts.factored(
            name, my_rows(getattr(r, "out_" + name)), my_half(column_of(rows_old)), float(rows_old.shape[1] * outer * GROUP)
        )[3]
        rows.append(fold_lanes(jnp.sum(step * step, axis=0, keepdims=True)))
    step_sum.begin(jnp.concatenate(rows + [jnp.zeros((4, 128), F32)], axis=0))
    step_sum.turn()
    r.step_out[...] = step_sum.end()


    for copy in started.values():
        copy.leave()
    store_result.wait()
    store_input.wait()


def update_kernel(layout_sizes, names, *refs):
    outer, width, wide = layout_sizes
    r = Refs(names, refs)
    chip = lax.axis_index(FSDP)
    into = [
        pltpu.make_async_copy(r.result_in, r.result, r.sems.at[0]),
        pltpu.make_async_copy(r.input_in, r.straight, r.sems.at[1]),
    ]
    out_of = [
        pltpu.make_async_copy(r.result, r.block_output, r.sems.at[2]),
        pltpu.make_async_copy(r.straight, r.input_gradient, r.sems.at[3]),
    ]
    for copy in into:
        copy.start()
    vector_gradient = r.vector_sum[...]
    facts = Statistics(r, layout_sizes, r.column_sum, vector_gradient)
    r.global_norm[...] = facts.norm
    for coming, going in zip(into, out_of):
        coming.wait()
        going.start()
    for name in MATRICES:
        weight = getattr(r, name + "_weight")[...]
        rows_all = float(weight.shape[0] * outer * GROUP)
        count = rows_all * weight.shape[1]
        clipped, new_rows, new_columns, step = facts.factored(
            name, getattr(r, name + "_sum")[...], column_of(getattr(r, name + "_rows")[...]), rows_all
        )
        at = MATRICES.index(name)
        step_square = jnp.sum(r.step_sum[at : at + 1, :], axis=1, keepdims=True)
        weight_square = facts.lanes(SQUARES, name)
        shrunk = jnp.maximum(1.0, jnp.sqrt(step_square * (1.0 / count)) * (1.0 / UPDATE_LIMIT))
        stride = LEARN_RATE * jnp.maximum(0.001, jnp.sqrt(weight_square * (1.0 / count)))
        updated = weight - (stride / shrunk) * step
        getattr(r, name + "_gradient")[...] = clipped
        getattr(r, name + "_updated")[...] = updated
        getattr(r, name + "_bfloat")[...] = updated.astype(BF16)
        getattr(r, name + "_newrows")[...] = row_of(new_rows)
        size = getattr(r, name + "_newcols").shape[1]
        wide_row = jnp.broadcast_to(new_columns, (8, new_columns.shape[1]))
        whole = new_columns.shape[1]
        own = pltpu.roll(wide_row, lax.rem(whole - chip * size, whole), 1)
        getattr(r, name + "_newcols")[...] = own[0:1, 0:size]
    vectors = r.early[...]
    clipped, variance, step = vector_steps(
        vector_gradient, r.late[0:8, :], facts.clip
    )
    shrunk = jnp.maximum(1.0, jnp.sqrt(lane_mean(step * step)) * (1.0 / UPDATE_LIMIT))
    stride = LEARN_RATE * jnp.maximum(0.001, jnp.sqrt(lane_mean(vectors * vectors)))
    updated = vectors - stride * (step / shrunk)
    thin = r.vector_updated.shape[1]
    turn = lax.rem(width - chip * thin, width)
    for ref, value in (
        (r.vector_gradient, clipped),
        (r.vector_variance, variance),
        (r.vector_updated, updated),
    ):
        ref[...] = pltpu.roll(value, turn, 1)[0:6, 0:thin]
    for copy in out_of:
        copy.wait()


def in_vmem():
    return pl.BlockSpec(memory_space=pltpu.VMEM)


def anywhere():
    return pl.BlockSpec(memory_space=pl.ANY)


def call(kernel, sizes, inputs, outputs, scratch, held, params, name):
    names = list(inputs) + list(outputs) + list(scratch)
    results = pl.pallas_call(
        functools.partial(kernel, sizes, names),
        in_specs=[anywhere() if key in held else in_vmem() for key in inputs],
        out_specs=[anywhere() if key in held else in_vmem() for key in outputs],
        out_shape=list(outputs.values()),
        scratch_shapes=list(scratch.values()),
        compiler_params=params,
        name=name,
    )(*inputs.values())
    return dict(zip(outputs, results, strict=True))


def add_part(scratch, outer, name, held, half):
    far_first = name in FAR_FIRST
    near_block = half if far_first else (outer,) + half
    far_block = (GROUP,) + half if far_first else half
    scratch[name] = pltpu.VMEM((outer, GROUP, 2) + held, BF16)
    scratch["g_" + name] = pltpu.VMEM((outer, GROUP, 2) + half, BF16)
    scratch["pair_" + name] = pltpu.VMEM((outer, GROUP) + half, BF16)
    scratch["near_" + name] = pltpu.VMEM((GROUP - 1,) + near_block, BF16)
    scratch["far_" + name] = pltpu.VMEM((max(1, outer - 1),) + far_block, BF16)
    scratch["done_" + name] = pltpu.VMEM((2,) + half, F32)
    for way in ("_sends", "_receives"):
        scratch[name + way] = pltpu.SemaphoreType.DMA((GROUP * outer + GROUP,))
        scratch["sum_" + name + way] = pltpu.SemaphoreType.DMA((GROUP + outer + 1,))


def staged_shards(devices, tokens, lengths, weights, vectors, rows, columns, moments, cotangent):
    outer = devices // GROUP
    slots, width = tokens.shape[1:]
    wide = weights[EXPAND].shape[1]
    sizes = (outer, width, wide)
    shape = jax.ShapeDtypeStruct
    row_in = {name + "_rows": rows[name].reshape(1, -1) for name in MATRICES}
    column_in = {name + "_columns": columns[name].reshape(1, -1) for name in MATRICES}
    weight_in = {name + "_weight": weights[name] for name in MATRICES}
    inputs = dict(
        tokens_in=tokens[0], lengths=lengths, cotangent_in=cotangent[0],
        vectors_own=vectors, moments_own=moments, **weight_in, **row_in, **column_in,
    )
    outputs = dict(
        result_out=shape((slots, width), BF16),
        input_out=shape((slots, width), F32),
        vector_out=shape((8, width), F32),
        early_out=shape((EARLY_ROWS, width), F32),
        late_out=shape((LATE_ROWS, width), F32),
        column_out=shape((2 * COLUMN_ROWS, width), F32),
        step_out=shape((8, 128), F32),
        **{"out_" + name: shape(weights[name].shape, F32) for name in MATRICES},
    )
    scratch = row_scratch(slots, width, wide)
    scratch.update(
        tokens=pltpu.VMEM((slots, width), BF16),
        cotangent=pltpu.VMEM((slots, width), BF16),
        straight=pltpu.VMEM((slots, width), F32),
        vectors=pltpu.VMEM((8, width), F32),
        early=pltpu.VMEM((EARLY_ROWS, width), F32),
        late=pltpu.VMEM((LATE_ROWS, width), F32),
        packed=pltpu.VMEM((LATE_ROWS, width), F32),
        spread=pltpu.VMEM((8, wide), F32),
        local_sems=pltpu.SemaphoreType.DMA((2,)),
    )
    for name, cores, size in (
        ("early", 1, (EARLY_ROWS, width)),
        ("late", 1, (LATE_ROWS, width)),
        ("vector", 2, (8, width)),
        ("column", 1, (COLUMN_ROWS, width)),
        ("last", 2, (COLUMN_ROWS, width)),
        ("step", 2, (8, 128)),
    ):
        scratch[name + "_near"] = pltpu.VMEM((cores, GROUP) + size, F32)
        scratch[name + "_far"] = pltpu.VMEM((outer,) + size, F32)
        for way in ("_sends", "_receives"):
            scratch[name + way] = pltpu.SemaphoreType.DMA((2 * GROUP + outer,))
    for of in MATRICES:
        for name in PARTS_OF[of]:
            rows, all_columns = weights[of].shape
            wide_now = all_columns // len(PARTS_OF[of])
            held = (rows // 2, wide_now)
            half = (wide_now // 2, rows) if of == SHRINK else held
            add_part(scratch, outer, name, held, half)
    got = call(
        shard_kernel, sizes, inputs, outputs, scratch,
        ("tokens_in", "cotangent_in", "result_out", "input_out"),
        pltpu.CompilerParams(
            collective_id=1, has_side_effects=True, vmem_limit_bytes=VMEM_LIMIT
        ),
        "row_and_sums",
    )
    inputs = dict(
        result_in=got["result_out"], input_in=got["input_out"], vector_sum=got["vector_out"],
        early=got["early_out"], late=got["late_out"], column_sum=got["column_out"], step_sum=got["step_out"],
        **{name + "_sum": got["out_" + name] for name in MATRICES},
        **weight_in, **row_in, **column_in,
    )
    outputs = dict(
        block_output=shape((slots, width), BF16),
        input_gradient=shape((slots, width), F32),
        global_norm=shape((1, 1), F32),
    )
    for name in MATRICES:
        outputs[name + "_gradient"] = shape(weights[name].shape, F32)
        outputs[name + "_newrows"] = shape(row_in[name + "_rows"].shape, F32)
        outputs[name + "_newcols"] = shape(column_in[name + "_columns"].shape, F32)
        outputs[name + "_updated"] = shape(weights[name].shape, F32)
        outputs[name + "_bfloat"] = shape(weights[name].shape, BF16)
    for name in ("vector_gradient", "vector_variance", "vector_updated"):
        outputs[name] = shape(vectors.shape, F32)
    out = call(
        update_kernel, sizes, inputs, outputs,
        dict(
            sems=pltpu.SemaphoreType.DMA((4,)),
            result=pltpu.VMEM((slots, width), BF16),
            straight=pltpu.VMEM((slots, width), F32),
        ),
        ("result_in", "input_in", "block_output", "input_gradient"),
        pltpu.CompilerParams(vmem_limit_bytes=VMEM_LIMIT),
        "update",
    )
    out["block_output"] = out["block_output"][None]
    out["input_gradient"] = out["input_gradient"][None]
    out["global_norm"] = out["global_norm"].reshape(())
    for name in MATRICES:
        for kind in ("_newrows", "_newcols"):
            out[name + kind] = out[name + kind].reshape(-1)
    return tuple(out.values())


def tiled_gradient(into, left, right):
    def tile(step, carry):
        columns = aligned(step * 2 * TILE, 2 * TILE)
        into[:, columns] = dot_nn(left[...], right[:, columns]).astype(into.dtype)
        return carry

    lax.fori_loop(0, into.shape[1] // (2 * TILE), tile, 0)


def row_kernel(names, *refs):
    r = Refs(names, refs)
    r.attend = (r.attend_low, r.attend_high)
    r.expand, r.shrink = (r.expand,), (r.shrink,)
    r.g_attend = (r.g_attend_low, r.g_attend_high)
    pairs = r.tokens.shape[1] // 128
    steps = (
        functools.partial(prepare, r),
        functools.partial(project, r, 0),
        functools.partial(project, r, 1),
        functools.partial(attend_forward, r, 0, pairs, ()),
        functools.partial(first_half, r),
        functools.partial(second_half, r),
        functools.partial(tiled_gradient, r.g_shrink, r.d_second_t, r.active),
        functools.partial(way_back, r),
        functools.partial(tiled_gradient, r.g_expand, r.first_t, r.d_hidden),
        functools.partial(tiled_gradient, r.g_merger, r.context_t, r.d_branch),
        functools.partial(attend_backward, r, 0, pairs, ()),
        functools.partial(attend_gradient, r, 0),
        functools.partial(attend_gradient, r, 1),
        functools.partial(input_gradient, r),
    )
    for step in steps:
        pl.when(lax.axis_index(FSDP) >= 0)(step)
    r.g_vectors[...] = vector_total(r)


def plain_shards(devices, tokens, lengths, weights, vectors, rows, columns, moments, cotangent):
    slots, width = tokens.shape[1:]
    wide = weights[EXPAND].shape[1]
    shape = jax.ShapeDtypeStruct
    whole = {
        name: lax.all_gather(weights[name].astype(BF16), FSDP, axis=0, tiled=True)
        for name in MATRICES
    }
    vector_rows = lax.all_gather(vectors.astype(BF16), FSDP, axis=1, tiled=True).astype(F32)
    vector_rows = jnp.concatenate([vector_rows, jnp.zeros((2, width), F32)], axis=0)
    whole["attend_low"], whole["attend_high"] = heads_apart(whole.pop(ATTEND))
    inputs = dict(
        tokens=tokens[0], lengths=lengths, cotangent=cotangent[0], vectors=vector_rows, **whole
    )
    outputs = dict(
        result=shape((slots, width), BF16),
        straight=shape((slots, width), F32),
        g_vectors=shape((8, width), F32),
        g_attend_low=shape((width, 3 * width // 2), BF16),
        g_attend_high=shape((width, 3 * width // 2), BF16),
        g_merger=shape((width, width), BF16),
        g_expand=shape((width, wide), BF16),
        g_shrink=shape((width, wide), BF16),
    )
    scratch = row_scratch(slots, width, wide)
    scratch["d_branch"] = pltpu.VMEM((slots, width), BF16)
    names = list(inputs) + list(outputs) + list(scratch)
    got = pl.pallas_call(
        functools.partial(row_kernel, names),
        in_specs=[in_vmem()] * len(inputs),
        out_specs=[in_vmem()] * len(outputs),
        out_shape=list(outputs.values()),
        scratch_shapes=list(scratch.values()),
        compiler_params=pltpu.CompilerParams(vmem_limit_bytes=VMEM_LIMIT),
        name="row",
    )(*inputs.values())
    got = dict(zip(outputs, got, strict=True))
    got["g_" + ATTEND] = heads_together((got["g_attend_low"], got["g_attend_high"]))
    grads = []
    for name in MATRICES:
        value = lax.psum(got["g_" + name], DP).astype(F32)
        if name == SHRINK:
            grads.append(lax.psum_scatter(value.T, FSDP, scatter_dimension=0, tiled=True))
        else:
            grads.append(lax.psum_scatter(value, FSDP, scatter_dimension=0, tiled=True))
    vector_all = lax.psum(got["g_vectors"][:6], (DP, FSDP))
    index = lax.axis_index(FSDP)

    def spread(own, dim):
        size = own.shape[dim]
        extent = own.shape[:dim] + (size * devices,) + own.shape[dim + 1 :]
        return lax.dynamic_update_slice_in_dim(
            jnp.zeros(extent, F32), own, index * size, dim
        )

    early = (
        [spread(columns[name], 0) for name in MATRICES],
        [jnp.sum(weights[name] * weights[name]) for name in MATRICES],
        [jnp.sum(rows[name]) for name in MATRICES],
        [jnp.sum(grad * grad, axis=0) for grad in grads],
        jnp.sum(vectors * vectors, axis=1),
    )
    old_columns, weight_squares, row_sums, columns_now, vector_squares = lax.psum(early, FSDP)
    squares = [jnp.sum(value) for value in columns_now]
    total = jnp.sum(vector_all * vector_all)
    for value in squares:
        total = total + value
    norm = jnp.sqrt(total)
    clip = jnp.minimum(1.0, THRESHOLD / norm)
    power = clip * clip
    pieces = []
    for at, name in enumerate(MATRICES):
        grad = grads[at]
        rows_all = float(grad.shape[0] * devices)
        count = rows_all * grad.shape[1]
        new_rows = FORGET * rows[name] + (1.0 - FORGET) * (
            power * jnp.mean(grad * grad, axis=1) + TINY_VALUE
        )
        new_columns = FORGET * old_columns[at] + (1.0 - FORGET) * (
            power * columns_now[at] / rows_all + TINY_VALUE
        )
        mean = FORGET * row_sums[at] / rows_all + (1.0 - FORGET) * (
            power * squares[at] / count + TINY_VALUE
        )
        clipped = clip * grad
        step = clipped * lax.rsqrt(new_rows[:, None] * new_columns[None, :] / mean)
        pieces.append((clipped, new_rows, new_columns, step, count))
    thin = vectors.shape[1]
    vector_clipped = clip * lax.dynamic_slice_in_dim(vector_all, index * thin, thin, 1)
    variance = FORGET * moments + (1.0 - FORGET) * (vector_clipped * vector_clipped + TINY_VALUE)
    vector_step = vector_clipped * lax.rsqrt(variance)
    step_squares, vector_step_squares = lax.psum(
        (
            [jnp.sum(piece[3] * piece[3]) for piece in pieces],
            jnp.sum(vector_step * vector_step, axis=1),
        ),
        FSDP,
    )
    results = [got["result"][None], got["straight"][None], norm]
    for at, name in enumerate(MATRICES):
        clipped, new_rows, new_columns, step, count = pieces[at]
        shrunk = jnp.maximum(1.0, jnp.sqrt(step_squares[at] / count) / UPDATE_LIMIT)
        stride = LEARN_RATE * jnp.maximum(0.001, jnp.sqrt(weight_squares[at] / count))
        updated = weights[name] - stride * (step / shrunk)
        size = columns[name].shape[0]
        own = lax.dynamic_slice_in_dim(new_columns, index * size, size, 0)
        results.extend([clipped, new_rows, own, updated, updated.astype(BF16)])
    extent = float(width)
    shrunk = jnp.maximum(1.0, jnp.sqrt(vector_step_squares / extent) / UPDATE_LIMIT)[:, None]
    stride = LEARN_RATE * jnp.maximum(0.001, jnp.sqrt(vector_squares / extent))[:, None]
    results.extend([vector_clipped, variance, vectors - stride * (vector_step / shrunk)])
    return tuple(results)


def shards(
    devices,
    tokens,
    lengths,
    attend_weight,
    merger_weight,
    expand_weight,
    shrink_weight,
    vectors,
    attend_rows,
    attend_columns,
    merger_rows,
    merger_columns,
    expand_rows,
    expand_columns,
    shrink_rows,
    shrink_columns,
    vector_moments,
    cotangent,
):
    weights = dict(
        attend=attend_weight, merger=merger_weight, expand=expand_weight, shrink=shrink_weight
    )
    rows = dict(attend=attend_rows, merger=merger_rows, expand=expand_rows, shrink=shrink_rows)
    columns = dict(
        attend=attend_columns, merger=merger_columns, expand=expand_columns, shrink=shrink_columns
    )
    assert tokens.shape[0] == 1
    fits = devices % GROUP == 0 and all(
        weight.shape[0] % 32 == 0 for weight in weights.values()
    ) and shrink_weight.shape[0] % 128 == 0
    body = staged_shards if fits else plain_shards
    return body(
        devices, tokens, lengths, weights, vectors, rows, columns, vector_moments, cotangent
    )


def solution(mesh):
    split = P(FSDP, None)
    row = P((DP, FSDP), None, None)
    one = P(FSDP)
    thin = P(None, FSDP)
    in_specs = (
        (row, P((DP, FSDP), None)) + (split,) * 4 + (thin,) + (one,) * 8 + (thin, row)
    )
    out_specs = (row, row, P()) + (split, one, one, split, split) * 4 + (thin,) * 3
    return jax.shard_map(
        functools.partial(shards, mesh.shape[FSDP]),
        mesh=mesh, in_specs=in_specs, out_specs=out_specs, check_vma=False,
    )
```

```python
import functools

import jax
import jax.numpy as jnp
from jax import lax
from jax.experimental import pallas as pl
from jax.experimental.pallas import tpu as pltpu
from jax.sharding import PartitionSpec as P

F32 = jnp.float32
BF16 = jnp.bfloat16
HEAD_DIM = 64
STEP = 3
EPSILON = 1e-05
TINY_VALUE = 1e-30
NEGATIVE = -1e30
THRESHOLD = 1.0
UPDATE_LIMIT = 1.0
LEARN_RATE = 0.5
FORGET = 1.0 - float(STEP) ** (-0.8)
LOG2_E = 1.4426950408889634
GELU_A = 0.7978845608028654
GELU_B = 0.044715 * GELU_A

REACH = 256
QUERY_BLOCK = 128
TILE = 256
GROUP = 4
DP, FSDP = "dp", "fsdp"
ATTEND, MERGER, EXPAND, SHRINK = "attend", "merger", "expand", "shrink"
MATRICES = (ATTEND, MERGER, EXPAND, SHRINK)
MESH = pl.DeviceIdType.MESH
VMEM_LIMIT = 63 << 20


def dot_general(left, right, left_dim, right_dim):
    return lax.dot_general(
        left, right, (((left_dim,), (right_dim,)), ((), ())), preferred_element_type=F32
    )


def dot_nn(left, right):
    return dot_general(left, right, 1, 0)


def dot_nt(left, right):
    return dot_general(left, right, 1, 1)


def dot_tn(left, right):
    return dot_general(left, right, 0, 0)


def flat(value):
    return value.reshape(-1, value.shape[-1])


def whole(parts):
    return jnp.concatenate([flat(part[...]) for part in parts], axis=1)


def fold_rows(value):
    return jnp.sum(value.reshape(value.shape[0] // 8, 8, value.shape[1]), axis=0)


def fold_lanes(row):
    total = row[:, :128]
    for start in range(128, row.shape[1], 128):
        total = total + row[:, start : start + 128]
    return total


def diagonal(size):
    return lax.broadcasted_iota(jnp.int32, (size, size), 0) == lax.broadcasted_iota(
        jnp.int32, (size, size), 1
    )


def column_of(row):
    size = row.shape[1]
    return jnp.sum(jnp.where(diagonal(size), row, 0.0), axis=1, keepdims=True)


def row_of(column):
    size = column.shape[0]
    return jnp.sum(jnp.where(diagonal(size), column, 0.0), axis=0, keepdims=True)


def lane_mean(value):
    return jnp.mean(value, axis=-1, keepdims=True)


def aligned(start, size):
    return pl.ds(pl.multiple_of(start, size), size)


def band(slots):
    pieces = []
    place = 0
    for first in range(0, slots, QUERY_BLOCK):
        low = max(0, first - REACH)
        high = first + QUERY_BLOCK
        pieces.append((first, low, high, place))
        place += high - low
    return pieces, place


def prepare(r):
    slots = r.tokens.shape[0]
    count = r.lengths.shape[1]
    for start in range(0, slots, TILE):
        r.tokens_t[:, start : start + TILE] = r.tokens[start : start + TILE, :].T
    lengths = r.lengths[...].astype(F32)
    rows = jnp.broadcast_to(lengths, (8, count)).astype(BF16)
    upto = lax.broadcasted_iota(jnp.int32, (count, count), 1) <= lax.broadcasted_iota(
        jnp.int32, (count, count), 0
    )
    ends = dot_nt(jnp.where(upto, 1.0, 0.0).astype(BF16), rows)[:, 0:1]
    places = lax.broadcasted_iota(jnp.int32, (count, slots), 1).astype(F32)
    ended = jnp.where(ends <= places, 1.0, 0.0).astype(BF16)
    begin = dot_nn(rows, ended)[0:1, :]
    total = jnp.sum(lengths, axis=1, keepdims=True)
    r.total[...] = jnp.broadcast_to(total, r.total.shape)
    slot = lax.broadcasted_iota(jnp.int32, (1, slots), 1).astype(F32)
    begin = jnp.where(slot < total, begin, slot)
    for first, low, high, place in band(slots)[0]:
        key = (lax.broadcasted_iota(jnp.int32, (high - low, QUERY_BLOCK), 0) + low).astype(F32)
        query = slot[:, first : first + QUERY_BLOCK]
        fits = (key >= begin[:, first : first + QUERY_BLOCK]) & (key <= query)
        r.mask[place : place + high - low, :] = jnp.where(fits, 1.0, 0.0).astype(BF16)


def project(r, part):
    width = r.tokens.shape[1]
    half = width // 2
    columns = flat(r.attend[part][...])
    for at in range(3):
        rows = slice(at * width + part * half, at * width + (part + 1) * half)
        value = dot_tn(columns[:, at * half : (at + 1) * half], r.tokens_t[...]).astype(BF16)
        r.projected_t[rows, :] = value
    for at in range(2):
        start = at * width + part * half
        r.key_value[:, start : start + half] = r.projected_t[
            width + start : width + start + half, :
        ].T


def beside_zeros(value, head):
    zeros = jnp.zeros_like(value)
    return jnp.concatenate([value, zeros] if head == 0 else [zeros, value], axis=0)


def head_rows(part, width, pair, head):
    return pl.ds(pl.multiple_of(part * width + pair * 128 + HEAD_DIM * head, HEAD_DIM), HEAD_DIM)


def by_pairs(first, last, hooks, body):
    def pair(step, carry):
        for at, hook in hooks:
            pl.when(step == at)(hook)
        body(step)
        return carry

    lax.fori_loop(first, last, pair, 0)


def attend_forward(r, first_pair, last_pair, hooks):
    slots, width = r.tokens.shape
    factor = HEAD_DIM ** -0.5 * LOG2_E
    items = [(head,) + piece for head in (0, 1) for piece in band(slots)[0]]

    def body(pair):
        lanes = pl.ds(pl.multiple_of(pair * 128, 128), 128)

        def scores_of(item):
            head, first, low, high, _ = item
            queries = r.projected_t[head_rows(0, width, pair, head), first : first + QUERY_BLOCK]
            return dot_nn(r.key_value[low:high, lanes], beside_zeros(queries, head))

        def probs_of(item, scores):
            head, _, low, high, place = item
            fits = r.mask[place : place + high - low, :].astype(F32) > 0.5
            scores = jnp.where(fits, scores * factor, NEGATIVE)
            weights = jnp.exp2(scores - jnp.max(scores, axis=0, keepdims=True))
            inverse = 1.0 / jnp.sum(weights, axis=0, keepdims=True)
            probs = (weights * inverse).astype(BF16)
            r.probs[2 * pair + head, place : place + high - low, :] = probs
            return probs

        def put_context(item, probs):
            head, first, low, high, _ = item
            values = r.projected_t[head_rows(2, width, pair, head), low:high]
            r.context_t[head_rows(0, width, pair, head), first : first + QUERY_BLOCK] = dot_nn(
                values, probs
            ).astype(BF16)

        scores = [scores_of(item) for item in items]
        probs = [probs_of(item, value) for item, value in zip(items, scores)]
        for item, value in zip(items, probs):
            put_context(item, value)

    by_pairs(first_pair, last_pair, hooks, body)


def attend_backward(r, first_pair, last_pair, hooks):
    slots, width = r.tokens.shape
    scale = HEAD_DIM ** -0.5
    pieces = band(slots)[0]
    count = len(pieces)
    items = [(head, at) for head in (0, 1) for at in range(count)]

    def body(pair):
        lanes = pl.ds(pl.multiple_of(width + pair * 128, 128), 128)
        queries = [r.projected_t[head_rows(0, width, pair, head), :] for head in (0, 1)]
        keys_t = [r.projected_t[head_rows(1, width, pair, head), :] for head in (0, 1)]
        upstream = [r.d_context_t[head_rows(0, width, pair, head), :] for head in (0, 1)]

        def probs_of(item):
            _, low, high, place = pieces[item[1]]
            return r.probs[2 * pair + item[0], place : place + high - low, :]

        def d_probs_of(item):
            first, low, high, _ = pieces[item[1]]
            arriving = upstream[item[0]][:, first : first + QUERY_BLOCK]
            return dot_nn(r.key_value[low:high, lanes], beside_zeros(arriving, item[0]))

        def d_scores_of(item, d_probs):
            wide = probs_of(item).astype(F32)
            inner = jnp.sum(wide * d_probs, axis=0, keepdims=True)
            return (wide * (d_probs - inner)).astype(BF16)

        def put_queries(item, d_scores):
            first, low, high, _ = pieces[item[1]]
            value = dot_nn(keys_t[item[0]][:, low:high], d_scores) * scale
            r.projected_t[
                head_rows(0, width, pair, item[0]), first : first + QUERY_BLOCK
            ] = value.astype(BF16)

        def put_keys_and_values(item, known):
            head, at = item
            begin = pieces[at][0]
            seen = [i for i in range(count) if pieces[i][1] <= begin <= pieces[i][0]]
            span = slice(pieces[seen[0]][0], pieces[seen[-1]][0] + QUERY_BLOCK)
            here = slice(begin, begin + QUERY_BLOCK)

            def together(values):
                parts = []
                for i, value in zip(seen, values):
                    start = begin - pieces[i][1]
                    parts.append(value[start : start + QUERY_BLOCK, :])
                return jnp.concatenate(parts, axis=1)

            d_scores = together([known[(head, i)] for i in seen])
            probs = together([probs_of((head, i)) for i in seen])
            r.projected_t[head_rows(1, width, pair, head), here] = (
                dot_nt(queries[head][:, span], d_scores) * scale
            ).astype(BF16)
            r.projected_t[head_rows(2, width, pair, head), here] = dot_nt(
                upstream[head][:, span], probs
            ).astype(BF16)

        d_probs = [d_probs_of(item) for item in items]
        known = {item: d_scores_of(item, value) for item, value in zip(items, d_probs)}
        for item in items:
            put_queries(item, known[item])
        for item in items:
            put_keys_and_values(item, known)

    by_pairs(first_pair, last_pair, hooks, body)


def vector_rows(r):
    return [r.vectors[place : place + 1, :] for place in range(6)]


def token_blocks(r):
    return [slice(start, start + TILE) for start in range(0, r.tokens.shape[0], TILE)]


def keep_sums(r, places, folded):
    for place, parts in zip(places, zip(*folded)):
        r.vector_sums[place] = sum(parts[1:], parts[0])


def first_half(r):
    omega_one, gain_one, shift_one = vector_rows(r)[:3]

    def front(rows):
        inputs = r.tokens[rows, :].astype(F32)
        first_sum = omega_one * inputs + dot_tn(r.context_t[:, rows], flat(r.merger[...]))
        centered = first_sum - lane_mean(first_sum)
        first_inv = lax.rsqrt(lane_mean(centered * centered) + EPSILON)
        first_normed = centered * first_inv
        r.first_inv[rows, :] = jnp.broadcast_to(first_inv, (TILE, 128))
        r.straight[rows, :] = first_normed
        first_low = (first_normed * gain_one + shift_one).astype(BF16)
        r.first_t[:, rows] = first_low.T
        return first_low

    def gelu(rows, hidden):
        square = hidden * hidden
        part = 0.5 + 0.5 * jnp.tanh(hidden * (GELU_A + GELU_B * square))
        active = hidden * part
        r.active[rows, :] = active.astype(BF16)
        slope = part + active * (1.0 - part) * (2 * GELU_A + 6 * GELU_B * square)
        r.d_hidden[rows, :] = slope.astype(BF16)

    blocks = token_blocks(r)
    lows = [front(rows) for rows in blocks]
    for rows, low in zip(blocks, lows):
        gelu(rows, dot_nn(low, whole(r.expand)))


def second_half(r):
    _, gain_one, shift_one, omega_two, gain_two, shift_two = vector_rows(r)

    def rest(rows, product):
        first_out = r.straight[rows, :] * gain_one + shift_one
        second_sum = omega_two * first_out + product
        centered = second_sum - lane_mean(second_sum)
        second_inv = lax.rsqrt(lane_mean(centered * centered) + EPSILON)
        second_normed = centered * second_inv
        arriving = r.cotangent[rows, :].astype(F32)
        r.result[rows, :] = (second_normed * gain_two + shift_two).astype(BF16)
        place = (lax.broadcasted_iota(jnp.int32, (TILE, 1), 0) + rows.start).astype(F32)
        upstream = arriving * jnp.where(place < r.total[0:1, 0:1], 1.0, 0.0)
        scaled = upstream * gain_two
        d_second = second_inv * (
            scaled - lane_mean(scaled) - second_normed * lane_mean(scaled * second_normed)
        )
        r.d_second[rows, :] = d_second
        r.d_second_t[:, rows] = d_second.astype(BF16).T
        return (
            fold_rows(upstream * second_normed),
            fold_rows(upstream),
            fold_rows(first_out * d_second),
        )

    blocks = token_blocks(r)
    products = [dot_nn(r.active[rows, :], whole(r.shrink)) for rows in blocks]
    keep_sums(r, (4, 5, 3), [rest(rows, value) for rows, value in zip(blocks, products)])


def way_back(r, hook=None):
    omega_one, gain_one, _, omega_two = vector_rows(r)[:4]

    def to_hidden(rows):
        d_active = dot_nt(r.d_second[rows, :].astype(BF16), whole(r.shrink))
        d_hidden = (d_active * r.d_hidden[rows, :].astype(F32)).astype(BF16)
        r.d_hidden[rows, :] = d_hidden
        return d_hidden

    def to_branch(rows, product):
        d_first = product + omega_two * r.d_second[rows, :]
        first_normed = r.straight[rows, :]
        scaled = d_first * gain_one
        d_first_sum = r.first_inv[rows, 0:1] * (
            scaled - lane_mean(scaled) - first_normed * lane_mean(scaled * first_normed)
        )
        inputs = r.tokens[rows, :].astype(F32)
        r.straight[rows, :] = omega_one * d_first_sum
        branch_low = d_first_sum.astype(BF16)
        r.d_branch[rows, :] = branch_low
        folded = (
            fold_rows(inputs * d_first_sum),
            fold_rows(d_first * first_normed),
            fold_rows(d_first),
        )
        return branch_low, folded

    blocks = token_blocks(r)
    hidden = [to_hidden(rows) for rows in blocks]
    if hook is not None:
        hook()
    products = [dot_nt(value, whole(r.expand)) for value in hidden]
    got = [to_branch(rows, value) for rows, value in zip(blocks, products)]
    for rows, value in zip(blocks, got):
        r.d_context_t[:, rows] = dot_nt(flat(r.merger[...]), value[0]).astype(BF16)
    keep_sums(r, (0, 1, 2), [value[1] for value in got])


def vector_total(r):
    rows = [jnp.sum(r.vector_sums[place], axis=0, keepdims=True) for place in range(6)]
    return jnp.concatenate(rows + [jnp.zeros((2, rows[0].shape[1]), F32)], axis=0)


def put_tile(ref, columns, value):
    ref[..., columns] = value.astype(ref.dtype).reshape(ref.shape[:-1] + (value.shape[1],))


def shrink_gradient(r, part):
    into = r.g_shrink[part]
    half = r.tokens.shape[1] // 2
    owned = into.shape[-1]
    rows = r.d_second_t[part * half : (part + 1) * half, :]
    value = dot_nn(rows, r.active[...]).astype(BF16)
    for owner in range(value.shape[1] // owned):
        into[owner // GROUP, owner % GROUP] = value[
            :, owner * owned : (owner + 1) * owned
        ].reshape(2, half // 2, owned)


def expand_gradient(r, part):
    half = r.active.shape[1] // 2
    columns = slice(part * half, (part + 1) * half)
    put_tile(r.g_expand[part], slice(None), dot_nn(r.first_t[...], r.d_hidden[:, columns]))


def merger_gradient(r):
    put_tile(r.g_merger, slice(None), dot_nn(r.context_t[...], r.d_branch[...]))


def span_of_heads(r, first, last, slots):
    width = r.tokens.shape[1]
    return jnp.concatenate(
        [r.projected_t[at * width + first : at * width + last, slots] for at in range(3)], axis=0
    )


def attend_gradient(r, into, first, last):
    heads = span_of_heads(r, first, last, slice(None))
    put_tile(into, slice(None), dot_nt(r.tokens_t[...], heads))


def heads_together(parts):
    pieces = []
    for at in range(3):
        for part in parts:
            size = part.shape[1] // 3
            pieces.append(part[:, at * size : (at + 1) * size])
    return jnp.concatenate(pieces, axis=1)


def heads_apart(whole):
    half = whole.shape[1] // 6
    return [
        jnp.concatenate(
            [whole[:, (2 * at + part) * half : (2 * at + part + 1) * half] for at in range(3)],
            axis=1,
        )
        for part in range(2)
    ]


def input_gradient(r):
    blocks = token_blocks(r)
    half = r.tokens.shape[1] // 2
    products = []
    for rows in blocks:
        halves = [
            dot_general(
                span_of_heads(r, part * half, (part + 1) * half, rows),
                flat(r.attend[part][...]), 0, 1,
            )
            for part in range(2)
        ]
        products.append(halves[0] + halves[1])
    for rows, value in zip(blocks, products):
        r.straight[rows, :] += value


def row_scratch(slots, width, wide):
    packed = band(slots)[1]
    heads = width // HEAD_DIM
    return dict(
        tokens_t=pltpu.VMEM((width, slots), BF16),
        mask=pltpu.VMEM((packed, QUERY_BLOCK), BF16),
        total=pltpu.VMEM((8, 128), F32),
        projected_t=pltpu.VMEM((3 * width, slots), BF16),
        key_value=pltpu.VMEM((slots, 2 * width), BF16),
        probs=pltpu.VMEM((heads, packed, QUERY_BLOCK), BF16),
        context_t=pltpu.VMEM((width, slots), BF16),
        d_context_t=pltpu.VMEM((width, slots), BF16),
        active=pltpu.VMEM((slots, wide), BF16),
        d_hidden=pltpu.VMEM((slots, wide), BF16),
        first_t=pltpu.VMEM((width, slots), BF16),
        d_second_t=pltpu.VMEM((width, slots), BF16),
        vector_sums=pltpu.VMEM((6, 8, width), F32),
        first_inv=pltpu.VMEM((slots, 128), F32),
        d_second=pltpu.VMEM((slots, width), F32),
    )


class Refs:
    def __init__(self, names, refs):
        for name, ref in zip(names, refs, strict=True):
            setattr(self, name, ref)


LOW, HIGH = "low", "high"
EXPAND_A, EXPAND_B, SHRINK_A, SHRINK_B = "ea", "eb", "sa", "sb"
PARTS_OF = {
    ATTEND: (LOW, HIGH),
    MERGER: (MERGER,),
    EXPAND: (EXPAND_A, EXPAND_B),
    SHRINK: (SHRINK_A, SHRINK_B),
}
MID, LAST = "mid", "last"
SPANS = {LOW: (0, 2), MID: (2, 3), LAST: (3, 4)}
PARTS = (LOW, HIGH, MERGER, EXPAND_A, EXPAND_B, SHRINK_A, SHRINK_B)
NEAR_FIRST = (SHRINK_B,)
FAR_FIRST = (SHRINK_B, MERGER)


def in_parts(name, value):
    if name == ATTEND:
        return heads_apart(value)
    count = len(PARTS_OF[name])
    size = value.shape[1] // count
    return [value[:, at * size : (at + 1) * size] for at in range(count)]


def packed_rows(first, order, columns_of, width):
    places = {}
    for name in order:
        places[name] = (first, columns_of[name] // width)
        first += columns_of[name] // width
    return places


SQUARES, ROW_SUMS, EARLY_ROWS = 6, 7, 8
LATE_COLUMNS, LATE_ROWS = 6, 16
COLUMN_ROWS, LAST_ROWS = 8, 4
ALL = slice(None)


def late_places(columns_of, width):
    return packed_rows(LATE_COLUMNS, (MERGER, SHRINK, ATTEND, EXPAND), columns_of, width)


def column_places(columns_of, width):
    places = packed_rows(0, (MERGER, EXPAND, SHRINK), columns_of, width)
    places.update(packed_rows(COLUMN_ROWS, (ATTEND,), columns_of, width))
    return places


def joined(ref, start, count):
    return jnp.concatenate([ref[place : place + 1, :] for place in range(start, start + count)], 1)


def split_into(ref, start, row, width):
    for piece in range(row.shape[1] // width):
        ref[start + piece : start + piece + 1, :] = row[:, piece * width : (piece + 1) * width]


def scalar_sum(value):
    return jnp.sum(jnp.sum(value, axis=1, keepdims=True), axis=0, keepdims=True)


def flat_slots(value):
    return value.reshape((-1,) + value.shape[2:])


class Statistics:
    def __init__(self, r, sizes, columns, vector_gradient):
        outer, self.width, _ = sizes
        self.devices = outer * GROUP
        columns_of = {
            name: getattr(r, name + "_columns").shape[1] * self.devices for name in MATRICES
        }
        self.early, self.late, self.columns = r.early, r.late, columns
        self.late_at = late_places(columns_of, self.width)
        self.column_at = column_places(columns_of, self.width)
        self.squares = {
            name: scalar_sum(joined(columns, *self.column_at[name])) for name in MATRICES
        }
        total = scalar_sum(vector_gradient * vector_gradient)
        for name in MATRICES:
            total = total + self.squares[name]
        self.norm = jnp.sqrt(total)
        self.clip = jnp.minimum(1.0, THRESHOLD / self.norm)

    def lanes(self, row, name):
        at = MATRICES.index(name) * 128
        return jnp.sum(self.early[row : row + 1, at : at + 128], axis=1, keepdims=True)

    def factored(self, name, gradient, rows_old, rows_all):
        wide = gradient.shape[1]
        power = self.clip * self.clip
        row_mean = jnp.sum(gradient * gradient, axis=1, keepdims=True) * (1.0 / wide)
        new_rows = FORGET * rows_old + (1.0 - FORGET) * (power * row_mean + TINY_VALUE)
        now = joined(self.columns, *self.column_at[name]) * (1.0 / rows_all)
        new_columns = FORGET * joined(self.late, *self.late_at[name]) + (1.0 - FORGET) * (
            power * now + TINY_VALUE
        )
        mean = FORGET * (self.lanes(ROW_SUMS, name) * (1.0 / rows_all)) + (1.0 - FORGET) * (
            power * (self.squares[name] * (1.0 / (rows_all * wide))) + TINY_VALUE
        )
        clipped = self.clip * gradient
        step = clipped * lax.rsqrt(new_rows * new_columns * (1.0 / mean))
        return clipped, new_rows, new_columns, step


def vector_steps(gradient, moments, clip):
    clipped = clip * gradient
    variance = FORGET * moments + (1.0 - FORGET) * (clipped * clipped + TINY_VALUE)
    return clipped, variance, clipped * lax.rsqrt(variance)


def shard_kernel(layout_sizes, names, *refs):
    outer, width, wide = layout_sizes
    r = Refs(names, refs)
    r.result = r.cotangent
    r.d_branch = r.tokens
    for name in (ATTEND, EXPAND, SHRINK):
        setattr(r, name, [getattr(r, part) for part in PARTS_OF[name]])
    for name in (EXPAND, SHRINK):
        setattr(r, "g_" + name, [getattr(r, "g_" + part) for part in PARTS_OF[name]])
    core = lax.axis_index(DP)
    chip = lax.axis_index(FSDP)
    far = chip // GROUP
    near = lax.rem(chip, GROUP)
    sibling = (1 - core, chip)
    near_steps = range(1, GROUP)
    far_steps = range(1, outer)

    near_places = [near] + [jnp.bitwise_xor(near, step) for step in near_steps]
    far_places = [lax.rem(far + step, outer) for step in range(outer)]
    far_origins = [lax.rem(far + outer - step, outer) for step in range(outer)]
    near_devices = [(core, far * GROUP + place) for place in near_places]
    far_devices = [(core, place * GROUP + near) for place in far_places]
    other = 1 - core
    started = {}
    arrived = set()

    class Copy:
        def __init__(self, key, sems, index, device, source, target, landing=None):
            self.key = key + (index,)
            self.device = device
            self.sems = sems
            self.index = index
            self.source = source
            self.target = target
            self.landing = target if landing is None else landing

        def describe(self, source, target):
            return pltpu.make_async_remote_copy(
                src_ref=source[0].at[source[1]],
                dst_ref=target[0].at[target[1]],
                send_sem=self.sems[0].at[self.index],
                recv_sem=self.sems[1].at[self.index],
                device_id=self.device,
                device_id_type=MESH,
            )

        def start(self):
            self.describe(self.source, self.target).start()
            started[self.key] = self

        def arrive(self):
            self.describe(self.landing, self.landing).wait_recv()
            arrived.add(self.key)

        def leave(self):
            self.describe(self.source, self.target).wait_send()

    def local(source, target, index):
        return pltpu.make_async_copy(source, target, r.local_sems.at[index])

    load_tokens = local(r.tokens_in, r.tokens, 0)
    load_cotangent = local(r.cotangent_in, r.cotangent, 1)
    load_tokens.start()
    load_cotangent.start()

    barrier = pltpu.get_barrier_semaphore()
    for step in near_steps:
        pl.semaphore_signal(barrier, inc=1, device_id=near_devices[step], device_id_type=MESH)
    for step in far_steps:
        pl.semaphore_signal(barrier, inc=1, device_id=far_devices[step], device_id_type=MESH)
    pl.semaphore_signal(barrier, inc=1, device_id=sibling, device_id_type=MESH)
    pl.semaphore_wait(barrier, len(near_steps) + len(far_steps) + 1)


    class Sum:
        def __init__(self, name, cores):
            self.key = (name,)
            self.near = getattr(r, name + "_near")
            self.far = getattr(r, name + "_far")
            self.sems = (getattr(r, name + "_sends"), getattr(r, name + "_receives"))
            self.steps = [(0, step) for step in near_steps]
            if cores == 2:
                self.steps += [(1, step) for step in range(GROUP)]
            self.mine = core if cores == 2 else 0
            self.other = other if cores == 2 else 0

        def near_copy(self, cross, step):
            mine = (self.near, (self.mine, near))
            whose = self.other if cross else self.mine
            device = (other if cross else core, near_devices[step][1])
            return Copy(
                self.key, self.sems, cross * GROUP + step, device, mine, mine,
                (self.near, (whose, near_places[step])),
            )

        def far_copy(self, step):
            mine = (self.far, far)
            return Copy(
                self.key, self.sems, 2 * GROUP + step, far_devices[step], mine, mine,
                (self.far, far_origins[step]),
            )

        def begin(self, value):
            self.near[self.mine, near] = value
            for cross, step in self.steps:
                self.near_copy(cross, step).start()

        def turn(self):
            for cross, step in self.steps:
                self.near_copy(cross, step).arrive()
            self.far[far] = jnp.sum(flat_slots(self.near[...]), axis=0)
            for step in far_steps:
                self.far_copy(step).start()

        def end(self):
            for step in far_steps:
                self.far_copy(step).arrive()
            return jnp.sum(self.far[...], axis=0)


    class Gather:
        def __init__(self, name):
            self.key = (name,)
            self.near_first = name in NEAR_FIRST
            self.held = getattr(r, name)
            self.sems = (getattr(r, name + "_sends"), getattr(r, name + "_receives"))

        def far_copy(self, step):
            block = ALL if self.near_first else near
            mine = (self.held, (far, block, core))
            return Copy(
                self.key, self.sems, step, far_devices[step], mine, mine,
                (self.held, (far_origins[step], block, core)),
            )

        def near_copy(self, step, hop):
            slot = far_origins[hop]
            mine = (self.held, (slot, near, core))
            return Copy(
                self.key, self.sems, step * outer + hop, near_devices[step], mine, mine,
                (self.held, (slot, near_places[step], core)),
            )

        def cross(self, step):
            if self.near_first:
                block = (far_origins[step], ALL)
            else:
                block = (ALL, near_places[step])
            mine = (self.held, block + (core,))
            return Copy(
                self.key, self.sems, GROUP * outer + step, sibling, mine, mine,
                (self.held, block + (other,)),
            )

        def place(self, mine):
            self.held[far, near, core] = mine.astype(BF16)

        def far_start(self):
            for step in far_steps:
                self.far_copy(step).start()

        def near_start(self, hop):
            for step in near_steps:
                self.near_copy(step, hop).start()

        def begin(self):
            if not self.near_first:
                self.far_start()

        def turn(self):
            if self.near_first:
                for step in near_steps:
                    self.near_copy(step, 0).arrive()
                self.far_start()
            else:
                for hop in far_steps:
                    self.far_copy(hop).arrive()
                    self.near_start(hop)
            self.cross(0).start()

        def pass_on(self):
            if self.near_first:
                for step in far_steps:
                    self.far_copy(step).arrive()
                    self.cross(step).start()
                return
            for step in near_steps:
                for hop in range(outer):
                    self.near_copy(step, hop).arrive()
                self.cross(step).start()

        def end(self):
            for step in range(outer if self.near_first else GROUP):
                self.cross(step).arrive()


    class Reduce:
        def __init__(self, name):
            self.key = ("sum", name)
            self.far_first = name in FAR_FIRST
            for part in ("g", "pair", "near", "far", "done"):
                setattr(self, part, getattr(r, part + "_" + name))
            self.sems = (
                getattr(r, "sum_" + name + "_sends"), getattr(r, "sum_" + name + "_receives")
            )

        def pair_copy(self):
            return Copy(
                self.key, self.sems, 0, sibling, (self.g, (ALL, ALL, other)),
                (self.pair, ALL),
            )

        def near_copy(self, step):
            block = far if self.far_first else ALL
            return Copy(
                self.key, self.sems, step, near_devices[step],
                (self.pair, (block, near_places[step])), (self.near, step - 1),
            )

        def far_copy(self, step):
            block = ALL if self.far_first else near
            return Copy(
                self.key, self.sems, GROUP + step - 1, far_devices[step],
                (self.pair, (far_places[step], block)), (self.far, step - 1),
            )

        def done_copy(self):
            mine = (self.done, core)
            return Copy(
                self.key, self.sems, GROUP + outer, sibling, mine, mine,
                (self.done, other),
            )

        def begin(self):
            self.pair_copy().start()

        def turn(self):
            self.pair_copy().arrive()

            both = self.g[:, :, core].astype(F32) + self.pair[...].astype(F32)
            self.pair[...] = both.astype(BF16)
            if self.far_first:
                for step in far_steps:
                    self.far_copy(step).start()
            else:
                for step in near_steps:
                    self.near_copy(step).start()

        def pass_on(self):
            if self.far_first:
                for step in far_steps:
                    self.far_copy(step).arrive()
                total = self.pair[far].astype(F32)
                for step in far_steps:
                    total = total + self.far[step - 1].astype(F32)
                self.pair[far] = total.astype(BF16)
                for step in near_steps:
                    self.near_copy(step).start()
                return
            for step in near_steps:
                self.near_copy(step).arrive()

            total = self.pair[:, near].astype(F32)
            for step in near_steps:
                total = total + self.near[step - 1].astype(F32)
            self.pair[:, near] = total.astype(BF16)
            for step in far_steps:
                self.far_copy(step).start()

        def collect(self):
            total = self.pair[far, near].astype(F32)
            if self.far_first:
                for step in near_steps:
                    self.near_copy(step).arrive()
                    total = total + self.near[step - 1].astype(F32)
            else:
                for step in far_steps:
                    self.far_copy(step).arrive()
                    total = total + self.far[step - 1].astype(F32)
            self.done[core] = total
            self.done_copy().start()

        def end(self):
            self.done_copy().arrive()

    early = Sum("early", 1)
    late = Sum("late", 1)
    vector_sum = Sum("vector", 2)
    column_sum = Sum("column", 1)
    last_sum = Sum("ends", 2)
    step_sum = Sum("step", 2)
    gathers = {name: Gather(name) for name in PARTS}
    sums = {name: Reduce(name) for name in tuple(SPANS) + PARTS[2:]}
    shards = {name: getattr(r, name + "_weight") for name in MATRICES}

    def my_rows(shard):
        half = shard.shape[0] // 2
        return shard[pl.ds(pl.multiple_of(core * half, half), half), :]

    def place(name):
        for part, mine in zip(PARTS_OF[name], in_parts(name, my_rows(shards[name]))):
            gathers[part].place(mine)

    place(ATTEND)
    gathers[LOW].begin()
    gathers[LOW].near_start(0)
    gathers[HIGH].begin()
    place(SHRINK)
    for part in NEAR_FIRST:
        gathers[part].near_start(0)
    gathers[HIGH].near_start(0)


    columns_of = {name: getattr(r, name + "_columns").shape[1] * outer * GROUP for name in MATRICES}
    late_at = late_places(columns_of, width)
    column_at = column_places(columns_of, width)

    def early_value():
        thin = r.vectors_own.shape[1]
        r.packed[...] = jnp.zeros_like(r.packed)
        r.packed[0:6, 0:thin] = r.vectors_own[...]
        vectors = pltpu.roll(r.packed[0:8, :], chip * thin, 1)
        r.packed[0:8, :] = vectors
        for at, name in enumerate(MATRICES):
            lanes = slice(at * 128, at * 128 + 128)
            shard = shards[name][...]
            r.packed[SQUARES : SQUARES + 1, lanes] = fold_lanes(
                jnp.sum(fold_rows(shard * shard), axis=0, keepdims=True)
            )
            total = jnp.sum(getattr(r, name + "_rows")[...], axis=1, keepdims=True)
            first_lane = lax.broadcasted_iota(jnp.int32, (1, 128), 1) == 0
            r.packed[ROW_SUMS : ROW_SUMS + 1, lanes] = jnp.where(first_lane, total, 0.0)
        return r.packed[0:EARLY_ROWS, :]

    def late_value():
        thin = r.vectors_own.shape[1]
        r.packed[...] = jnp.zeros_like(r.packed)
        r.packed[0:6, 0:thin] = r.moments_own[...]
        for name in (MERGER, SHRINK):
            row, _ = late_at[name]
            r.packed[row : row + 1, 0:thin] = getattr(r, name + "_columns")[...]
        r.packed[0:8, :] = pltpu.roll(r.packed[0:8, :], chip * thin, 1)
        for name in (ATTEND, EXPAND):
            own = getattr(r, name + "_columns")
            size = own.shape[1]
            r.spread[...] = jnp.zeros_like(r.spread)
            r.spread[0:1, 0:size] = own[...]
            whole = pltpu.roll(r.spread[:, : columns_of[name]], chip * size, 1)[0:1, :]
            split_into(r.packed, late_at[name][0], whole, width)
        return r.packed[...]


    place(MERGER)
    place(EXPAND)
    early.begin(early_value())
    load_tokens.wait()
    prepare(r)
    gathers[LOW].turn()
    later = [part for part in PARTS[2:] if part not in NEAR_FIRST]
    for part in later:
        gathers[part].begin()
    gathers[HIGH].turn()
    early.turn()
    for part in later:
        gathers[part].near_start(0)
    for part in NEAR_FIRST:
        gathers[part].turn()
    gathers[LOW].pass_on()
    gathers[LOW].end()
    project(r, 0)
    gathers[MERGER].turn()
    attend_forward(r, 0, 2, ())
    gathers[HIGH].pass_on()
    gathers[EXPAND_A].turn()
    gathers[EXPAND_B].turn()
    gathers[HIGH].end()
    project(r, 1)
    gathers[SHRINK_A].turn()
    attend_forward(r, 2, 4, ())
    gathers[MERGER].pass_on()
    early_all = early.end()
    r.early[...] = early_all
    r.vectors[...] = early_all.astype(BF16).astype(F32)
    gathers[EXPAND_A].pass_on()
    gathers[MERGER].end()
    gathers[EXPAND_B].pass_on()
    gathers[EXPAND_A].end()
    gathers[EXPAND_B].end()
    first_half(r)
    late.begin(late_value())
    load_cotangent.wait()
    gathers[SHRINK_A].pass_on()
    gathers[SHRINK_B].pass_on()
    gathers[SHRINK_A].end()
    gathers[SHRINK_B].end()
    second_half(r)
    store_result = local(r.result, r.result_out, 0)
    store_result.start()


    shrink_gradient(r, 0)
    sums[SHRINK_A].begin()
    shrink_gradient(r, 1)
    sums[SHRINK_B].begin()
    sums[SHRINK_A].turn()
    late.turn()
    way_back(r, sums[SHRINK_B].turn)
    expand_gradient(r, 0)
    sums[EXPAND_A].begin()
    expand_gradient(r, 1)
    sums[EXPAND_B].begin()
    vector_sum.begin(vector_total(r))
    merger_gradient(r)
    sums[MERGER].begin()
    sums[EXPAND_A].turn()

    def hook_one():
        sums[EXPAND_B].turn()
        sums[MERGER].turn()
        sums[SHRINK_A].pass_on()

    def hook_three():
        attend_part(MID)
        sums[LOW].turn()
        vector_sum.turn()
        sums[SHRINK_B].pass_on()
        sums[EXPAND_A].pass_on()

    def attend_part(name):
        first, last = [place * (width // 4) for place in SPANS[name]]
        attend_gradient(r, getattr(r, "g_" + name), first, last)
        sums[name].begin()

    pairs = width // 128
    attend_backward(r, 0, pairs // 2, ((1, hook_one),))
    attend_part(LOW)
    attend_backward(r, pairs // 2, pairs, ((pairs // 2 + 1, hook_three),))
    attend_part(LAST)
    sums[MID].turn()
    sums[LAST].turn()


    def keep(name):
        for part in PARTS_OF[name]:
            sums[part].end()
        done = [flat(getattr(r, "done_" + part)[...]) for part in PARTS_OF[name]]
        if name == SHRINK:
            done = [value.T for value in done]
        whole_done = jnp.concatenate(done, axis=1)
        getattr(r, "out_" + name)[...] = whole_done
        squares = jnp.sum(whole_done * whole_done, axis=0, keepdims=True)
        split_into(r.packed, column_at[name][0], squares, width)

    sums[EXPAND_B].pass_on()
    sums[MERGER].pass_on()
    sums[LOW].pass_on()
    sums[SHRINK_A].collect()
    sums[MID].pass_on()
    r.late[...] = late.end()
    r.vector_out[...] = vector_sum.end()
    r.packed[...] = jnp.zeros_like(r.packed)
    sums[LAST].pass_on()
    sums[SHRINK_B].collect()
    sums[MERGER].collect()
    sums[EXPAND_A].collect()
    sums[LOW].collect()
    sums[EXPAND_B].collect()
    sums[MID].collect()
    sums[LAST].collect()
    attend_half = heads_together([getattr(r, "done_" + name)[core] for name in SPANS])
    squares = jnp.sum(attend_half * attend_half, axis=0, keepdims=True)
    row = COLUMN_ROWS
    split_into(r.packed, row, squares, width)
    last_sum.begin(r.packed[row : row + LAST_ROWS, :])
    keep(SHRINK)
    keep(MERGER)
    keep(EXPAND)
    column_sum.begin(r.packed[0:COLUMN_ROWS, :])
    input_gradient(r)
    store_input = local(r.straight, r.input_out, 1)
    store_input.start()
    last_sum.turn()
    column_sum.turn()
    for name in SPANS:
        sums[name].end()
    r.out_attend[...] = heads_together([flat(getattr(r, "done_" + name)[...]) for name in SPANS])
    r.early_out[...] = r.early[...]
    r.late_out[...] = r.late[...]
    r.column_out[row : row + LAST_ROWS, :] = last_sum.end()
    r.column_out[0:COLUMN_ROWS, :] = column_sum.end()
    facts = Statistics(r, layout_sizes, r.column_out, r.vector_out[...])

    def my_half(value):
        half = value.shape[0] // 2
        return jnp.where(core == 0, value[:half], value[half:])

    rows = []
    for name in MATRICES:
        rows_old = getattr(r, name + "_rows")[...]
        step = facts.factored(
            name, my_rows(getattr(r, "out_" + name)), my_half(column_of(rows_old)),
            float(rows_old.shape[1] * outer * GROUP),
        )[3]
        rows.append(fold_lanes(jnp.sum(step * step, axis=0, keepdims=True)))
    step_sum.begin(jnp.concatenate(rows + [jnp.zeros((4, 128), F32)], axis=0))
    step_sum.turn()
    r.step_out[...] = step_sum.end()


    for copy in started.values():
        copy.leave()
    store_result.wait()
    store_input.wait()


def update_kernel(layout_sizes, names, *refs):
    outer, width, wide = layout_sizes
    r = Refs(names, refs)
    chip = lax.axis_index(FSDP)
    out_of = [
        pltpu.make_async_copy(r.result_in, r.block_output, r.sems.at[2]),
        pltpu.make_async_copy(r.input_in, r.input_gradient, r.sems.at[3]),
    ]
    for copy in out_of:
        copy.start()
    vector_gradient = r.vector_sum[...]
    facts = Statistics(r, layout_sizes, r.column_sum, vector_gradient)
    r.global_norm[...] = facts.norm
    for name in MATRICES:
        weight = getattr(r, name + "_weight")[...]
        rows_all = float(weight.shape[0] * outer * GROUP)
        count = rows_all * weight.shape[1]
        clipped, new_rows, new_columns, step = facts.factored(
            name, getattr(r, name + "_sum")[...], column_of(getattr(r, name + "_rows")[...]), rows_all
        )
        at = MATRICES.index(name)
        step_square = jnp.sum(r.step_sum[at : at + 1, :], axis=1, keepdims=True)
        weight_square = facts.lanes(SQUARES, name)
        shrunk = jnp.maximum(1.0, jnp.sqrt(step_square * (1.0 / count)) * (1.0 / UPDATE_LIMIT))
        stride = LEARN_RATE * jnp.maximum(0.001, jnp.sqrt(weight_square * (1.0 / count)))
        updated = weight - (stride / shrunk) * step
        getattr(r, name + "_gradient")[...] = clipped
        getattr(r, name + "_updated")[...] = updated
        getattr(r, name + "_bfloat")[...] = updated.astype(BF16)
        getattr(r, name + "_newrows")[...] = row_of(new_rows)
        size = getattr(r, name + "_newcols").shape[1]
        wide_row = jnp.broadcast_to(new_columns, (8, new_columns.shape[1]))
        whole = new_columns.shape[1]
        own = pltpu.roll(wide_row, lax.rem(whole - chip * size, whole), 1)
        getattr(r, name + "_newcols")[...] = own[0:1, 0:size]
    vectors = r.early[...]
    clipped, variance, step = vector_steps(
        vector_gradient, r.late[0:8, :], facts.clip
    )
    shrunk = jnp.maximum(1.0, jnp.sqrt(lane_mean(step * step)) * (1.0 / UPDATE_LIMIT))
    stride = LEARN_RATE * jnp.maximum(0.001, jnp.sqrt(lane_mean(vectors * vectors)))
    updated = vectors - stride * (step / shrunk)
    thin = r.vector_updated.shape[1]
    turn = lax.rem(width - chip * thin, width)
    for ref, value in (
        (r.vector_gradient, clipped),
        (r.vector_variance, variance),
        (r.vector_updated, updated),
    ):
        ref[...] = pltpu.roll(value, turn, 1)[0:6, 0:thin]
    for copy in out_of:
        copy.wait()


def in_vmem():
    return pl.BlockSpec(memory_space=pltpu.VMEM)


def anywhere():
    return pl.BlockSpec(memory_space=pl.ANY)


def call(kernel, sizes, inputs, outputs, scratch, held, params, name):
    names = list(inputs) + list(outputs) + list(scratch)
    results = pl.pallas_call(
        functools.partial(kernel, sizes, names),
        in_specs=[anywhere() if key in held else in_vmem() for key in inputs],
        out_specs=[anywhere() if key in held else in_vmem() for key in outputs],
        out_shape=list(outputs.values()),
        scratch_shapes=list(scratch.values()),
        compiler_params=params,
        name=name,
    )(*inputs.values())
    return dict(zip(outputs, results, strict=True))


def add_gather(scratch, outer, name, held):
    scratch[name] = pltpu.VMEM((outer, GROUP, 2) + held, BF16)
    for way in ("_sends", "_receives"):
        scratch[name + way] = pltpu.SemaphoreType.DMA((GROUP * outer + GROUP,))


def add_reduce(scratch, outer, name, half):
    far_first = name in FAR_FIRST
    near_block = half if far_first else (outer,) + half
    far_block = (GROUP,) + half if far_first else half
    scratch["g_" + name] = pltpu.VMEM((outer, GROUP, 2) + half, BF16)
    scratch["pair_" + name] = pltpu.VMEM((outer, GROUP) + half, BF16)
    scratch["near_" + name] = pltpu.VMEM((GROUP - 1,) + near_block, BF16)
    scratch["far_" + name] = pltpu.VMEM((max(1, outer - 1),) + far_block, BF16)
    scratch["done_" + name] = pltpu.VMEM((2,) + half, F32)
    for way in ("_sends", "_receives"):
        scratch["sum_" + name + way] = pltpu.SemaphoreType.DMA((GROUP + outer + 1,))


def staged_shards(devices, tokens, lengths, weights, vectors, rows, columns, moments, cotangent):
    outer = devices // GROUP
    slots, width = tokens.shape[1:]
    wide = weights[EXPAND].shape[1]
    sizes = (outer, width, wide)
    shape = jax.ShapeDtypeStruct
    row_in = {name + "_rows": rows[name].reshape(1, -1) for name in MATRICES}
    column_in = {name + "_columns": columns[name].reshape(1, -1) for name in MATRICES}
    weight_in = {name + "_weight": weights[name] for name in MATRICES}
    inputs = dict(
        tokens_in=tokens[0], lengths=lengths, cotangent_in=cotangent[0],
        vectors_own=vectors, moments_own=moments, **weight_in, **row_in, **column_in,
    )
    outputs = dict(
        result_out=shape((slots, width), BF16),
        input_out=shape((slots, width), F32),
        vector_out=shape((8, width), F32),
        early_out=shape((EARLY_ROWS, width), F32),
        late_out=shape((LATE_ROWS, width), F32),
        column_out=shape((2 * COLUMN_ROWS, width), F32),
        step_out=shape((8, 128), F32),
        **{"out_" + name: shape(weights[name].shape, F32) for name in MATRICES},
    )
    scratch = row_scratch(slots, width, wide)
    scratch.update(
        tokens=pltpu.VMEM((slots, width), BF16),
        cotangent=pltpu.VMEM((slots, width), BF16),
        straight=pltpu.VMEM((slots, width), F32),
        vectors=pltpu.VMEM((8, width), F32),
        early=pltpu.VMEM((EARLY_ROWS, width), F32),
        late=pltpu.VMEM((LATE_ROWS, width), F32),
        packed=pltpu.VMEM((LATE_ROWS, width), F32),
        spread=pltpu.VMEM((8, wide), F32),
        local_sems=pltpu.SemaphoreType.DMA((2,)),
    )
    for name, cores, size in (
        ("early", 1, (EARLY_ROWS, width)),
        ("late", 1, (LATE_ROWS, width)),
        ("vector", 2, (8, width)),
        ("column", 1, (COLUMN_ROWS, width)),
        ("ends", 2, (LAST_ROWS, width)),
        ("step", 2, (8, 128)),
    ):
        scratch[name + "_near"] = pltpu.VMEM((cores, GROUP) + size, F32)
        scratch[name + "_far"] = pltpu.VMEM((outer,) + size, F32)
        for way in ("_sends", "_receives"):
            scratch[name + way] = pltpu.SemaphoreType.DMA((2 * GROUP + outer,))
    for of in MATRICES:
        rows, all_columns = weights[of].shape
        wide_now = all_columns // len(PARTS_OF[of])
        for name in PARTS_OF[of]:
            add_gather(scratch, outer, name, (rows // 2, wide_now))
            if of != ATTEND:
                half = (wide_now // 2, rows) if of == SHRINK else (rows // 2, wide_now)
                add_reduce(scratch, outer, name, half)
    rows, all_columns = weights[ATTEND].shape
    for name, (first, last) in SPANS.items():
        add_reduce(scratch, outer, name, (rows // 2, (last - first) * all_columns // 4))
    got = call(
        shard_kernel, sizes, inputs, outputs, scratch,
        ("tokens_in", "cotangent_in", "result_out", "input_out"),
        pltpu.CompilerParams(
            collective_id=1, has_side_effects=True, vmem_limit_bytes=VMEM_LIMIT
        ),
        "row_and_sums",
    )
    inputs = dict(
        result_in=got["result_out"], input_in=got["input_out"], vector_sum=got["vector_out"],
        early=got["early_out"], late=got["late_out"], column_sum=got["column_out"], step_sum=got["step_out"],
        **{name + "_sum": got["out_" + name] for name in MATRICES},
        **weight_in, **row_in, **column_in,
    )
    outputs = dict(
        block_output=shape((slots, width), BF16),
        input_gradient=shape((slots, width), F32),
        global_norm=shape((1, 1), F32),
    )
    for name in MATRICES:
        outputs[name + "_gradient"] = shape(weights[name].shape, F32)
        outputs[name + "_newrows"] = shape(row_in[name + "_rows"].shape, F32)
        outputs[name + "_newcols"] = shape(column_in[name + "_columns"].shape, F32)
        outputs[name + "_updated"] = shape(weights[name].shape, F32)
        outputs[name + "_bfloat"] = shape(weights[name].shape, BF16)
    for name in ("vector_gradient", "vector_variance", "vector_updated"):
        outputs[name] = shape(vectors.shape, F32)
    out = call(
        update_kernel, sizes, inputs, outputs,
        dict(
            sems=pltpu.SemaphoreType.DMA((4,)),
        ),
        ("block_output", "input_gradient"),
        pltpu.CompilerParams(vmem_limit_bytes=VMEM_LIMIT),
        "update",
    )
    out["block_output"] = out["block_output"][None]
    out["input_gradient"] = out["input_gradient"][None]
    out["global_norm"] = out["global_norm"].reshape(())
    for name in MATRICES:
        for kind in ("_newrows", "_newcols"):
            out[name + kind] = out[name + kind].reshape(-1)
    return tuple(out.values())


def tiled_gradient(into, left, right):
    def tile(step, carry):
        columns = aligned(step * 2 * TILE, 2 * TILE)
        into[:, columns] = dot_nn(left[...], right[:, columns]).astype(into.dtype)
        return carry

    lax.fori_loop(0, into.shape[1] // (2 * TILE), tile, 0)


def row_kernel(names, *refs):
    r = Refs(names, refs)
    r.attend = (r.attend_low, r.attend_high)
    r.expand, r.shrink = (r.expand,), (r.shrink,)
    width = r.tokens.shape[1]
    pairs = width // 128
    steps = (
        functools.partial(prepare, r),
        functools.partial(project, r, 0),
        functools.partial(project, r, 1),
        functools.partial(attend_forward, r, 0, pairs, ()),
        functools.partial(first_half, r),
        functools.partial(second_half, r),
        functools.partial(tiled_gradient, r.g_shrink, r.d_second_t, r.active),
        functools.partial(way_back, r),
        functools.partial(tiled_gradient, r.g_expand, r.first_t, r.d_hidden),
        functools.partial(tiled_gradient, r.g_merger, r.context_t, r.d_branch),
        functools.partial(attend_backward, r, 0, pairs, ()),
        functools.partial(attend_gradient, r, r.g_attend_low, 0, width // 2),
        functools.partial(attend_gradient, r, r.g_attend_high, width // 2, width),
        functools.partial(input_gradient, r),
    )
    for step in steps:
        pl.when(lax.axis_index(FSDP) >= 0)(step)
    r.g_vectors[...] = vector_total(r)


def plain_shards(devices, tokens, lengths, weights, vectors, rows, columns, moments, cotangent):
    slots, width = tokens.shape[1:]
    wide = weights[EXPAND].shape[1]
    shape = jax.ShapeDtypeStruct
    whole = {
        name: lax.all_gather(weights[name].astype(BF16), FSDP, axis=0, tiled=True)
        for name in MATRICES
    }
    vector_rows = lax.all_gather(vectors.astype(BF16), FSDP, axis=1, tiled=True).astype(F32)
    vector_rows = jnp.concatenate([vector_rows, jnp.zeros((2, width), F32)], axis=0)
    whole["attend_low"], whole["attend_high"] = heads_apart(whole.pop(ATTEND))
    inputs = dict(
        tokens=tokens[0], lengths=lengths, cotangent=cotangent[0], vectors=vector_rows, **whole
    )
    outputs = dict(
        result=shape((slots, width), BF16),
        straight=shape((slots, width), F32),
        g_vectors=shape((8, width), F32),
        g_attend_low=shape((width, 3 * width // 2), BF16),
        g_attend_high=shape((width, 3 * width // 2), BF16),
        g_merger=shape((width, width), BF16),
        g_expand=shape((width, wide), BF16),
        g_shrink=shape((width, wide), BF16),
    )
    scratch = row_scratch(slots, width, wide)
    scratch["d_branch"] = pltpu.VMEM((slots, width), BF16)
    names = list(inputs) + list(outputs) + list(scratch)
    got = pl.pallas_call(
        functools.partial(row_kernel, names),
        in_specs=[in_vmem()] * len(inputs),
        out_specs=[in_vmem()] * len(outputs),
        out_shape=list(outputs.values()),
        scratch_shapes=list(scratch.values()),
        compiler_params=pltpu.CompilerParams(vmem_limit_bytes=VMEM_LIMIT),
        name="row",
    )(*inputs.values())
    got = dict(zip(outputs, got, strict=True))
    got["g_" + ATTEND] = heads_together((got["g_attend_low"], got["g_attend_high"]))
    grads = []
    for name in MATRICES:
        value = lax.psum(got["g_" + name], DP).astype(F32)
        if name == SHRINK:
            grads.append(lax.psum_scatter(value.T, FSDP, scatter_dimension=0, tiled=True))
        else:
            grads.append(lax.psum_scatter(value, FSDP, scatter_dimension=0, tiled=True))
    vector_all = lax.psum(got["g_vectors"][:6], (DP, FSDP))
    index = lax.axis_index(FSDP)

    def spread(own, dim):
        size = own.shape[dim]
        extent = own.shape[:dim] + (size * devices,) + own.shape[dim + 1 :]
        return lax.dynamic_update_slice_in_dim(
            jnp.zeros(extent, F32), own, index * size, dim
        )

    early = (
        [spread(columns[name], 0) for name in MATRICES],
        [jnp.sum(weights[name] * weights[name]) for name in MATRICES],
        [jnp.sum(rows[name]) for name in MATRICES],
        [jnp.sum(grad * grad, axis=0) for grad in grads],
        jnp.sum(vectors * vectors, axis=1),
    )
    old_columns, weight_squares, row_sums, columns_now, vector_squares = lax.psum(early, FSDP)
    squares = [jnp.sum(value) for value in columns_now]
    total = jnp.sum(vector_all * vector_all)
    for value in squares:
        total = total + value
    norm = jnp.sqrt(total)
    clip = jnp.minimum(1.0, THRESHOLD / norm)
    power = clip * clip
    pieces = []
    for at, name in enumerate(MATRICES):
        grad = grads[at]
        rows_all = float(grad.shape[0] * devices)
        count = rows_all * grad.shape[1]
        new_rows = FORGET * rows[name] + (1.0 - FORGET) * (
            power * jnp.mean(grad * grad, axis=1) + TINY_VALUE
        )
        new_columns = FORGET * old_columns[at] + (1.0 - FORGET) * (
            power * columns_now[at] / rows_all + TINY_VALUE
        )
        mean = FORGET * row_sums[at] / rows_all + (1.0 - FORGET) * (
            power * squares[at] / count + TINY_VALUE
        )
        clipped = clip * grad
        step = clipped * lax.rsqrt(new_rows[:, None] * new_columns[None, :] / mean)
        pieces.append((clipped, new_rows, new_columns, step, count))
    thin = vectors.shape[1]
    vector_clipped = clip * lax.dynamic_slice_in_dim(vector_all, index * thin, thin, 1)
    variance = FORGET * moments + (1.0 - FORGET) * (vector_clipped * vector_clipped + TINY_VALUE)
    vector_step = vector_clipped * lax.rsqrt(variance)
    step_squares, vector_step_squares = lax.psum(
        (
            [jnp.sum(piece[3] * piece[3]) for piece in pieces],
            jnp.sum(vector_step * vector_step, axis=1),
        ),
        FSDP,
    )
    results = [got["result"][None], got["straight"][None], norm]
    for at, name in enumerate(MATRICES):
        clipped, new_rows, new_columns, step, count = pieces[at]
        shrunk = jnp.maximum(1.0, jnp.sqrt(step_squares[at] / count) / UPDATE_LIMIT)
        stride = LEARN_RATE * jnp.maximum(0.001, jnp.sqrt(weight_squares[at] / count))
        updated = weights[name] - stride * (step / shrunk)
        size = columns[name].shape[0]
        own = lax.dynamic_slice_in_dim(new_columns, index * size, size, 0)
        results.extend([clipped, new_rows, own, updated, updated.astype(BF16)])
    extent = float(width)
    shrunk = jnp.maximum(1.0, jnp.sqrt(vector_step_squares / extent) / UPDATE_LIMIT)[:, None]
    stride = LEARN_RATE * jnp.maximum(0.001, jnp.sqrt(vector_squares / extent))[:, None]
    results.extend([vector_clipped, variance, vectors - stride * (vector_step / shrunk)])
    return tuple(results)


def shards(
    devices,
    tokens,
    lengths,
    attend_weight,
    merger_weight,
    expand_weight,
    shrink_weight,
    vectors,
    attend_rows,
    attend_columns,
    merger_rows,
    merger_columns,
    expand_rows,
    expand_columns,
    shrink_rows,
    shrink_columns,
    vector_moments,
    cotangent,
):
    weights = dict(
        attend=attend_weight, merger=merger_weight, expand=expand_weight, shrink=shrink_weight
    )
    rows = dict(attend=attend_rows, merger=merger_rows, expand=expand_rows, shrink=shrink_rows)
    columns = dict(
        attend=attend_columns, merger=merger_columns, expand=expand_columns, shrink=shrink_columns
    )
    assert tokens.shape[0] == 1
    fits = devices % GROUP == 0 and all(
        weight.shape[0] % 32 == 0 for weight in weights.values()
    ) and shrink_weight.shape[0] % 128 == 0
    body = staged_shards if fits else plain_shards
    return body(
        devices, tokens, lengths, weights, vectors, rows, columns, vector_moments, cotangent
    )


def solution(mesh):
    split = P(FSDP, None)
    row = P((DP, FSDP), None, None)
    one = P(FSDP)
    thin = P(None, FSDP)
    in_specs = (
        (row, P((DP, FSDP), None)) + (split,) * 4 + (thin,) + (one,) * 8 + (thin, row)
    )
    out_specs = (row, row, P()) + (split, one, one, split, split) * 4 + (thin,) * 3
    return jax.shard_map(
        functools.partial(shards, mesh.shape[FSDP]),
        mesh=mesh, in_specs=in_specs, out_specs=out_specs, check_vma=False,
    )
```

```python
import functools

import jax
import jax.numpy as jnp
from jax import lax
from jax.experimental import pallas as pl
from jax.experimental.pallas import tpu as pltpu
from jax.sharding import PartitionSpec as P

F32 = jnp.float32
BF16 = jnp.bfloat16
HEAD_DIM = 64
STEP = 3
EPSILON = 1e-05
TINY_VALUE = 1e-30
NEGATIVE = -1e30
THRESHOLD = 1.0
UPDATE_LIMIT = 1.0
LEARN_RATE = 0.5
FORGET = 1.0 - float(STEP) ** (-0.8)
LOG2_E = 1.4426950408889634
GELU_A = 0.7978845608028654
GELU_B = 0.044715 * GELU_A

REACH = 256
QUERY_BLOCK = 128
TILE = 256
GROUP = 4
DP, FSDP = "dp", "fsdp"
ATTEND, MERGER, EXPAND, SHRINK = "attend", "merger", "expand", "shrink"
MATRICES = (ATTEND, MERGER, EXPAND, SHRINK)
MESH = pl.DeviceIdType.MESH
VMEM_LIMIT = 63 << 20


def dot_general(left, right, left_dim, right_dim):
    return lax.dot_general(
        left, right, (((left_dim,), (right_dim,)), ((), ())), preferred_element_type=F32
    )


def dot_nn(left, right):
    return dot_general(left, right, 1, 0)


def dot_nt(left, right):
    return dot_general(left, right, 1, 1)


def dot_tn(left, right):
    return dot_general(left, right, 0, 0)


def flat(value):
    return value.reshape(-1, value.shape[-1])


def whole(parts):
    return jnp.concatenate([flat(part[...]) for part in parts], axis=1)


def fold_rows(value):
    return jnp.sum(value.reshape(value.shape[0] // 8, 8, value.shape[1]), axis=0)


def fold_lanes(row):
    total = row[:, :128]
    for start in range(128, row.shape[1], 128):
        total = total + row[:, start : start + 128]
    return total


def diagonal(size):
    return lax.broadcasted_iota(jnp.int32, (size, size), 0) == lax.broadcasted_iota(
        jnp.int32, (size, size), 1
    )


def column_of(row):
    size = row.shape[1]
    return jnp.sum(jnp.where(diagonal(size), row, 0.0), axis=1, keepdims=True)


def row_of(column):
    size = column.shape[0]
    return jnp.sum(jnp.where(diagonal(size), column, 0.0), axis=0, keepdims=True)


def lane_mean(value):
    return jnp.mean(value, axis=-1, keepdims=True)


def aligned(start, size):
    return pl.ds(pl.multiple_of(start, size), size)


def band(slots):
    pieces = []
    place = 0
    for first in range(0, slots, QUERY_BLOCK):
        low = max(0, first - REACH)
        high = first + QUERY_BLOCK
        pieces.append((first, low, high, place))
        place += high - low
    return pieces, place


def prepare(r):
    slots = r.tokens.shape[0]
    count = r.lengths.shape[1]
    for start in range(0, slots, TILE):
        r.tokens_t[:, start : start + TILE] = r.tokens[start : start + TILE, :].T
    lengths = r.lengths[...].astype(F32)
    rows = jnp.broadcast_to(lengths, (8, count)).astype(BF16)
    upto = lax.broadcasted_iota(jnp.int32, (count, count), 1) <= lax.broadcasted_iota(
        jnp.int32, (count, count), 0
    )
    ends = dot_nt(jnp.where(upto, 1.0, 0.0).astype(BF16), rows)[:, 0:1]
    places = lax.broadcasted_iota(jnp.int32, (count, slots), 1).astype(F32)
    ended = jnp.where(ends <= places, 1.0, 0.0).astype(BF16)
    begin = dot_nn(rows, ended)[0:1, :]
    total = jnp.sum(lengths, axis=1, keepdims=True)
    r.total[...] = jnp.broadcast_to(total, r.total.shape)
    slot = lax.broadcasted_iota(jnp.int32, (1, slots), 1).astype(F32)
    begin = jnp.where(slot < total, begin, slot)
    for first, low, high, place in band(slots)[0]:
        key = (lax.broadcasted_iota(jnp.int32, (high - low, QUERY_BLOCK), 0) + low).astype(F32)
        query = slot[:, first : first + QUERY_BLOCK]
        fits = (key >= begin[:, first : first + QUERY_BLOCK]) & (key <= query)
        r.mask[place : place + high - low, :] = jnp.where(fits, 1.0, 0.0).astype(BF16)


def project(r, part):
    width = r.tokens.shape[1]
    half = width // 2
    columns = flat(r.attend[part][...])
    for at in range(3):
        rows = slice(at * width + part * half, at * width + (part + 1) * half)
        value = dot_tn(columns[:, at * half : (at + 1) * half], r.tokens_t[...]).astype(BF16)
        r.projected_t[rows, :] = value
    for at in range(2):
        start = at * width + part * half
        r.key_value[:, start : start + half] = r.projected_t[
            width + start : width + start + half, :
        ].T


def beside_zeros(value, head):
    zeros = jnp.zeros_like(value)
    return jnp.concatenate([value, zeros] if head == 0 else [zeros, value], axis=0)


def head_rows(part, width, pair, head):
    return pl.ds(pl.multiple_of(part * width + pair * 128 + HEAD_DIM * head, HEAD_DIM), HEAD_DIM)


def by_pairs(first, last, hooks, body):
    def pair(step, carry):
        for at, hook in hooks:
            pl.when(step == at)(hook)
        body(step)
        return carry

    lax.fori_loop(first, last, pair, 0)


def attend_forward(r, first_pair, last_pair, hooks):
    slots, width = r.tokens.shape
    factor = HEAD_DIM ** -0.5 * LOG2_E
    items = [(head,) + piece for head in (0, 1) for piece in band(slots)[0]]

    def body(pair):
        lanes = pl.ds(pl.multiple_of(pair * 128, 128), 128)

        def scores_of(item):
            head, first, low, high, _ = item
            queries = r.projected_t[head_rows(0, width, pair, head), first : first + QUERY_BLOCK]
            return dot_nn(r.key_value[low:high, lanes], beside_zeros(queries, head))

        def probs_of(item, scores):
            head, _, low, high, place = item
            fits = r.mask[place : place + high - low, :].astype(F32) > 0.5
            scores = jnp.where(fits, scores * factor, NEGATIVE)
            weights = jnp.exp2(scores - jnp.max(scores, axis=0, keepdims=True))
            inverse = 1.0 / jnp.sum(weights, axis=0, keepdims=True)
            probs = (weights * inverse).astype(BF16)
            r.probs[2 * pair + head, place : place + high - low, :] = probs
            return probs

        def put_context(item, probs):
            head, first, low, high, _ = item
            values = r.projected_t[head_rows(2, width, pair, head), low:high]
            r.context_t[head_rows(0, width, pair, head), first : first + QUERY_BLOCK] = dot_nn(
                values, probs
            ).astype(BF16)

        scores = [scores_of(item) for item in items]
        probs = [probs_of(item, value) for item, value in zip(items, scores)]
        for item, value in zip(items, probs):
            put_context(item, value)

    by_pairs(first_pair, last_pair, hooks, body)


def attend_backward(r, first_pair, last_pair, hooks):
    slots, width = r.tokens.shape
    scale = HEAD_DIM ** -0.5
    pieces = band(slots)[0]
    count = len(pieces)
    items = [(head, at) for head in (0, 1) for at in range(count)]

    def body(pair):
        lanes = pl.ds(pl.multiple_of(width + pair * 128, 128), 128)
        queries = [r.projected_t[head_rows(0, width, pair, head), :] for head in (0, 1)]
        keys_t = [r.projected_t[head_rows(1, width, pair, head), :] for head in (0, 1)]
        upstream = [r.d_context_t[head_rows(0, width, pair, head), :] for head in (0, 1)]

        def probs_of(item):
            _, low, high, place = pieces[item[1]]
            return r.probs[2 * pair + item[0], place : place + high - low, :]

        def d_probs_of(item):
            first, low, high, _ = pieces[item[1]]
            arriving = upstream[item[0]][:, first : first + QUERY_BLOCK]
            return dot_nn(r.key_value[low:high, lanes], beside_zeros(arriving, item[0]))

        def d_scores_of(item, d_probs):
            wide = probs_of(item).astype(F32)
            inner = jnp.sum(wide * d_probs, axis=0, keepdims=True)
            return (wide * (d_probs - inner)).astype(BF16)

        def put_queries(item, d_scores):
            first, low, high, _ = pieces[item[1]]
            value = dot_nn(keys_t[item[0]][:, low:high], d_scores) * scale
            r.projected_t[
                head_rows(0, width, pair, item[0]), first : first + QUERY_BLOCK
            ] = value.astype(BF16)

        def put_keys_and_values(item, known):
            head, at = item
            begin = pieces[at][0]
            seen = [i for i in range(count) if pieces[i][1] <= begin <= pieces[i][0]]
            span = slice(pieces[seen[0]][0], pieces[seen[-1]][0] + QUERY_BLOCK)
            here = slice(begin, begin + QUERY_BLOCK)

            def together(values):
                parts = []
                for i, value in zip(seen, values):
                    start = begin - pieces[i][1]
                    parts.append(value[start : start + QUERY_BLOCK, :])
                return jnp.concatenate(parts, axis=1)

            d_scores = together([known[(head, i)] for i in seen])
            probs = together([probs_of((head, i)) for i in seen])
            r.projected_t[head_rows(1, width, pair, head), here] = (
                dot_nt(queries[head][:, span], d_scores) * scale
            ).astype(BF16)
            r.projected_t[head_rows(2, width, pair, head), here] = dot_nt(
                upstream[head][:, span], probs
            ).astype(BF16)

        d_probs = [d_probs_of(item) for item in items]
        known = {item: d_scores_of(item, value) for item, value in zip(items, d_probs)}
        for item in items:
            put_queries(item, known[item])
        for item in items:
            put_keys_and_values(item, known)

    by_pairs(first_pair, last_pair, hooks, body)


def vector_rows(r):
    return [r.vectors[place : place + 1, :] for place in range(6)]


def token_blocks(r):
    return [slice(start, start + TILE) for start in range(0, r.tokens.shape[0], TILE)]


def keep_sums(r, places, folded):
    for place, parts in zip(places, zip(*folded)):
        r.vector_sums[place] = sum(parts[1:], parts[0])


def first_half(r):
    omega_one, gain_one, shift_one = vector_rows(r)[:3]

    def front(rows):
        inputs = r.tokens[rows, :].astype(F32)
        first_sum = omega_one * inputs + dot_tn(r.context_t[:, rows], flat(r.merger[...]))
        centered = first_sum - lane_mean(first_sum)
        first_inv = lax.rsqrt(lane_mean(centered * centered) + EPSILON)
        first_normed = centered * first_inv
        r.first_inv[rows, :] = jnp.broadcast_to(first_inv, (TILE, 128))
        r.straight[rows, :] = first_normed
        first_low = (first_normed * gain_one + shift_one).astype(BF16)
        r.first_t[:, rows] = first_low.T
        return first_low

    def gelu(rows, hidden):
        square = hidden * hidden
        part = 0.5 + 0.5 * jnp.tanh(hidden * (GELU_A + GELU_B * square))
        active = hidden * part
        r.active[rows, :] = active.astype(BF16)
        slope = part + active * (1.0 - part) * (2 * GELU_A + 6 * GELU_B * square)
        r.d_hidden[rows, :] = slope.astype(BF16)

    blocks = token_blocks(r)
    lows = [front(rows) for rows in blocks]
    for rows, low in zip(blocks, lows):
        gelu(rows, dot_nn(low, whole(r.expand)))


def second_half(r):
    _, gain_one, shift_one, omega_two, gain_two, shift_two = vector_rows(r)

    def rest(rows, product):
        first_out = r.straight[rows, :] * gain_one + shift_one
        second_sum = omega_two * first_out + product
        centered = second_sum - lane_mean(second_sum)
        second_inv = lax.rsqrt(lane_mean(centered * centered) + EPSILON)
        second_normed = centered * second_inv
        arriving = r.cotangent[rows, :].astype(F32)
        r.result[rows, :] = (second_normed * gain_two + shift_two).astype(BF16)
        place = (lax.broadcasted_iota(jnp.int32, (TILE, 1), 0) + rows.start).astype(F32)
        upstream = arriving * jnp.where(place < r.total[0:1, 0:1], 1.0, 0.0)
        scaled = upstream * gain_two
        d_second = second_inv * (
            scaled - lane_mean(scaled) - second_normed * lane_mean(scaled * second_normed)
        )
        r.d_second[rows, :] = d_second
        r.d_second_t[:, rows] = d_second.astype(BF16).T
        return (
            fold_rows(upstream * second_normed),
            fold_rows(upstream),
            fold_rows(first_out * d_second),
        )

    blocks = token_blocks(r)
    products = [dot_nn(r.active[rows, :], whole(r.shrink)) for rows in blocks]
    keep_sums(r, (4, 5, 3), [rest(rows, value) for rows, value in zip(blocks, products)])


def way_back(r, hook=None):
    omega_one, gain_one, _, omega_two = vector_rows(r)[:4]

    def to_hidden(rows):
        d_active = dot_nt(r.d_second[rows, :].astype(BF16), whole(r.shrink))
        d_hidden = (d_active * r.d_hidden[rows, :].astype(F32)).astype(BF16)
        r.d_hidden[rows, :] = d_hidden
        return d_hidden

    def to_branch(rows, product):
        d_first = product + omega_two * r.d_second[rows, :]
        first_normed = r.straight[rows, :]
        scaled = d_first * gain_one
        d_first_sum = r.first_inv[rows, 0:1] * (
            scaled - lane_mean(scaled) - first_normed * lane_mean(scaled * first_normed)
        )
        inputs = r.tokens[rows, :].astype(F32)
        r.straight[rows, :] = omega_one * d_first_sum
        branch_low = d_first_sum.astype(BF16)
        r.d_branch[rows, :] = branch_low
        folded = (
            fold_rows(inputs * d_first_sum),
            fold_rows(d_first * first_normed),
            fold_rows(d_first),
        )
        return branch_low, folded

    blocks = token_blocks(r)
    hidden = [to_hidden(rows) for rows in blocks]
    if hook is not None:
        hook()
    products = [dot_nt(value, whole(r.expand)) for value in hidden]
    got = [to_branch(rows, value) for rows, value in zip(blocks, products)]
    for rows, value in zip(blocks, got):
        r.d_context_t[:, rows] = dot_nt(flat(r.merger[...]), value[0]).astype(BF16)
    keep_sums(r, (0, 1, 2), [value[1] for value in got])


def vector_total(r):
    rows = [jnp.sum(r.vector_sums[place], axis=0, keepdims=True) for place in range(6)]
    return jnp.concatenate(rows + [jnp.zeros((2, rows[0].shape[1]), F32)], axis=0)


def put_tile(ref, columns, value):
    ref[..., columns] = value.astype(ref.dtype).reshape(ref.shape[:-1] + (value.shape[1],))


def shrink_gradient(r, part):
    into = r.g_shrink[part]
    half = r.tokens.shape[1] // 2
    owned = into.shape[-1]
    rows = r.d_second_t[part * half : (part + 1) * half, :]
    value = dot_nn(rows, r.active[...]).astype(BF16)
    for owner in range(value.shape[1] // owned):
        into[owner // GROUP, owner % GROUP] = value[
            :, owner * owned : (owner + 1) * owned
        ].reshape(2, half // 2, owned)


def expand_gradient(r, part):
    half = r.active.shape[1] // 2
    columns = slice(part * half, (part + 1) * half)
    put_tile(r.g_expand[part], slice(None), dot_nn(r.first_t[...], r.d_hidden[:, columns]))


def merger_gradient(r):
    put_tile(r.g_merger, slice(None), dot_nn(r.context_t[...], r.d_branch[...]))


def half_heads(r, part, slots):
    width = r.tokens.shape[1]
    half = width // 2
    starts = [at * width + part * half for at in range(3)]
    return jnp.concatenate([r.projected_t[start : start + half, slots] for start in starts], axis=0)


def attend_gradient(r, part):
    put_tile(r.g_attend[part], slice(None), dot_nt(r.tokens_t[...], half_heads(r, part, slice(None))))


def heads_together(parts):
    half = parts[0].shape[1] // 3
    return jnp.concatenate(
        [part[:, at * half : (at + 1) * half] for at in range(3) for part in parts], axis=1
    )


def heads_apart(whole):
    half = whole.shape[1] // 6
    return [
        jnp.concatenate(
            [whole[:, (2 * at + part) * half : (2 * at + part + 1) * half] for at in range(3)],
            axis=1,
        )
        for part in range(2)
    ]


def input_gradient(r):
    blocks = token_blocks(r)
    products = []
    for rows in blocks:
        halves = [
            dot_general(half_heads(r, part, rows), flat(r.attend[part][...]), 0, 1)
            for part in range(2)
        ]
        products.append(halves[0] + halves[1])
    for rows, value in zip(blocks, products):
        r.straight[rows, :] += value


def row_scratch(slots, width, wide):
    packed = band(slots)[1]
    heads = width // HEAD_DIM
    return dict(
        tokens_t=pltpu.VMEM((width, slots), BF16),
        mask=pltpu.VMEM((packed, QUERY_BLOCK), BF16),
        total=pltpu.VMEM((8, 128), F32),
        projected_t=pltpu.VMEM((3 * width, slots), BF16),
        key_value=pltpu.VMEM((slots, 2 * width), BF16),
        probs=pltpu.VMEM((heads, packed, QUERY_BLOCK), BF16),
        context_t=pltpu.VMEM((width, slots), BF16),
        d_context_t=pltpu.VMEM((width, slots), BF16),
        active=pltpu.VMEM((slots, wide), BF16),
        d_hidden=pltpu.VMEM((slots, wide), BF16),
        first_t=pltpu.VMEM((width, slots), BF16),
        d_second_t=pltpu.VMEM((width, slots), BF16),
        vector_sums=pltpu.VMEM((6, 8, width), F32),
        first_inv=pltpu.VMEM((slots, 128), F32),
        d_second=pltpu.VMEM((slots, width), F32),
    )


class Refs:
    def __init__(self, names, refs):
        for name, ref in zip(names, refs, strict=True):
            setattr(self, name, ref)


LOW, HIGH = "low", "high"
EXPAND_A, EXPAND_B, SHRINK_A, SHRINK_B = "ea", "eb", "sa", "sb"
PARTS_OF = {
    ATTEND: (LOW, HIGH),
    MERGER: (MERGER,),
    EXPAND: (EXPAND_A, EXPAND_B),
    SHRINK: (SHRINK_A, SHRINK_B),
}
PARTS = (LOW, HIGH, MERGER, EXPAND_A, EXPAND_B, SHRINK_A, SHRINK_B)
NEAR_FIRST = (EXPAND_B,)
FAR_FIRST = (SHRINK_A, MERGER)


def in_parts(name, value):
    if name == ATTEND:
        return heads_apart(value)
    count = len(PARTS_OF[name])
    size = value.shape[1] // count
    return [value[:, at * size : (at + 1) * size] for at in range(count)]


def packed_rows(first, order, columns_of, width):
    places = {}
    for name in order:
        places[name] = (first, columns_of[name] // width)
        first += columns_of[name] // width
    return places


SQUARES, ROW_SUMS, EARLY_ROWS = 6, 7, 8
LATE_COLUMNS, LATE_ROWS = 6, 16
COLUMN_ROWS, LAST_ROWS = 8, 4
ALL = slice(None)


def late_places(columns_of, width):
    return packed_rows(LATE_COLUMNS, (MERGER, SHRINK, ATTEND, EXPAND), columns_of, width)


def column_places(columns_of, width):
    places = packed_rows(0, (MERGER, EXPAND, SHRINK), columns_of, width)
    places.update(packed_rows(COLUMN_ROWS, (ATTEND,), columns_of, width))
    return places


def joined(ref, start, count):
    return jnp.concatenate([ref[place : place + 1, :] for place in range(start, start + count)], 1)


def split_into(ref, start, row, width):
    for piece in range(row.shape[1] // width):
        ref[start + piece : start + piece + 1, :] = row[:, piece * width : (piece + 1) * width]


def scalar_sum(value):
    return jnp.sum(jnp.sum(value, axis=1, keepdims=True), axis=0, keepdims=True)


def flat_slots(value):
    return value.reshape((-1,) + value.shape[2:])


class Statistics:
    def __init__(self, r, sizes, columns, vector_gradient):
        outer, self.width, _ = sizes
        self.devices = outer * GROUP
        columns_of = {
            name: getattr(r, name + "_columns").shape[1] * self.devices for name in MATRICES
        }
        self.early, self.late, self.columns = r.early, r.late, columns
        self.late_at = late_places(columns_of, self.width)
        self.column_at = column_places(columns_of, self.width)
        self.squares = {
            name: scalar_sum(joined(columns, *self.column_at[name])) for name in MATRICES
        }
        total = scalar_sum(vector_gradient * vector_gradient)
        for name in MATRICES:
            total = total + self.squares[name]
        self.norm = jnp.sqrt(total)
        self.clip = jnp.minimum(1.0, THRESHOLD / self.norm)

    def lanes(self, row, name):
        at = MATRICES.index(name) * 128
        return jnp.sum(self.early[row : row + 1, at : at + 128], axis=1, keepdims=True)

    def factored(self, name, gradient, rows_old, rows_all):
        wide = gradient.shape[1]
        power = self.clip * self.clip
        row_mean = jnp.sum(gradient * gradient, axis=1, keepdims=True) * (1.0 / wide)
        new_rows = FORGET * rows_old + (1.0 - FORGET) * (power * row_mean + TINY_VALUE)
        now = joined(self.columns, *self.column_at[name]) * (1.0 / rows_all)
        new_columns = FORGET * joined(self.late, *self.late_at[name]) + (1.0 - FORGET) * (
            power * now + TINY_VALUE
        )
        mean = FORGET * (self.lanes(ROW_SUMS, name) * (1.0 / rows_all)) + (1.0 - FORGET) * (
            power * (self.squares[name] * (1.0 / (rows_all * wide))) + TINY_VALUE
        )
        clipped = self.clip * gradient
        step = clipped * lax.rsqrt(new_rows * new_columns * (1.0 / mean))
        return clipped, new_rows, new_columns, step


def vector_steps(gradient, moments, clip):
    clipped = clip * gradient
    variance = FORGET * moments + (1.0 - FORGET) * (clipped * clipped + TINY_VALUE)
    return clipped, variance, clipped * lax.rsqrt(variance)


def shard_kernel(layout_sizes, names, *refs):
    outer, width, wide = layout_sizes
    r = Refs(names, refs)
    r.result = r.cotangent
    r.d_branch = r.tokens
    for name in (ATTEND, EXPAND, SHRINK):
        setattr(r, name, [getattr(r, part) for part in PARTS_OF[name]])
        setattr(r, "g_" + name, [getattr(r, "g_" + part) for part in PARTS_OF[name]])
    core = lax.axis_index(DP)
    chip = lax.axis_index(FSDP)
    far = chip // GROUP
    near = lax.rem(chip, GROUP)
    sibling = (1 - core, chip)
    near_steps = range(1, GROUP)
    far_steps = range(1, outer)

    near_places = [near] + [jnp.bitwise_xor(near, step) for step in near_steps]
    far_places = [lax.rem(far + step, outer) for step in range(outer)]
    far_origins = [lax.rem(far + outer - step, outer) for step in range(outer)]
    near_devices = [(core, far * GROUP + place) for place in near_places]
    far_devices = [(core, place * GROUP + near) for place in far_places]
    other = 1 - core
    started = {}
    arrived = set()

    class Copy:
        def __init__(self, key, sems, index, device, source, target, landing=None):
            self.key = key + (index,)
            self.device = device
            self.sems = sems
            self.index = index
            self.source = source
            self.target = target
            self.landing = target if landing is None else landing

        def describe(self, source, target):
            return pltpu.make_async_remote_copy(
                src_ref=source[0].at[source[1]],
                dst_ref=target[0].at[target[1]],
                send_sem=self.sems[0].at[self.index],
                recv_sem=self.sems[1].at[self.index],
                device_id=self.device,
                device_id_type=MESH,
            )

        def start(self):
            self.describe(self.source, self.target).start()
            started[self.key] = self

        def arrive(self):
            self.describe(self.landing, self.landing).wait_recv()
            arrived.add(self.key)

        def leave(self):
            self.describe(self.source, self.target).wait_send()

    def local(source, target, index):
        return pltpu.make_async_copy(source, target, r.local_sems.at[index])

    load_tokens = local(r.tokens_in, r.tokens, 0)
    load_cotangent = local(r.cotangent_in, r.cotangent, 1)
    load_tokens.start()
    load_cotangent.start()

    barrier = pltpu.get_barrier_semaphore()
    for step in near_steps:
        pl.semaphore_signal(barrier, inc=1, device_id=near_devices[step], device_id_type=MESH)
    for step in far_steps:
        pl.semaphore_signal(barrier, inc=1, device_id=far_devices[step], device_id_type=MESH)
    pl.semaphore_signal(barrier, inc=1, device_id=sibling, device_id_type=MESH)
    pl.semaphore_wait(barrier, len(near_steps) + len(far_steps) + 1)


    class Sum:
        def __init__(self, name, cores):
            self.key = (name,)
            self.near = getattr(r, name + "_near")
            self.far = getattr(r, name + "_far")
            self.sems = (getattr(r, name + "_sends"), getattr(r, name + "_receives"))
            self.steps = [(0, step) for step in near_steps]
            if cores == 2:
                self.steps += [(1, step) for step in range(GROUP)]
            self.mine = core if cores == 2 else 0
            self.other = other if cores == 2 else 0

        def near_copy(self, cross, step):
            mine = (self.near, (self.mine, near))
            whose = self.other if cross else self.mine
            device = (other if cross else core, near_devices[step][1])
            return Copy(
                self.key, self.sems, cross * GROUP + step, device, mine, mine,
                (self.near, (whose, near_places[step])),
            )

        def far_copy(self, step):
            mine = (self.far, far)
            return Copy(
                self.key, self.sems, 2 * GROUP + step, far_devices[step], mine, mine,
                (self.far, far_origins[step]),
            )

        def begin(self, value):
            self.near[self.mine, near] = value
            for cross, step in self.steps:
                self.near_copy(cross, step).start()

        def turn(self):
            for cross, step in self.steps:
                self.near_copy(cross, step).arrive()
            self.far[far] = jnp.sum(flat_slots(self.near[...]), axis=0)
            for step in far_steps:
                self.far_copy(step).start()

        def end(self):
            for step in far_steps:
                self.far_copy(step).arrive()
            return jnp.sum(self.far[...], axis=0)


    class Gather:
        def __init__(self, name):
            self.key = (name,)
            self.near_first = name in NEAR_FIRST
            self.held = getattr(r, name)
            self.sems = (getattr(r, name + "_sends"), getattr(r, name + "_receives"))

        def far_copy(self, step):
            block = ALL if self.near_first else near
            mine = (self.held, (far, block, core))
            return Copy(
                self.key, self.sems, step, far_devices[step], mine, mine,
                (self.held, (far_origins[step], block, core)),
            )

        def near_copy(self, step, hop):
            slot = far_origins[hop]
            mine = (self.held, (slot, near, core))
            return Copy(
                self.key, self.sems, step * outer + hop, near_devices[step], mine, mine,
                (self.held, (slot, near_places[step], core)),
            )

        def cross(self, step):
            if self.near_first:
                block = (far_origins[step], ALL)
            else:
                block = (ALL, near_places[step])
            mine = (self.held, block + (core,))
            return Copy(
                self.key, self.sems, GROUP * outer + step, sibling, mine, mine,
                (self.held, block + (other,)),
            )

        def place(self, mine):
            self.held[far, near, core] = mine.astype(BF16)

        def far_start(self):
            for step in far_steps:
                self.far_copy(step).start()

        def near_start(self, hop):
            for step in near_steps:
                self.near_copy(step, hop).start()

        def begin(self):
            if not self.near_first:
                self.far_start()

        def turn(self):
            if self.near_first:
                for step in near_steps:
                    self.near_copy(step, 0).arrive()
                self.far_start()
            else:
                for hop in far_steps:
                    self.far_copy(hop).arrive()
                    self.near_start(hop)
            self.cross(0).start()

        def pass_on(self):
            if self.near_first:
                for step in far_steps:
                    self.far_copy(step).arrive()
                    self.cross(step).start()
                return
            for step in near_steps:
                for hop in range(outer):
                    self.near_copy(step, hop).arrive()
                self.cross(step).start()

        def end(self):
            for step in range(outer if self.near_first else GROUP):
                self.cross(step).arrive()


    class Reduce:
        def __init__(self, name):
            self.key = ("sum", name)
            self.far_first = name in FAR_FIRST
            for part in ("g", "pair", "near", "far", "done"):
                setattr(self, part, getattr(r, part + "_" + name))
            self.sems = (
                getattr(r, "sum_" + name + "_sends"), getattr(r, "sum_" + name + "_receives")
            )

        def pair_copy(self):
            return Copy(
                self.key, self.sems, 0, sibling, (self.g, (ALL, ALL, other)),
                (self.pair, ALL),
            )

        def near_copy(self, step):
            block = far if self.far_first else ALL
            return Copy(
                self.key, self.sems, step, near_devices[step],
                (self.pair, (block, near_places[step])), (self.near, step - 1),
            )

        def far_copy(self, step):
            block = ALL if self.far_first else near
            return Copy(
                self.key, self.sems, GROUP + step - 1, far_devices[step],
                (self.pair, (far_places[step], block)), (self.far, step - 1),
            )

        def done_copy(self):
            mine = (self.done, core)
            return Copy(
                self.key, self.sems, GROUP + outer, sibling, mine, mine,
                (self.done, other),
            )

        def begin(self):
            self.pair_copy().start()

        def turn(self):
            self.pair_copy().arrive()

            def block(step, carry):
                both = self.g[step, :, core].astype(F32) + self.pair[step].astype(F32)
                self.pair[step] = both.astype(BF16)
                return carry

            lax.fori_loop(0, outer, block, 0)
            if self.far_first:
                for step in far_steps:
                    self.far_copy(step).start()
            else:
                for step in near_steps:
                    self.near_copy(step).start()

        def pass_on(self):
            if self.far_first:
                for step in far_steps:
                    self.far_copy(step).arrive()
                total = self.pair[far].astype(F32)
                for step in far_steps:
                    total = total + self.far[step - 1].astype(F32)
                self.pair[far] = total.astype(BF16)
                for step in near_steps:
                    self.near_copy(step).start()
                return
            for step in near_steps:
                self.near_copy(step).arrive()

            def block(step, carry):
                total = self.pair[step, near].astype(F32)
                for place in near_steps:
                    total = total + self.near[place - 1, step].astype(F32)
                self.pair[step, near] = total.astype(BF16)
                return carry

            lax.fori_loop(0, outer, block, 0)
            for step in far_steps:
                self.far_copy(step).start()

        def collect(self):
            total = self.pair[far, near].astype(F32)
            if self.far_first:
                for step in near_steps:
                    self.near_copy(step).arrive()
                    total = total + self.near[step - 1].astype(F32)
            else:
                for step in far_steps:
                    self.far_copy(step).arrive()
                    total = total + self.far[step - 1].astype(F32)
            self.done[core] = total
            self.done_copy().start()

        def end(self):
            self.done_copy().arrive()

    early = Sum("early", 1)
    late = Sum("late", 1)
    vector_sum = Sum("vector", 2)
    column_sum = Sum("column", 1)
    last_sum = Sum("last", 2)
    step_sum = Sum("step", 2)
    gathers = {name: Gather(name) for name in PARTS}
    sums = {name: Reduce(name) for name in PARTS}
    shards = {name: getattr(r, name + "_weight") for name in MATRICES}

    def my_rows(shard):
        half = shard.shape[0] // 2
        return shard[pl.ds(pl.multiple_of(core * half, half), half), :]

    def place(name):
        for part, mine in zip(PARTS_OF[name], in_parts(name, my_rows(shards[name]))):
            gathers[part].place(mine)

    place(ATTEND)
    gathers[LOW].begin()
    gathers[LOW].near_start(0)
    gathers[HIGH].begin()
    place(EXPAND)
    for part in NEAR_FIRST:
        gathers[part].near_start(0)
    gathers[HIGH].near_start(0)


    columns_of = {name: getattr(r, name + "_columns").shape[1] * outer * GROUP for name in MATRICES}
    late_at = late_places(columns_of, width)
    column_at = column_places(columns_of, width)

    def early_value():
        thin = r.vectors_own.shape[1]
        r.packed[...] = jnp.zeros_like(r.packed)
        r.packed[0:6, 0:thin] = r.vectors_own[...]
        vectors = pltpu.roll(r.packed[0:8, :], chip * thin, 1)
        r.packed[0:8, :] = vectors
        for at, name in enumerate(MATRICES):
            lanes = slice(at * 128, at * 128 + 128)
            shard = shards[name][...]
            r.packed[SQUARES : SQUARES + 1, lanes] = fold_lanes(
                jnp.sum(fold_rows(shard * shard), axis=0, keepdims=True)
            )
            total = jnp.sum(getattr(r, name + "_rows")[...], axis=1, keepdims=True)
            first_lane = lax.broadcasted_iota(jnp.int32, (1, 128), 1) == 0
            r.packed[ROW_SUMS : ROW_SUMS + 1, lanes] = jnp.where(first_lane, total, 0.0)
        return r.packed[0:EARLY_ROWS, :]

    def late_value():
        thin = r.vectors_own.shape[1]
        r.packed[...] = jnp.zeros_like(r.packed)
        r.packed[0:6, 0:thin] = r.moments_own[...]
        for name in (MERGER, SHRINK):
            row, _ = late_at[name]
            r.packed[row : row + 1, 0:thin] = getattr(r, name + "_columns")[...]
        r.packed[0:8, :] = pltpu.roll(r.packed[0:8, :], chip * thin, 1)
        for name in (ATTEND, EXPAND):
            own = getattr(r, name + "_columns")
            size = own.shape[1]
            r.spread[...] = jnp.zeros_like(r.spread)
            r.spread[0:1, 0:size] = own[...]
            whole = pltpu.roll(r.spread[:, : columns_of[name]], chip * size, 1)[0:1, :]
            split_into(r.packed, late_at[name][0], whole, width)
        return r.packed[...]


    place(MERGER)
    place(SHRINK)
    early.begin(early_value())
    load_tokens.wait()
    prepare(r)
    gathers[LOW].turn()
    later = [part for part in PARTS[2:] if part not in NEAR_FIRST]
    for part in later:
        gathers[part].begin()
    gathers[HIGH].turn()
    early.turn()
    for part in later:
        gathers[part].near_start(0)
    for part in NEAR_FIRST:
        gathers[part].turn()
    gathers[LOW].pass_on()
    gathers[LOW].end()
    project(r, 0)
    gathers[MERGER].turn()
    attend_forward(r, 0, 2, ())
    gathers[HIGH].pass_on()
    gathers[EXPAND_A].turn()
    gathers[HIGH].end()
    project(r, 1)
    gathers[SHRINK_A].turn()
    gathers[SHRINK_B].turn()
    attend_forward(r, 2, 4, ())
    gathers[MERGER].pass_on()
    early_all = early.end()
    r.early[...] = early_all
    r.vectors[...] = early_all.astype(BF16).astype(F32)
    gathers[EXPAND_A].pass_on()
    gathers[MERGER].end()
    gathers[EXPAND_B].pass_on()
    gathers[EXPAND_A].end()
    gathers[EXPAND_B].end()
    first_half(r)
    late.begin(late_value())
    load_cotangent.wait()
    gathers[SHRINK_A].pass_on()
    gathers[SHRINK_B].pass_on()
    gathers[SHRINK_A].end()
    gathers[SHRINK_B].end()
    second_half(r)
    store_result = local(r.result, r.result_out, 0)
    store_result.start()


    shrink_gradient(r, 0)
    sums[SHRINK_A].begin()
    shrink_gradient(r, 1)
    sums[SHRINK_B].begin()
    sums[SHRINK_A].turn()
    late.turn()
    way_back(r, sums[SHRINK_B].turn)
    expand_gradient(r, 0)
    sums[EXPAND_A].begin()
    expand_gradient(r, 1)
    sums[EXPAND_B].begin()
    vector_sum.begin(vector_total(r))
    merger_gradient(r)
    sums[MERGER].begin()
    sums[EXPAND_A].turn()

    def hook_one():
        sums[EXPAND_B].turn()
        sums[MERGER].turn()

    def hook_three():
        sums[LOW].turn()
        vector_sum.turn()
        sums[SHRINK_A].pass_on()

    pairs = width // 128
    attend_backward(r, 0, pairs // 2, ((1, hook_one),))
    attend_gradient(r, 0)
    sums[LOW].begin()
    attend_backward(r, pairs // 2, pairs, ((pairs // 2 + 1, hook_three),))
    attend_gradient(r, 1)
    sums[HIGH].begin()
    sums[SHRINK_B].pass_on()
    sums[HIGH].turn()


    def keep(name):
        for part in PARTS_OF[name]:
            sums[part].end()
        done = [flat(getattr(r, "done_" + part)[...]) for part in PARTS_OF[name]]
        if name == SHRINK:
            done = [value.T for value in done]
        whole_done = jnp.concatenate(done, axis=1)
        getattr(r, "out_" + name)[...] = whole_done
        squares = jnp.sum(whole_done * whole_done, axis=0, keepdims=True)
        split_into(r.packed, column_at[name][0], squares, width)

    sums[MERGER].pass_on()
    sums[EXPAND_A].pass_on()
    sums[LOW].pass_on()
    sums[SHRINK_A].collect()
    sums[EXPAND_B].pass_on()
    sums[SHRINK_B].collect()
    sums[MERGER].collect()
    r.late[...] = late.end()
    r.vector_out[...] = vector_sum.end()
    r.packed[...] = jnp.zeros_like(r.packed)
    sums[HIGH].pass_on()
    sums[LOW].collect()
    keep(SHRINK)
    keep(MERGER)
    sums[EXPAND_A].collect()
    sums[EXPAND_B].collect()
    sums[HIGH].collect()
    attend_half = heads_together([getattr(r, "done_" + name)[core] for name in (LOW, HIGH)])
    squares = jnp.sum(attend_half * attend_half, axis=0, keepdims=True)
    row = COLUMN_ROWS
    split_into(r.packed, row, squares, width)
    last_sum.begin(r.packed[row : row + LAST_ROWS, :])
    keep(EXPAND)
    column_sum.begin(r.packed[0:COLUMN_ROWS, :])
    input_gradient(r)
    store_input = local(r.straight, r.input_out, 1)
    store_input.start()
    last_sum.turn()
    column_sum.turn()
    sums[LOW].end()
    sums[HIGH].end()
    r.out_attend[...] = heads_together([flat(getattr(r, "done_" + name)[...]) for name in (LOW, HIGH)])
    r.early_out[...] = r.early[...]
    r.late_out[...] = r.late[...]
    r.column_out[row : row + LAST_ROWS, :] = last_sum.end()
    r.column_out[0:COLUMN_ROWS, :] = column_sum.end()
    facts = Statistics(r, layout_sizes, r.column_out, r.vector_out[...])

    def my_half(value):
        half = value.shape[0] // 2
        return jnp.where(core == 0, value[:half], value[half:])

    rows = []
    for name in MATRICES:
        rows_old = getattr(r, name + "_rows")[...]
        step = facts.factored(
            name, my_rows(getattr(r, "out_" + name)), my_half(column_of(rows_old)),
            float(rows_old.shape[1] * outer * GROUP),
        )[3]
        rows.append(fold_lanes(jnp.sum(step * step, axis=0, keepdims=True)))
    step_sum.begin(jnp.concatenate(rows + [jnp.zeros((4, 128), F32)], axis=0))
    step_sum.turn()
    r.step_out[...] = step_sum.end()


    for copy in started.values():
        copy.leave()
    store_result.wait()
    store_input.wait()


def update_kernel(layout_sizes, names, *refs):
    outer, width, wide = layout_sizes
    r = Refs(names, refs)
    chip = lax.axis_index(FSDP)
    out_of = [
        pltpu.make_async_copy(r.result_in, r.block_output, r.sems.at[2]),
        pltpu.make_async_copy(r.input_in, r.input_gradient, r.sems.at[3]),
    ]
    for copy in out_of:
        copy.start()
    vector_gradient = r.vector_sum[...]
    facts = Statistics(r, layout_sizes, r.column_sum, vector_gradient)
    r.global_norm[...] = facts.norm
    for name in MATRICES:
        weight = getattr(r, name + "_weight")[...]
        rows_all = float(weight.shape[0] * outer * GROUP)
        count = rows_all * weight.shape[1]
        clipped, new_rows, new_columns, step = facts.factored(
            name, getattr(r, name + "_sum")[...], column_of(getattr(r, name + "_rows")[...]), rows_all
        )
        at = MATRICES.index(name)
        step_square = jnp.sum(r.step_sum[at : at + 1, :], axis=1, keepdims=True)
        weight_square = facts.lanes(SQUARES, name)
        shrunk = jnp.maximum(1.0, jnp.sqrt(step_square * (1.0 / count)) * (1.0 / UPDATE_LIMIT))
        stride = LEARN_RATE * jnp.maximum(0.001, jnp.sqrt(weight_square * (1.0 / count)))
        updated = weight - (stride / shrunk) * step
        getattr(r, name + "_gradient")[...] = clipped
        getattr(r, name + "_updated")[...] = updated
        getattr(r, name + "_bfloat")[...] = updated.astype(BF16)
        getattr(r, name + "_newrows")[...] = row_of(new_rows)
        size = getattr(r, name + "_newcols").shape[1]
        wide_row = jnp.broadcast_to(new_columns, (8, new_columns.shape[1]))
        whole = new_columns.shape[1]
        own = pltpu.roll(wide_row, lax.rem(whole - chip * size, whole), 1)
        getattr(r, name + "_newcols")[...] = own[0:1, 0:size]
    vectors = r.early[...]
    clipped, variance, step = vector_steps(
        vector_gradient, r.late[0:8, :], facts.clip
    )
    shrunk = jnp.maximum(1.0, jnp.sqrt(lane_mean(step * step)) * (1.0 / UPDATE_LIMIT))
    stride = LEARN_RATE * jnp.maximum(0.001, jnp.sqrt(lane_mean(vectors * vectors)))
    updated = vectors - stride * (step / shrunk)
    thin = r.vector_updated.shape[1]
    turn = lax.rem(width - chip * thin, width)
    for ref, value in (
        (r.vector_gradient, clipped),
        (r.vector_variance, variance),
        (r.vector_updated, updated),
    ):
        ref[...] = pltpu.roll(value, turn, 1)[0:6, 0:thin]
    for copy in out_of:
        copy.wait()


def in_vmem():
    return pl.BlockSpec(memory_space=pltpu.VMEM)


def anywhere():
    return pl.BlockSpec(memory_space=pl.ANY)


def call(kernel, sizes, inputs, outputs, scratch, held, params, name):
    names = list(inputs) + list(outputs) + list(scratch)
    results = pl.pallas_call(
        functools.partial(kernel, sizes, names),
        in_specs=[anywhere() if key in held else in_vmem() for key in inputs],
        out_specs=[anywhere() if key in held else in_vmem() for key in outputs],
        out_shape=list(outputs.values()),
        scratch_shapes=list(scratch.values()),
        compiler_params=params,
        name=name,
    )(*inputs.values())
    return dict(zip(outputs, results, strict=True))


def add_part(scratch, outer, name, held, half):
    far_first = name in FAR_FIRST
    near_block = half if far_first else (outer,) + half
    far_block = (GROUP,) + half if far_first else half
    scratch[name] = pltpu.VMEM((outer, GROUP, 2) + held, BF16)
    scratch["g_" + name] = pltpu.VMEM((outer, GROUP, 2) + half, BF16)
    scratch["pair_" + name] = pltpu.VMEM((outer, GROUP) + half, BF16)
    scratch["near_" + name] = pltpu.VMEM((GROUP - 1,) + near_block, BF16)
    scratch["far_" + name] = pltpu.VMEM((max(1, outer - 1),) + far_block, BF16)
    scratch["done_" + name] = pltpu.VMEM((2,) + half, F32)
    for way in ("_sends", "_receives"):
        scratch[name + way] = pltpu.SemaphoreType.DMA((GROUP * outer + GROUP,))
        scratch["sum_" + name + way] = pltpu.SemaphoreType.DMA((GROUP + outer + 1,))


def staged_shards(devices, tokens, lengths, weights, vectors, rows, columns, moments, cotangent):
    outer = devices // GROUP
    slots, width = tokens.shape[1:]
    wide = weights[EXPAND].shape[1]
    sizes = (outer, width, wide)
    shape = jax.ShapeDtypeStruct
    row_in = {name + "_rows": rows[name].reshape(1, -1) for name in MATRICES}
    column_in = {name + "_columns": columns[name].reshape(1, -1) for name in MATRICES}
    weight_in = {name + "_weight": weights[name] for name in MATRICES}
    inputs = dict(
        tokens_in=tokens[0], lengths=lengths, cotangent_in=cotangent[0],
        vectors_own=vectors, moments_own=moments, **weight_in, **row_in, **column_in,
    )
    outputs = dict(
        result_out=shape((slots, width), BF16),
        input_out=shape((slots, width), F32),
        vector_out=shape((8, width), F32),
        early_out=shape((EARLY_ROWS, width), F32),
        late_out=shape((LATE_ROWS, width), F32),
        column_out=shape((2 * COLUMN_ROWS, width), F32),
        step_out=shape((8, 128), F32),
        **{"out_" + name: shape(weights[name].shape, F32) for name in MATRICES},
    )
    scratch = row_scratch(slots, width, wide)
    scratch.update(
        tokens=pltpu.VMEM((slots, width), BF16),
        cotangent=pltpu.VMEM((slots, width), BF16),
        straight=pltpu.VMEM((slots, width), F32),
        vectors=pltpu.VMEM((8, width), F32),
        early=pltpu.VMEM((EARLY_ROWS, width), F32),
        late=pltpu.VMEM((LATE_ROWS, width), F32),
        packed=pltpu.VMEM((LATE_ROWS, width), F32),
        spread=pltpu.VMEM((8, wide), F32),
        local_sems=pltpu.SemaphoreType.DMA((2,)),
    )
    for name, cores, size in (
        ("early", 1, (EARLY_ROWS, width)),
        ("late", 1, (LATE_ROWS, width)),
        ("vector", 2, (8, width)),
        ("column", 1, (COLUMN_ROWS, width)),
        ("last", 2, (LAST_ROWS, width)),
        ("step", 2, (8, 128)),
    ):
        scratch[name + "_near"] = pltpu.VMEM((cores, GROUP) + size, F32)
        scratch[name + "_far"] = pltpu.VMEM((outer,) + size, F32)
        for way in ("_sends", "_receives"):
            scratch[name + way] = pltpu.SemaphoreType.DMA((2 * GROUP + outer,))
    for of in MATRICES:
        for name in PARTS_OF[of]:
            rows, all_columns = weights[of].shape
            wide_now = all_columns // len(PARTS_OF[of])
            held = (rows // 2, wide_now)
            half = (wide_now // 2, rows) if of == SHRINK else held
            add_part(scratch, outer, name, held, half)
    got = call(
        shard_kernel, sizes, inputs, outputs, scratch,
        ("tokens_in", "cotangent_in", "result_out", "input_out"),
        pltpu.CompilerParams(
            collective_id=1, has_side_effects=True, vmem_limit_bytes=VMEM_LIMIT
        ),
        "row_and_sums",
    )
    inputs = dict(
        result_in=got["result_out"], input_in=got["input_out"], vector_sum=got["vector_out"],
        early=got["early_out"], late=got["late_out"], column_sum=got["column_out"], step_sum=got["step_out"],
        **{name + "_sum": got["out_" + name] for name in MATRICES},
        **weight_in, **row_in, **column_in,
    )
    outputs = dict(
        block_output=shape((slots, width), BF16),
        input_gradient=shape((slots, width), F32),
        global_norm=shape((1, 1), F32),
    )
    for name in MATRICES:
        outputs[name + "_gradient"] = shape(weights[name].shape, F32)
        outputs[name + "_newrows"] = shape(row_in[name + "_rows"].shape, F32)
        outputs[name + "_newcols"] = shape(column_in[name + "_columns"].shape, F32)
        outputs[name + "_updated"] = shape(weights[name].shape, F32)
        outputs[name + "_bfloat"] = shape(weights[name].shape, BF16)
    for name in ("vector_gradient", "vector_variance", "vector_updated"):
        outputs[name] = shape(vectors.shape, F32)
    out = call(
        update_kernel, sizes, inputs, outputs,
        dict(
            sems=pltpu.SemaphoreType.DMA((4,)),
        ),
        ("block_output", "input_gradient"),
        pltpu.CompilerParams(vmem_limit_bytes=VMEM_LIMIT),
        "update",
    )
    out["block_output"] = out["block_output"][None]
    out["input_gradient"] = out["input_gradient"][None]
    out["global_norm"] = out["global_norm"].reshape(())
    for name in MATRICES:
        for kind in ("_newrows", "_newcols"):
            out[name + kind] = out[name + kind].reshape(-1)
    return tuple(out.values())


def tiled_gradient(into, left, right):
    def tile(step, carry):
        columns = aligned(step * 2 * TILE, 2 * TILE)
        into[:, columns] = dot_nn(left[...], right[:, columns]).astype(into.dtype)
        return carry

    lax.fori_loop(0, into.shape[1] // (2 * TILE), tile, 0)


def row_kernel(names, *refs):
    r = Refs(names, refs)
    r.attend = (r.attend_low, r.attend_high)
    r.expand, r.shrink = (r.expand,), (r.shrink,)
    r.g_attend = (r.g_attend_low, r.g_attend_high)
    pairs = r.tokens.shape[1] // 128
    steps = (
        functools.partial(prepare, r),
        functools.partial(project, r, 0),
        functools.partial(project, r, 1),
        functools.partial(attend_forward, r, 0, pairs, ()),
        functools.partial(first_half, r),
        functools.partial(second_half, r),
        functools.partial(tiled_gradient, r.g_shrink, r.d_second_t, r.active),
        functools.partial(way_back, r),
        functools.partial(tiled_gradient, r.g_expand, r.first_t, r.d_hidden),
        functools.partial(tiled_gradient, r.g_merger, r.context_t, r.d_branch),
        functools.partial(attend_backward, r, 0, pairs, ()),
        functools.partial(attend_gradient, r, 0),
        functools.partial(attend_gradient, r, 1),
        functools.partial(input_gradient, r),
    )
    for step in steps:
        pl.when(lax.axis_index(FSDP) >= 0)(step)
    r.g_vectors[...] = vector_total(r)


def plain_shards(devices, tokens, lengths, weights, vectors, rows, columns, moments, cotangent):
    slots, width = tokens.shape[1:]
    wide = weights[EXPAND].shape[1]
    shape = jax.ShapeDtypeStruct
    whole = {
        name: lax.all_gather(weights[name].astype(BF16), FSDP, axis=0, tiled=True)
        for name in MATRICES
    }
    vector_rows = lax.all_gather(vectors.astype(BF16), FSDP, axis=1, tiled=True).astype(F32)
    vector_rows = jnp.concatenate([vector_rows, jnp.zeros((2, width), F32)], axis=0)
    whole["attend_low"], whole["attend_high"] = heads_apart(whole.pop(ATTEND))
    inputs = dict(
        tokens=tokens[0], lengths=lengths, cotangent=cotangent[0], vectors=vector_rows, **whole
    )
    outputs = dict(
        result=shape((slots, width), BF16),
        straight=shape((slots, width), F32),
        g_vectors=shape((8, width), F32),
        g_attend_low=shape((width, 3 * width // 2), BF16),
        g_attend_high=shape((width, 3 * width // 2), BF16),
        g_merger=shape((width, width), BF16),
        g_expand=shape((width, wide), BF16),
        g_shrink=shape((width, wide), BF16),
    )
    scratch = row_scratch(slots, width, wide)
    scratch["d_branch"] = pltpu.VMEM((slots, width), BF16)
    names = list(inputs) + list(outputs) + list(scratch)
    got = pl.pallas_call(
        functools.partial(row_kernel, names),
        in_specs=[in_vmem()] * len(inputs),
        out_specs=[in_vmem()] * len(outputs),
        out_shape=list(outputs.values()),
        scratch_shapes=list(scratch.values()),
        compiler_params=pltpu.CompilerParams(vmem_limit_bytes=VMEM_LIMIT),
        name="row",
    )(*inputs.values())
    got = dict(zip(outputs, got, strict=True))
    got["g_" + ATTEND] = heads_together((got["g_attend_low"], got["g_attend_high"]))
    grads = []
    for name in MATRICES:
        value = lax.psum(got["g_" + name], DP).astype(F32)
        if name == SHRINK:
            grads.append(lax.psum_scatter(value.T, FSDP, scatter_dimension=0, tiled=True))
        else:
            grads.append(lax.psum_scatter(value, FSDP, scatter_dimension=0, tiled=True))
    vector_all = lax.psum(got["g_vectors"][:6], (DP, FSDP))
    index = lax.axis_index(FSDP)

    def spread(own, dim):
        size = own.shape[dim]
        extent = own.shape[:dim] + (size * devices,) + own.shape[dim + 1 :]
        return lax.dynamic_update_slice_in_dim(
            jnp.zeros(extent, F32), own, index * size, dim
        )

    early = (
        [spread(columns[name], 0) for name in MATRICES],
        [jnp.sum(weights[name] * weights[name]) for name in MATRICES],
        [jnp.sum(rows[name]) for name in MATRICES],
        [jnp.sum(grad * grad, axis=0) for grad in grads],
        jnp.sum(vectors * vectors, axis=1),
    )
    old_columns, weight_squares, row_sums, columns_now, vector_squares = lax.psum(early, FSDP)
    squares = [jnp.sum(value) for value in columns_now]
    total = jnp.sum(vector_all * vector_all)
    for value in squares:
        total = total + value
    norm = jnp.sqrt(total)
    clip = jnp.minimum(1.0, THRESHOLD / norm)
    power = clip * clip
    pieces = []
    for at, name in enumerate(MATRICES):
        grad = grads[at]
        rows_all = float(grad.shape[0] * devices)
        count = rows_all * grad.shape[1]
        new_rows = FORGET * rows[name] + (1.0 - FORGET) * (
            power * jnp.mean(grad * grad, axis=1) + TINY_VALUE
        )
        new_columns = FORGET * old_columns[at] + (1.0 - FORGET) * (
            power * columns_now[at] / rows_all + TINY_VALUE
        )
        mean = FORGET * row_sums[at] / rows_all + (1.0 - FORGET) * (
            power * squares[at] / count + TINY_VALUE
        )
        clipped = clip * grad
        step = clipped * lax.rsqrt(new_rows[:, None] * new_columns[None, :] / mean)
        pieces.append((clipped, new_rows, new_columns, step, count))
    thin = vectors.shape[1]
    vector_clipped = clip * lax.dynamic_slice_in_dim(vector_all, index * thin, thin, 1)
    variance = FORGET * moments + (1.0 - FORGET) * (vector_clipped * vector_clipped + TINY_VALUE)
    vector_step = vector_clipped * lax.rsqrt(variance)
    step_squares, vector_step_squares = lax.psum(
        (
            [jnp.sum(piece[3] * piece[3]) for piece in pieces],
            jnp.sum(vector_step * vector_step, axis=1),
        ),
        FSDP,
    )
    results = [got["result"][None], got["straight"][None], norm]
    for at, name in enumerate(MATRICES):
        clipped, new_rows, new_columns, step, count = pieces[at]
        shrunk = jnp.maximum(1.0, jnp.sqrt(step_squares[at] / count) / UPDATE_LIMIT)
        stride = LEARN_RATE * jnp.maximum(0.001, jnp.sqrt(weight_squares[at] / count))
        updated = weights[name] - stride * (step / shrunk)
        size = columns[name].shape[0]
        own = lax.dynamic_slice_in_dim(new_columns, index * size, size, 0)
        results.extend([clipped, new_rows, own, updated, updated.astype(BF16)])
    extent = float(width)
    shrunk = jnp.maximum(1.0, jnp.sqrt(vector_step_squares / extent) / UPDATE_LIMIT)[:, None]
    stride = LEARN_RATE * jnp.maximum(0.001, jnp.sqrt(vector_squares / extent))[:, None]
    results.extend([vector_clipped, variance, vectors - stride * (vector_step / shrunk)])
    return tuple(results)


def shards(
    devices,
    tokens,
    lengths,
    attend_weight,
    merger_weight,
    expand_weight,
    shrink_weight,
    vectors,
    attend_rows,
    attend_columns,
    merger_rows,
    merger_columns,
    expand_rows,
    expand_columns,
    shrink_rows,
    shrink_columns,
    vector_moments,
    cotangent,
):
    weights = dict(
        attend=attend_weight, merger=merger_weight, expand=expand_weight, shrink=shrink_weight
    )
    rows = dict(attend=attend_rows, merger=merger_rows, expand=expand_rows, shrink=shrink_rows)
    columns = dict(
        attend=attend_columns, merger=merger_columns, expand=expand_columns, shrink=shrink_columns
    )
    assert tokens.shape[0] == 1
    fits = devices % GROUP == 0 and all(
        weight.shape[0] % 32 == 0 for weight in weights.values()
    ) and shrink_weight.shape[0] % 128 == 0
    body = staged_shards if fits else plain_shards
    return body(
        devices, tokens, lengths, weights, vectors, rows, columns, vector_moments, cotangent
    )


def solution(mesh):
    split = P(FSDP, None)
    row = P((DP, FSDP), None, None)
    one = P(FSDP)
    thin = P(None, FSDP)
    in_specs = (
        (row, P((DP, FSDP), None)) + (split,) * 4 + (thin,) + (one,) * 8 + (thin, row)
    )
    out_specs = (row, row, P()) + (split, one, one, split, split) * 4 + (thin,) * 3
    return jax.shard_map(
        functools.partial(shards, mesh.shape[FSDP]),
        mesh=mesh, in_specs=in_specs, out_specs=out_specs, check_vma=False,
    )
```
